32 devices in a mesh: row: 8 (over y, x, core), col: 4 (over z).
Axes of the slice: x: 2, y: 2, z: 4, core: 2. Of those that a mesh axis runs over, the one named last changes fastest.
Arguments:
- multispectral: bfloat16 [2, 16384, 2048], P(None, 'row', 'col'), may hold values from -6 to 6
- hyperspectral: bfloat16 [96, 4096, 512], P(None, 'row', 'col'), may hold values from -6 to 6
- row_start: float32 [16384, 128], P(('row', 'col')), may hold values from -6 to 6
- col_factor: bfloat16 [2048, 128], P('col', 'row'), may hold values from -0.125 to 0.125
- band_factor: float32 [96, 128], replicated, may hold values from -2 to 2
- response: float32 [2, 96], replicated, may hold values from 0.2 to 1
- blur_taps: float32 [9], replicated, may hold values from 0.2 to 1
- offsets: int32 [9], replicated, may hold values from -8 to 8, as said below
Outputs:
- row_factor: float32 [16384, 128], P(('row', 'col'))
- residual: float32 [16384, 128], P(('row', 'col'))
The draws below stay inside these ranges and needn't reach their ends.
Inputs may be any that keep to these rules, and one draw needn't show every extreme that they name: 9 distinct offsets; -8 and 8 are always among them.
All inputs are finite; a program needn't handle non-finite values.
Results may differ from the reference program's by a relative error of at most 0.0023.
Values may be sent and summed in bfloat16 or wider, within the bound.
No kernel may reach another device: no remote copies, remote signals or barrier semaphores. Data moves between devices by JAX's collectives and lax.ppermute only.
A program may use at most 128 MiB of HBM per device.

```python
import math
import jax
import jax.numpy as jnp
from jax import lax

R = 128
KH = 96
KM = 2
DEC = 4
W = 8
TAPS = 9
ITERS = 4
NI = 16384
NJ = 2048
IH = 4096
JH = 512


def draw_offsets(key, part):
    middle = jnp.arange(1, 2 * W, dtype=jnp.int32) - W
    picked = jax.random.permutation(key, middle)[:TAPS - 2]
    ends = jnp.array([-W, W], dtype=jnp.int32)
    return jnp.concatenate([ends, picked]).astype(jnp.int32)


def level_of(own_key, dims, shards, smallest, top_value):
    level = 1.0
    for dim, shards_of in shards:
        draws = jax.random.uniform(jax.random.fold_in(jax.random.fold_in(own_key, 6), dim), (shards_of,), jnp.float32, smallest / len(shards), top_value / len(shards))
        level = level * jnp.repeat(jnp.exp(draws), dims[dim] // shards_of).reshape((-1,) + (1,) * (len(dims) - 1 - dim))
    return level


def centred(stream_key, extent, width, most, pieces=(), kind=jnp.bfloat16):
    drawn = width * jax.random.normal(stream_key, extent, jnp.float32)
    if pieces:
        drawn = drawn * level_of(stream_key, extent, pieces, -0.22, 0.18)
    return jnp.clip(drawn, -most, most).astype(kind)


def setup_inputs(seed: int = 0) -> dict:
    streams_of = jax.random.split(jax.random.key(seed), 9)
    return {
        "multispectral": centred(streams_of[0], (KM, NI, NJ), 1.0, 6.0, ((1, 8), (2, 4))),
        "hyperspectral": centred(streams_of[1], (KH, IH, JH), 1.0, 6.0, ((1, 8), (2, 4))),
        "row_start": centred(streams_of[2], (NI, R), 1.0, 6.0, ((0, 32),), jnp.float32),
        "col_factor": centred(streams_of[3], (NJ, R), NJ ** -0.5, 0.125, ((0, 4), (1, 8))),
        "band_factor": centred(streams_of[4], (KH, R), 0.15, 2.0, (), jnp.float32),
        "response": jnp.clip(jax.random.uniform(streams_of[5], (KM, KH), jnp.float32, 0.2, 1.0), 0.2, 1.0),
        "blur_taps": jnp.clip(jnp.exp(jax.random.uniform(streams_of[6], (TAPS,), jnp.float32, math.log(0.2), math.log(1.0))), 0.2, 1.0),
        "offsets": draw_offsets(jax.random.fold_in(streams_of[8], 71), 0),
    }


RIDGE_TERM = 0.1
FULL_PRECISION = lax.Precision.HIGHEST


def blur_down(values, weights, offsets):
    height = values.shape[0]
    result = jnp.zeros((height // DEC, values.shape[1]), jnp.float32)
    for number in range(TAPS):
        shifted = jnp.roll(values, -offsets[number], axis=0)
        picked = shifted.reshape(height // DEC, DEC, values.shape[1])[:, 0, :]
        result = result + weights[number] * picked.astype(jnp.float32)
    return result


def blur_up(coarse, weights, offsets):
    height, columns = coarse.shape
    padding = jnp.zeros((height, DEC - 1, columns), jnp.float32)
    spread_rows = jnp.concatenate([coarse[:, None, :], padding], axis=1).reshape(height * DEC, columns)
    result = jnp.zeros((height * DEC, columns), jnp.float32)
    for number in range(TAPS):
        result = result + weights[number] * jnp.roll(spread_rows, offsets[number], axis=0)
    return result


def reference(multispectral, hyperspectral, row_start, col_factor, band_factor, response, blur_taps, offsets):
    coarse_columns = blur_down(col_factor, blur_taps, offsets)
    merged = jnp.dot(response, band_factor, precision=FULL_PRECISION)
    multi_pairs = (merged[:, None, :] * col_factor.astype(jnp.float32)[None, :, :]).astype(jnp.bfloat16)
    hyper_pairs = (band_factor[:, None, :] * coarse_columns[None, :, :]).astype(jnp.bfloat16)
    multi_sums = jnp.zeros((NI, R), jnp.float32)
    for channel in range(KM):
        multi_sums = multi_sums + jnp.dot(multispectral[channel], multi_pairs[channel], preferred_element_type=jnp.float32)
    hyper_sums = jnp.zeros((IH, R), jnp.float32)
    for channel in range(KH):
        hyper_sums = hyper_sums + jnp.dot(hyperspectral[channel], hyper_pairs[channel], preferred_element_type=jnp.float32)
    column_gram = jnp.dot(col_factor.T, col_factor, preferred_element_type=jnp.float32)
    coarse_gram = jnp.dot(coarse_columns.T, coarse_columns, precision=FULL_PRECISION)
    band_gram = jnp.dot(band_factor.T, band_factor, precision=FULL_PRECISION)
    merged_gram = jnp.dot(merged.T, merged, precision=FULL_PRECISION)
    hyper_gram = coarse_gram * band_gram
    multi_gram = column_gram * merged_gram

    def operate(values):
        restored = blur_up(blur_down(values, blur_taps, offsets), blur_taps, offsets)
        return (jnp.dot(restored, hyper_gram, precision=FULL_PRECISION)
                + jnp.dot(values, multi_gram, precision=FULL_PRECISION) + RIDGE_TERM * values)

    right_side = blur_up(hyper_sums, blur_taps, offsets) + multi_sums
    solution = row_start
    residual = right_side - operate(solution)
    direction = residual
    norm_now = jnp.sum(residual * residual)
    for iteration in range(ITERS):
        mapped = operate(direction)
        step_size = norm_now / jnp.sum(direction * mapped)
        solution = solution + step_size * direction
        residual = residual - step_size * mapped
        norm_next = jnp.sum(residual * residual)
        direction = residual + (norm_next / norm_now) * direction
        norm_now = norm_next
    return solution, residual
```

```python
import functools

import jax
import jax.numpy as jnp
from jax import lax
from jax.experimental import pallas as pl
from jax.experimental.pallas import tpu as pltpu
from jax.sharding import PartitionSpec as P

DEC = 4
W = 8
REACH = W // DEC
ITERS = 4
RIDGE_TERM = 0.1
FULL_PRECISION = lax.Precision.HIGHEST
BOTH = ("row", "col")
ROWS_A = 256
BANDS_B = 16
RIM = 24
RIM_MULTI = 16
PAIRS = [(i, j) for i in range(ITERS + 1) for j in range(i, ITERS + 1)]
TRUST = 2.0e4
VMEM_LIMIT = 48 * 1024 * 1024


def params():
    return pltpu.CompilerParams(vmem_limit_bytes=VMEM_LIMIT)


def whole(shape):
    return pl.BlockSpec(shape, lambda *_: (0,) * len(shape))


SMEM = pl.BlockSpec(memory_space=pltpu.SMEM)


def multi_kernel(columns, band, response, image, out, gram, pairs):
    depth = columns.shape[0]

    @pl.when(pl.program_id(0) == 0)
    def _():
        wide = columns[...].astype(jnp.float32)
        merged = jnp.dot(
            response[...], band[...], precision=FULL_PRECISION, preferred_element_type=jnp.float32
        )
        for k in range(2):
            pairs[k * depth : (k + 1) * depth, :] = (merged[k : k + 1, :] * wide).astype(jnp.bfloat16)
        gram[...] = lax.dot_general(
            columns[...], columns[...], (((0,), (0,)), ((), ())), preferred_element_type=jnp.float32
        )

    total = jnp.dot(image[0], pairs[:depth, :], preferred_element_type=jnp.float32)
    total += jnp.dot(image[1], pairs[depth:, :], preferred_element_type=jnp.float32)
    out[...] = total.astype(jnp.bfloat16)


def contract_multi(columns, band, response, image):
    bands, rows, depth = image.shape
    rank = columns.shape[1]
    return pl.pallas_call(
        multi_kernel,
        grid=(rows // ROWS_A,),
        in_specs=[
            whole(columns.shape),
            whole(band.shape),
            whole(response.shape),
            pl.BlockSpec((bands, ROWS_A, depth), lambda i: (0, i, 0)),
        ],
        out_specs=[pl.BlockSpec((ROWS_A, rank), lambda i: (i, 0)), whole((rank, rank))],
        out_shape=[
            jax.ShapeDtypeStruct((rows, rank), jnp.bfloat16),
            jax.ShapeDtypeStruct((rank, rank), jnp.float32),
        ],
        scratch_shapes=[pltpu.VMEM((bands * depth, rank), jnp.bfloat16)],
        compiler_params=params(),
        name="contract_multi",
    )(columns, band, response, image)


def coarse_kernel(taps, columns, before, after, coarse, gram, wide):
    edge = before.shape[0]
    size = columns.shape[0]
    wide[:edge, :] = before[...].astype(jnp.float32)
    wide[edge : edge + size, :] = columns[...].astype(jnp.float32)
    wide[edge + size :, :] = after[...].astype(jnp.float32)
    total = jnp.zeros(coarse.shape, jnp.float32)
    for offset in range(-W, W + 1):
        total += taps[offset + W] * wide[pl.ds(edge + offset, size // DEC, stride=DEC), :]
    coarse[...] = total
    gram[...] = lax.dot_general(
        total, total, (((0,), (0,)), ((), ())), precision=FULL_PRECISION,
        preferred_element_type=jnp.float32,
    )


def coarsen(taps, columns, before, after):
    size, rank = columns.shape
    return pl.pallas_call(
        coarse_kernel,
        in_specs=[SMEM] + [whole(a.shape) for a in (columns, before, after)],
        out_specs=[whole((size // DEC, rank)), whole((rank, rank))],
        out_shape=[
            jax.ShapeDtypeStruct((size // DEC, rank), jnp.float32),
            jax.ShapeDtypeStruct((rank, rank), jnp.float32),
        ],
        scratch_shapes=[pltpu.VMEM((size + 2 * before.shape[0], rank), jnp.float32)],
        compiler_params=params(),
        name="coarsen",
    )(taps, columns, before, after)


def hyper_kernel(coarse, band, image, out, total):
    step = pl.program_id(0)
    field = coarse[...]
    pairs = jnp.concatenate(
        [(band[k : k + 1, :] * field).astype(jnp.bfloat16) for k in range(BANDS_B)], axis=0
    )
    pixels = jnp.concatenate([image[k] for k in range(BANDS_B)], axis=1)
    part = jnp.dot(pixels, pairs, preferred_element_type=jnp.float32)

    @pl.when(step == 0)
    def _():
        total[...] = part

    @pl.when(step > 0)
    def _():
        total[...] += part

    @pl.when(step == pl.num_programs(0) - 1)
    def _():
        out[...] = total[...].astype(jnp.bfloat16)


def contract_hyper(coarse, band, image):
    bands, rows, depth = image.shape
    rank = coarse.shape[1]
    return pl.pallas_call(
        hyper_kernel,
        grid=(bands // BANDS_B,),
        in_specs=[
            whole(coarse.shape),
            pl.BlockSpec((BANDS_B, rank), lambda i: (i, 0)),
            pl.BlockSpec((BANDS_B, rows, depth), lambda i: (i, 0, 0)),
        ],
        out_specs=whole((rows, rank)),
        out_shape=jax.ShapeDtypeStruct((rows, rank), jnp.bfloat16),
        scratch_shapes=[pltpu.VMEM((rows, rank), jnp.float32)],
        compiler_params=params(),
        name="contract_hyper",
    )(coarse, band, image)


def two_halves(matrix):
    high = matrix.astype(jnp.bfloat16)
    low = (matrix - high.astype(jnp.float32)).astype(jnp.bfloat16)
    return high, low


def operator_kernel(
    taps, band, response, column_gram, coarse_gram, hyper_out, multi_out, hyper_w, multi_w, bound
):
    rank = band.shape[1]

    def gram_of(values):
        return lax.dot_general(
            values, values, (((0,), (0,)), ((), ())), precision=FULL_PRECISION,
            preferred_element_type=jnp.float32,
        )

    merged = jnp.dot(
        response[...], band[...], precision=FULL_PRECISION, preferred_element_type=jnp.float32
    )
    merged_gram = gram_of(merged)
    hyper = coarse_gram[...] * gram_of(band[...])
    multi = column_gram[...] * merged_gram
    eye = (
        lax.broadcasted_iota(jnp.int32, (rank, rank), 0)
        == lax.broadcasted_iota(jnp.int32, (rank, rank), 1)
    ).astype(jnp.float32)
    multi = multi + RIDGE_TERM * eye
    hyper_out[...] = hyper
    multi_out[...] = multi
    squared = jnp.float32(0.0)
    for phase in range(DEC):
        in_phase = jnp.float32(0.0)
        for offset in range(-W, W + 1):
            if offset % DEC == phase:
                in_phase = in_phase + taps[offset + W]
        squared = squared + in_phase * in_phase
    largest = squared * hyper + multi

    def trace(values):
        return jnp.sum(jnp.sum(values * eye, axis=1, keepdims=True), axis=0, keepdims=True)

    power = largest / trace(largest)
    for _ in range(4):
        power = jnp.dot(power, power, preferred_element_type=jnp.float32)
        power = power / trace(power)
    value = jnp.sum(jnp.sum(power * largest, axis=1, keepdims=True), axis=0, keepdims=True)
    top = 1.1 * value
    bound[...] = jnp.broadcast_to(top, bound.shape)
    for matrix, weights in ((hyper, hyper_w), (multi, multi_w)):
        high, low = two_halves(matrix * (4.0 / top))
        weights[:rank, :rank] = high
        weights[:rank, rank:] = low
        weights[rank:, :rank] = high
        weights[rank:, rank:] = jnp.zeros_like(high)


def make_operator(taps, band, response, column_gram, coarse_gram):
    rank = band.shape[1]
    square = jax.ShapeDtypeStruct((rank, rank), jnp.float32)
    weights = jax.ShapeDtypeStruct((2 * rank, 2 * rank), jnp.bfloat16)
    bound = jax.ShapeDtypeStruct((8, rank), jnp.float32)
    outs = [square, square, weights, weights, bound]
    return pl.pallas_call(
        operator_kernel,
        in_specs=[SMEM] + [whole(a.shape) for a in (band, response, column_gram, coarse_gram)],
        out_specs=[whole(o.shape) for o in outs],
        out_shape=outs,
        compiler_params=params(),
        name="make_operator",
    )(taps, band, response, column_gram, coarse_gram)


def times(values, weights):
    rank = values.shape[1]
    both = jnp.dot(
        jnp.concatenate(two_halves(values), axis=1), weights, preferred_element_type=jnp.float32
    )
    return both[:, :rank] + both[:, rank:]


def shifted(values, by):
    size = values.shape[0]
    return values if by == 0 else pltpu.roll(values, by % size, 0)


def blur_down(taps, field):
    total = None
    for block in range(-REACH, REACH + 1):
        term = None
        for phase in range(DEC):
            offset = DEC * block + phase
            if offset <= W:
                more = taps[offset + W] * field(phase)
                term = more if term is None else term + more
        term = shifted(term, -block)
        total = term if total is None else total + term
    return total


def blur_up(taps, values, phase):
    total = None
    for block in range(-REACH, REACH + 1):
        offset = DEC * block + phase
        if offset <= W:
            term = taps[offset + W] * shifted(values, block)
            total = term if total is None else total + term
    return total


def sums_kernel(count, place, *refs):
    del place
    own = refs[:2]
    arrived = refs[2 : 2 + 2 * count]
    start = refs[2 + 2 * count]
    multi, hyper, low, high = refs[3 + 2 * count :]
    for which, out in ((0, multi), (1, hyper)):
        total = own[which][...].astype(jnp.float32)
        for number in range(count):
            total += arrived[2 * number + which][...].astype(jnp.float32)
        out[...] = total
    first, second = DEC * RIM_MULTI, DEC * RIM_MULTI + RIM
    for pack, top in ((low, True), (high, False)):
        for source, begin, size in (
            (multi, 0, first),
            (hyper, first, RIM),
            (start, second, DEC * RIM),
        ):
            rows = source.shape[0]
            at = 0 if top else rows - size
            pack[begin : begin + size, :] = source[at : at + size, :]


def add_sums(place, multi_part, hyper_part, arrived, start):
    fine, rank = start.shape
    coarse = fine // DEC
    count = len(arrived) // 2
    pack = jax.ShapeDtypeStruct((DEC * RIM_MULTI + RIM + DEC * RIM, rank), jnp.float32)
    outs = [
        jax.ShapeDtypeStruct((fine, rank), jnp.float32),
        jax.ShapeDtypeStruct((coarse, rank), jnp.float32),
        pack,
        pack,
    ]
    return pl.pallas_call(
        functools.partial(sums_kernel, count),
        grid_spec=pltpu.PrefetchScalarGridSpec(
            num_scalar_prefetch=1,
            grid=(1,),
            in_specs=[
                pl.BlockSpec((fine, rank), lambda i, place: (place[0], 0)),
                pl.BlockSpec((coarse, rank), lambda i, place: (place[0], 0)),
            ]
            + [whole(a.shape) for a in arrived]
            + [whole(start.shape)],
            out_specs=[whole(o.shape) for o in outs],
        ),
        out_shape=outs,
        compiler_params=params(),
        name="add_sums",
    )(place, multi_part, hyper_part, *arrived, start)


def basis_kernel(
    devices, taps, multi, hyper, start, before, after, hyper_w, multi_w, bound, basis, products,
    natural, lifted, held,
):
    fine = multi.shape[0]
    coarse = fine // DEC
    wide = coarse + 2 * RIM
    first, second = DEC * RIM_MULTI, DEC * RIM_MULTI + RIM
    own = slice(RIM, RIM + coarse)

    def apply(field):
        lowered = times(blur_down(taps, field), hyper_w[...])
        return [blur_up(taps, lowered, phase) + times(field(phase), multi_w[...]) for phase in range(DEC)]

    natural[: DEC * RIM, :] = before[second:, :]
    natural[DEC * RIM : DEC * RIM + fine, :] = start[...]
    natural[DEC * RIM + fine :, :] = after[second:, :]
    for phase in range(DEC):
        held[1, phase] = natural[pl.ds(phase, wide, stride=DEC), :]
    mapped = apply(lambda phase: held[1, phase])

    lifted[:RIM, :] = before[first:second, :]
    lifted[own, :] = hyper[...]
    lifted[RIM + coarse :, :] = after[first:second, :]
    margin = DEC * (RIM - RIM_MULTI)
    none = jnp.zeros((margin, multi.shape[1]), jnp.float32)
    natural[:margin, :] = none
    natural[margin : DEC * RIM, :] = before[:first, :]
    natural[DEC * RIM : DEC * RIM + fine, :] = multi[...]
    natural[DEC * RIM + fine : 2 * DEC * RIM + fine - margin, :] = after[:first, :]
    natural[2 * DEC * RIM + fine - margin :, :] = none
    quarter = bound[0:1, :] * 0.25
    sums = lifted[...]
    for phase in range(DEC):
        right = natural[pl.ds(phase, wide, stride=DEC), :] + blur_up(taps, sums, phase)
        held[0, phase] = right - quarter * mapped[phase]

    for step in range(ITERS):
        now = step % 2
        mapped = apply(lambda phase: held[now, phase])
        for phase in range(DEC):
            basis[step, phase] = held[now, phase, own, :]
            if step == 0:
                result = 0.5 * mapped[phase] - held[now, phase]
            else:
                result = mapped[phase] - 2.0 * held[now, phase] - held[1 - now, phase]
            if step < ITERS - 1:
                held[1 - now, phase] = result
            else:
                basis[ITERS, phase] = result[own, :]
    rows = []
    for i, j in PAIRS:
        total = jnp.zeros((coarse, multi.shape[1]), jnp.float32)
        for phase in range(DEC):
            total += basis[i, phase] * basis[j, phase]
        rows.append(jnp.sum(total, axis=0, keepdims=True))
    rows.append(jnp.zeros_like(rows[0]))
    block = jnp.concatenate(rows, axis=0)
    for device in range(devices):
        products[device] = block


def make_basis(devices, taps, multi, hyper, start, before, after, hyper_w, multi_w, bound):
    fine, rank = multi.shape
    coarse = fine // DEC
    wide = coarse + 2 * RIM
    arrays = (multi, hyper, start, before, after, hyper_w, multi_w, bound)
    outs = [
        jax.ShapeDtypeStruct((ITERS + 1, DEC, coarse, rank), jnp.float32),
        jax.ShapeDtypeStruct((devices, len(PAIRS) + 1, rank), jnp.float32),
    ]
    return pl.pallas_call(
        functools.partial(basis_kernel, devices),
        in_specs=[SMEM] + [whole(a.shape) for a in arrays],
        out_specs=[whole(o.shape) for o in outs],
        out_shape=outs,
        scratch_shapes=[
            pltpu.VMEM((DEC * wide, rank), jnp.float32),
            pltpu.VMEM((wide, rank), jnp.float32),
            pltpu.VMEM((2, DEC, wide, rank), jnp.float32),
        ],
        compiler_params=params(),
        name="make_basis",
    )(taps, *arrays)


def advance_kernel(products, basis, start, bound, solution, residual, amplified):
    count = ITERS + 1
    sums = jnp.sum(products[...], axis=0)
    sums = jnp.sum(sums, axis=1, keepdims=True)
    inner = {}
    for number, (i, j) in enumerate(PAIRS):
        inner[i, j] = inner[j, i] = sums[number : number + 1, :]
    zero = jnp.zeros((1, 1), jnp.float32)
    one = jnp.ones((1, 1), jnp.float32)

    def mapped_of(coefficients):
        result = [2.0 * c for c in coefficients] + [zero] * (count - len(coefficients))
        for j, c in enumerate(coefficients):
            if j + 1 < count:
                result[j + 1] = result[j + 1] + (2.0 * c if j == 0 else c)
            if j > 0:
                result[j - 1] = result[j - 1] + c
        return result

    def product(first, second):
        total = spread = zero
        for i, a in enumerate(first):
            if a is zero:
                continue
            for j, b in enumerate(second):
                if b is zero:
                    continue
                term = a * b * inner[i, j]
                total = total + term
                spread = spread + jnp.abs(term)
        return total, spread / jnp.abs(total)

    walked = [zero] * ITERS
    rest = [one] + [zero] * ITERS
    heading = [one]
    norm = inner[0, 0]
    worst = zero
    for iteration in range(ITERS):
        mapped = mapped_of(heading)
        mapped = mapped[: iteration + 2]
        curved, spread = product(heading, mapped)
        worst = jnp.maximum(worst, spread)
        step = norm / curved
        for j, c in enumerate(heading):
            walked[j] = walked[j] + step * c
        for j, c in enumerate(mapped):
            rest[j] = rest[j] - step * c
        if iteration < ITERS - 1:
            active = rest[: iteration + 2]
            following, spread = product(active, active)
            worst = jnp.maximum(worst, spread)
            ratio = following / norm
            heading = [
                c + ratio * heading[j] if j < len(heading) else c for j, c in enumerate(active)
            ]
            norm = following
    amplified[...] = jnp.broadcast_to(worst, amplified.shape)
    scale = 4.0 / bound[0:1, 0:1]
    walked = [c * scale for c in walked]
    coarse = basis.shape[2]
    for phase in range(DEC):
        rows = pl.ds(phase, coarse, stride=DEC)
        total = start[rows, :]
        for j in range(ITERS):
            total += walked[j] * basis[j, phase]
        solution[rows, :] = total
        total = rest[0] * basis[0, phase]
        for j in range(1, count):
            total += rest[j] * basis[j, phase]
        residual[rows, :] = total


def advance(products, basis, start, bound):
    rank = start.shape[1]
    outs = [
        jax.ShapeDtypeStruct(start.shape, jnp.float32),
        jax.ShapeDtypeStruct(start.shape, jnp.float32),
        jax.ShapeDtypeStruct((8, rank), jnp.float32),
    ]
    arrays = (products, basis, start, bound)
    return pl.pallas_call(
        advance_kernel,
        in_specs=[whole(a.shape) for a in arrays],
        out_specs=[whole(o.shape) for o in outs],
        out_shape=outs,
        compiler_params=params(),
        name="advance",
    )(*arrays)


def to_next(values, axis, count):
    return lax.ppermute(values, axis, [(i, (i + 1) % count) for i in range(count)])


def to_previous(values, axis, count):
    return lax.ppermute(values, axis, [((i + 1) % count, i) for i in range(count)])


def step_by_step(taps, multi, hyper, start, hyper_gram, multi_gram, devices):
    def widened(values, breadth):
        return jnp.concatenate(
            [
                to_next(values[-breadth:], BOTH, devices),
                values,
                to_previous(values[:breadth], BOTH, devices),
            ]
        )

    def down(values):
        rows = values.shape[0] // DEC
        parts = values.reshape(rows, DEC, -1)
        size = rows - 2 * REACH
        total = 0.0
        for offset in range(-W, W + 1):
            block, phase = divmod(offset, DEC)
            total = total + taps[offset + W] * lax.slice_in_dim(
                parts[:, phase], REACH + block, REACH + block + size, axis=0
            )
        return total

    def up(values):
        size = values.shape[0] - 2 * REACH
        phases = []
        for phase in range(DEC):
            total = 0.0
            for block in range(-REACH, REACH + 1):
                offset = DEC * block + phase
                if offset <= W:
                    total = total + taps[offset + W] * lax.slice_in_dim(
                        values, REACH - block, REACH - block + size, axis=0
                    )
            phases.append(total)
        return jnp.stack(phases, axis=1).reshape(DEC * size, -1)

    def operate(values):
        lowered = jnp.dot(down(widened(values, 2 * W)), hyper_gram, precision=FULL_PRECISION)
        return up(lowered) + jnp.dot(values, multi_gram, precision=FULL_PRECISION)

    def inner_sum(first, second):
        return lax.psum(jnp.sum(first * second), BOTH)

    solution = start
    residual = up(widened(hyper, REACH)) + multi - operate(solution)
    direction = residual
    norm = inner_sum(residual, residual)

    def iterate(_, state):
        solution, residual, direction, norm = state
        mapped = operate(direction)
        step = norm / inner_sum(direction, mapped)
        solution = solution + step * direction
        residual = residual - step * mapped
        following = inner_sum(residual, residual)
        return solution, residual, residual + following / norm * direction, following

    solution, residual, _, _ = lax.fori_loop(0, ITERS, iterate, (solution, residual, direction, norm))
    return solution, residual


def body(
    multispectral, hyperspectral, row_start, col_factor, band_factor, response, blur_taps, offsets
):
    across = lax.axis_size("col")
    devices = across * lax.axis_size("row")
    place = lax.axis_index("col")
    spread = jnp.arange(-W, W + 1, dtype=jnp.int32)
    taps = jnp.sum(
        jnp.where(offsets[:, None] == spread[None, :], blur_taps[:, None], jnp.float32(0.0)), axis=0
    )
    columns = lax.all_gather(col_factor.T, "row", axis=0, tiled=True).T
    edge = 2 * W
    before = to_next(columns[-edge:], "col", across)
    after = to_previous(columns[:edge], "col", across)
    multi_part, column_part = contract_multi(columns, band_factor, response, multispectral)

    fine = row_start.shape[0]

    def exchange(values, size):
        arrived = []
        for distance in range(1, across):
            piece = lax.dynamic_slice_in_dim(values, (place + distance) % across * size, size, 0)
            arrived.append(
                lax.ppermute(piece, "col", [(i, (i + distance) % across) for i in range(across)])
            )
        return arrived

    multi_arrived = exchange(multi_part, fine)
    coarse, coarse_part = coarsen(taps, columns, before, after)
    column_gram, coarse_gram = lax.psum((column_part, coarse_part), "col")
    hyper_part = contract_hyper(coarse, band_factor, hyperspectral)
    hyper_arrived = exchange(hyper_part, fine // DEC)
    hyper_gram, multi_gram, hyper_w, multi_w, bound = make_operator(
        taps, band_factor, response, column_gram, coarse_gram
    )
    arrived = [a for pair in zip(multi_arrived, hyper_arrived) for a in pair]
    multi, hyper, low, high = add_sums(place[None], multi_part, hyper_part, arrived, row_start)
    before_rows = to_next(high, BOTH, devices)
    after_rows = to_previous(low, BOTH, devices)
    basis, products = make_basis(
        devices, taps, multi, hyper, row_start, before_rows, after_rows, hyper_w, multi_w, bound
    )
    products = lax.all_to_all(products, BOTH, 0, 0, tiled=True)
    solution, residual, amplified = advance(products, basis, row_start, bound)
    return lax.cond(
        amplified[0, 0] < TRUST,
        lambda: (solution, residual),
        lambda: step_by_step(taps, multi, hyper, row_start, hyper_gram, multi_gram, devices),
    )


def solution(mesh):
    in_specs = (
        P(None, "row", "col"),
        P(None, "row", "col"),
        P(("row", "col"), None),
        P("col", "row"),
        P(),
        P(),
        P(),
        P(),
    )
    out_specs = (P(("row", "col"), None), P(("row", "col"), None))
    return jax.shard_map(body, mesh=mesh, in_specs=in_specs, out_specs=out_specs, check_vma=False)
```

```python
import functools

import jax
import jax.numpy as jnp
from jax import lax
from jax.experimental import pallas as pl
from jax.experimental.pallas import tpu as pltpu
from jax.sharding import PartitionSpec as P

DEC = 4
W = 8
REACH = W // DEC
ITERS = 4
RIDGE_TERM = 0.1
FULL_PRECISION = lax.Precision.HIGHEST
BOTH = ("row", "col")
ROWS_A = 256
BANDS_B = 16
RIM = 24
RIM_MULTI = 16
PAIRS = [(i, j) for i in range(ITERS + 1) for j in range(i, ITERS + 1)]
TRUST = 2.0e4
EDGE = 16
VMEM_LIMIT = 48 * 1024 * 1024


def params():
    return pltpu.CompilerParams(vmem_limit_bytes=VMEM_LIMIT)


def whole(shape):
    return pl.BlockSpec(shape, lambda *_: (0,) * len(shape))


SMEM = pl.BlockSpec(memory_space=pltpu.SMEM)


def in_hbm(values):
    return pltpu.with_memory_space_constraint(values, pltpu.HBM)


def two_halves(matrix):
    high = matrix.astype(jnp.bfloat16)
    low = (matrix - high.astype(jnp.float32)).astype(jnp.bfloat16)
    return high, low


def gram_of(values):
    return lax.dot_general(
        values, values, (((0,), (0,)), ((), ())), precision=FULL_PRECISION,
        preferred_element_type=jnp.float32,
    )


def multi_kernel(
    share, taps, place, gathered, band, response, image, out, coarse, gram, pairs, wide, grams
):
    depth = image.shape[2]
    rank = out.shape[1]
    edge = EDGE

    @pl.when(pl.program_id(0) == 0)
    def _():
        for start in range(0, depth, rank):
            square = gathered[:, start : start + rank].astype(jnp.float32)
            wide[edge + start : edge + start + rank, :] = square.T
        edges = gathered[:, depth : depth + rank].astype(jnp.float32).T
        wide[:edge, :] = edges[:edge, :]
        wide[edge + depth :, :] = edges[edge : 2 * edge, :]
        columns = wide[edge : edge + depth, :]
        merged = jnp.dot(
            response[...], band[...], precision=FULL_PRECISION, preferred_element_type=jnp.float32
        )
        for k in range(2):
            pairs[k * depth : (k + 1) * depth, :] = (merged[k : k + 1, :] * columns).astype(
                jnp.bfloat16
            )
        total = jnp.zeros(coarse.shape, jnp.float32)
        for offset in range(-W, W + 1):
            total += taps[offset + W] * wide[pl.ds(edge + offset, depth // DEC, stride=DEC), :]
        coarse[...] = total
        exact = columns.astype(jnp.bfloat16)
        grams[0] = lax.dot_general(
            exact, exact, (((0,), (0,)), ((), ())), preferred_element_type=jnp.float32
        )
        grams[1] = gram_of(total)
        first = pl.multiple_of(place[0] * share, share)
        halves = two_halves(
            jnp.concatenate([grams[0, pl.ds(first, share), :], grams[1, pl.ds(first, share), :]])
        )
        gram[: 2 * share, :] = halves[0]
        gram[2 * share :, :] = halves[1]

    total = jnp.dot(image[0], pairs[:depth, :], preferred_element_type=jnp.float32)
    total += jnp.dot(image[1], pairs[depth:, :], preferred_element_type=jnp.float32)
    out[...] = total.astype(jnp.bfloat16)


def contract_multi(share, taps, place, gathered, band, response, image):
    bands, rows, depth = image.shape
    rank = band.shape[1]
    outs = [
        jax.ShapeDtypeStruct((rows, rank), jnp.bfloat16),
        jax.ShapeDtypeStruct((depth // DEC, rank), jnp.float32),
        jax.ShapeDtypeStruct((4 * share, rank), jnp.bfloat16),
    ]
    return pl.pallas_call(
        functools.partial(multi_kernel, share),
        grid=(rows // ROWS_A,),
        in_specs=[SMEM, SMEM]
        + [whole(a.shape) for a in (gathered, band, response)]
        + [pl.BlockSpec((bands, ROWS_A, depth), lambda i: (0, i, 0))],
        out_specs=[pl.BlockSpec((ROWS_A, rank), lambda i: (i, 0))]
        + [whole(o.shape) for o in outs[1:]],
        out_shape=outs,
        scratch_shapes=[
            pltpu.VMEM((bands * depth, rank), jnp.bfloat16),
            pltpu.VMEM((depth + 2 * EDGE, rank), jnp.float32),
            pltpu.VMEM((2, rank, rank), jnp.float32),
        ],
        compiler_params=params(),
        name="contract_multi",
    )(taps, place, gathered, band, response, in_hbm(image))


def hyper_kernel(coarse, band, image, out, total):
    step = pl.program_id(0)
    field = coarse[...]
    pairs = jnp.concatenate(
        [(band[k : k + 1, :] * field).astype(jnp.bfloat16) for k in range(BANDS_B)], axis=0
    )
    pixels = jnp.concatenate([image[k] for k in range(BANDS_B)], axis=1)
    part = jnp.dot(pixels, pairs, preferred_element_type=jnp.float32)

    @pl.when(step == 0)
    def _():
        total[...] = part

    @pl.when(step > 0)
    def _():
        total[...] += part

    @pl.when(step == pl.num_programs(0) - 1)
    def _():
        out[...] = total[...].astype(jnp.bfloat16)


def contract_hyper(coarse, band, image):
    bands, rows, depth = image.shape
    rank = coarse.shape[1]
    return pl.pallas_call(
        hyper_kernel,
        grid=(bands // BANDS_B,),
        in_specs=[
            whole(coarse.shape),
            pl.BlockSpec((BANDS_B, rank), lambda i: (i, 0)),
            pl.BlockSpec((BANDS_B, rows, depth), lambda i: (i, 0, 0)),
        ],
        out_specs=whole((rows, rank)),
        out_shape=jax.ShapeDtypeStruct((rows, rank), jnp.bfloat16),
        scratch_shapes=[pltpu.VMEM((rows, rank), jnp.float32)],
        compiler_params=params(),
        name="contract_hyper",
    )(coarse, band, in_hbm(image))


def operator_kernel(taps, band, response, grams, hyper_out, multi_out, hyper_w, multi_w, bound):
    rank = band.shape[1]
    shares = grams.shape[0]
    share = grams.shape[1] // 2
    column_gram = jnp.concatenate([grams[i, :share, :] for i in range(shares)], axis=0)
    coarse_gram = jnp.concatenate([grams[i, share:, :] for i in range(shares)], axis=0)
    merged = jnp.dot(
        response[...], band[...], precision=FULL_PRECISION, preferred_element_type=jnp.float32
    )
    hyper = coarse_gram * gram_of(band[...])
    multi = column_gram * gram_of(merged)
    eye = (
        lax.broadcasted_iota(jnp.int32, (rank, rank), 0)
        == lax.broadcasted_iota(jnp.int32, (rank, rank), 1)
    ).astype(jnp.float32)
    multi = multi + RIDGE_TERM * eye
    hyper_out[...] = hyper
    multi_out[...] = multi
    squared = jnp.float32(0.0)
    for phase in range(DEC):
        in_phase = jnp.float32(0.0)
        for offset in range(-W, W + 1):
            if offset % DEC == phase:
                in_phase = in_phase + taps[offset + W]
        squared = squared + in_phase * in_phase
    largest = squared * hyper + multi

    def trace(values):
        return jnp.sum(jnp.sum(values * eye, axis=1, keepdims=True), axis=0, keepdims=True)

    power = largest / trace(largest)
    for _ in range(4):
        power = jnp.dot(power, power, preferred_element_type=jnp.float32)
        power = power / trace(power)
    value = jnp.sum(jnp.sum(power * largest, axis=1, keepdims=True), axis=0, keepdims=True)
    top = 1.1 * value
    bound[...] = jnp.broadcast_to(top, bound.shape)
    for matrix, weights in ((hyper, hyper_w), (multi, multi_w)):
        high, low = two_halves(matrix * (4.0 / top))
        weights[:rank, :rank] = high
        weights[:rank, rank:] = low
        weights[rank:, :rank] = high
        weights[rank:, rank:] = jnp.zeros_like(high)


def make_operator(taps, band, response, grams):
    rank = band.shape[1]
    square = jax.ShapeDtypeStruct((rank, rank), jnp.float32)
    weights = jax.ShapeDtypeStruct((2 * rank, 2 * rank), jnp.bfloat16)
    bound = jax.ShapeDtypeStruct((8, rank), jnp.float32)
    outs = [square, square, weights, weights, bound]
    return pl.pallas_call(
        operator_kernel,
        in_specs=[SMEM] + [whole(a.shape) for a in (band, response, grams)],
        out_specs=[whole(o.shape) for o in outs],
        out_shape=outs,
        compiler_params=params(),
        name="make_operator",
    )(taps, band, response, grams)


def times(values, weights):
    rank = values.shape[1]
    both = jnp.dot(
        jnp.concatenate(two_halves(values), axis=1), weights, preferred_element_type=jnp.float32
    )
    return both[:, :rank] + both[:, rank:]


def shifted(values, by):
    size = values.shape[0]
    return values if by == 0 else pltpu.roll(values, by % size, 0)


def blur_down(taps, field):
    total = None
    for block in range(-REACH, REACH + 1):
        term = None
        for phase in range(DEC):
            offset = DEC * block + phase
            if offset <= W:
                more = taps[offset + W] * field(phase)
                term = more if term is None else term + more
        term = shifted(term, -block)
        total = term if total is None else total + term
    return total


def blur_up(taps, values, phase):
    total = None
    for block in range(-REACH, REACH + 1):
        offset = DEC * block + phase
        if offset <= W:
            term = taps[offset + W] * shifted(values, block)
            total = term if total is None else total + term
    return total


def sums_kernel(count, place, *refs):
    del place
    own = refs[:2]
    arrived = refs[2 : 2 + 2 * count]
    start = refs[2 + 2 * count]
    multi, hyper, low, high = refs[3 + 2 * count :]
    for which, out in ((0, multi), (1, hyper)):
        total = own[which][...].astype(jnp.float32)
        for number in range(count):
            total += arrived[2 * number + which][: out.shape[0], :].astype(jnp.float32)
        out[...] = total
    first, second = DEC * RIM_MULTI, DEC * RIM_MULTI + RIM
    for pack, top in ((low, True), (high, False)):
        for source, begin, size in (
            (multi, 0, first),
            (hyper, first, RIM),
            (start, second, DEC * RIM),
        ):
            rows = source.shape[0]
            at = 0 if top else rows - size
            pack[begin : begin + size, :] = source[at : at + size, :]


def add_sums(place, multi_part, hyper_part, arrived, start):
    fine, rank = start.shape
    coarse = fine // DEC
    count = len(arrived) // 2
    pack = jax.ShapeDtypeStruct((DEC * RIM_MULTI + RIM + DEC * RIM, rank), jnp.float32)
    outs = [
        jax.ShapeDtypeStruct((fine, rank), jnp.float32),
        jax.ShapeDtypeStruct((coarse, rank), jnp.float32),
        pack,
        pack,
    ]
    return pl.pallas_call(
        functools.partial(sums_kernel, count),
        grid_spec=pltpu.PrefetchScalarGridSpec(
            num_scalar_prefetch=1,
            grid=(1,),
            in_specs=[
                pl.BlockSpec((fine, rank), lambda i, place: (place[0], 0)),
                pl.BlockSpec((coarse, rank), lambda i, place: (place[0], 0)),
            ]
            + [whole(a.shape) for a in arrived]
            + [whole(start.shape)],
            out_specs=[whole(o.shape) for o in outs],
        ),
        out_shape=outs,
        compiler_params=params(),
        name="add_sums",
    )(place, multi_part, hyper_part, *arrived, start)


def basis_kernel(
    devices, taps, multi, hyper, start, before, after, hyper_w, multi_w, bound, basis, products,
    natural, lifted, held,
):
    fine = multi.shape[0]
    coarse = fine // DEC
    wide = coarse + 2 * RIM
    first, second = DEC * RIM_MULTI, DEC * RIM_MULTI + RIM
    own = slice(RIM, RIM + coarse)

    def apply(field):
        lowered = times(blur_down(taps, field), hyper_w[...])
        return [blur_up(taps, lowered, phase) + times(field(phase), multi_w[...]) for phase in range(DEC)]

    natural[: DEC * RIM, :] = before[second:, :]
    natural[DEC * RIM : DEC * RIM + fine, :] = start[...]
    natural[DEC * RIM + fine :, :] = after[second:, :]
    for phase in range(DEC):
        held[1, phase] = natural[pl.ds(phase, wide, stride=DEC), :]
    mapped = apply(lambda phase: held[1, phase])

    lifted[:RIM, :] = before[first:second, :]
    lifted[own, :] = hyper[...]
    lifted[RIM + coarse :, :] = after[first:second, :]
    margin = DEC * (RIM - RIM_MULTI)
    none = jnp.zeros((margin, multi.shape[1]), jnp.float32)
    natural[:margin, :] = none
    natural[margin : DEC * RIM, :] = before[:first, :]
    natural[DEC * RIM : DEC * RIM + fine, :] = multi[...]
    natural[DEC * RIM + fine : 2 * DEC * RIM + fine - margin, :] = after[:first, :]
    natural[2 * DEC * RIM + fine - margin :, :] = none
    quarter = bound[0:1, :] * 0.25
    sums = lifted[...]
    for phase in range(DEC):
        right = natural[pl.ds(phase, wide, stride=DEC), :] + blur_up(taps, sums, phase)
        held[0, phase] = right - quarter * mapped[phase]

    for step in range(ITERS):
        now = step % 2
        mapped = apply(lambda phase: held[now, phase])
        for phase in range(DEC):
            basis[step, phase] = held[now, phase, own, :]
            if step == 0:
                result = 0.5 * mapped[phase] - held[now, phase]
            else:
                result = mapped[phase] - 2.0 * held[now, phase] - held[1 - now, phase]
            if step < ITERS - 1:
                held[1 - now, phase] = result
            else:
                basis[ITERS, phase] = result[own, :]
    rows = []
    for i, j in PAIRS:
        total = jnp.zeros((coarse, multi.shape[1]), jnp.float32)
        for phase in range(DEC):
            total += basis[i, phase] * basis[j, phase]
        rows.append(jnp.sum(total, axis=0, keepdims=True))
    rows.append(jnp.zeros_like(rows[0]))
    block = jnp.concatenate(rows, axis=0)
    lanes = block.shape[1]
    half = block.shape[0] // 2
    block = block + pltpu.roll(block, lanes // 2, 1)
    lane = lax.broadcasted_iota(jnp.int32, (half, lanes), 1)
    block = jnp.where(lane < lanes // 2, block[:half, :], block[half:, :])
    for device in range(devices):
        products[device] = block


def make_basis(devices, taps, multi, hyper, start, before, after, hyper_w, multi_w, bound):
    fine, rank = multi.shape
    coarse = fine // DEC
    wide = coarse + 2 * RIM
    arrays = (multi, hyper, start, before, after, hyper_w, multi_w, bound)
    outs = [
        jax.ShapeDtypeStruct((ITERS + 1, DEC, coarse, rank), jnp.float32),
        jax.ShapeDtypeStruct((devices, (len(PAIRS) + 1) // 2, rank), jnp.float32),
    ]
    return pl.pallas_call(
        functools.partial(basis_kernel, devices),
        in_specs=[SMEM] + [whole(a.shape) for a in arrays],
        out_specs=[whole(o.shape) for o in outs],
        out_shape=outs,
        scratch_shapes=[
            pltpu.VMEM((DEC * wide, rank), jnp.float32),
            pltpu.VMEM((wide, rank), jnp.float32),
            pltpu.VMEM((2, DEC, wide, rank), jnp.float32),
        ],
        compiler_params=params(),
        name="make_basis",
    )(taps, *arrays)


def coefficients_kernel(products, bound, out, trusted):
    count = ITERS + 1
    folded = jnp.sum(products[...], axis=0)
    lanes = folded.shape[1]
    lane = lax.broadcasted_iota(jnp.int32, folded.shape, 1)
    left = jnp.sum(jnp.where(lane < lanes // 2, folded, 0.0), axis=1, keepdims=True)
    right = jnp.sum(jnp.where(lane < lanes // 2, 0.0, folded), axis=1, keepdims=True)
    sums = jnp.concatenate([left, right], axis=0)
    inner = {}
    for number, (i, j) in enumerate(PAIRS):
        inner[i, j] = inner[j, i] = sums[number : number + 1, :]
    zero = jnp.zeros((1, 1), jnp.float32)
    one = jnp.ones((1, 1), jnp.float32)

    def mapped_of(coefficients):
        result = [2.0 * c for c in coefficients] + [zero] * (count - len(coefficients))
        for j, c in enumerate(coefficients):
            if j + 1 < count:
                result[j + 1] = result[j + 1] + (2.0 * c if j == 0 else c)
            if j > 0:
                result[j - 1] = result[j - 1] + c
        return result

    def product(first, second):
        total = spread = zero
        for i, a in enumerate(first):
            if a is zero:
                continue
            for j, b in enumerate(second):
                if b is zero:
                    continue
                term = a * b * inner[i, j]
                total = total + term
                spread = spread + jnp.abs(term)
        return total, spread / jnp.abs(total)

    walked = [zero] * ITERS
    rest = [one] + [zero] * ITERS
    heading = [one]
    norm = inner[0, 0]
    worst = zero
    for iteration in range(ITERS):
        mapped = mapped_of(heading)
        mapped = mapped[: iteration + 2]
        curved, spread = product(heading, mapped)
        worst = jnp.maximum(worst, spread)
        step = norm / curved
        for j, c in enumerate(heading):
            walked[j] = walked[j] + step * c
        for j, c in enumerate(mapped):
            rest[j] = rest[j] - step * c
        if iteration < ITERS - 1:
            active = rest[: iteration + 2]
            following, spread = product(active, active)
            worst = jnp.maximum(worst, spread)
            ratio = following / norm
            heading = [
                c + ratio * heading[j] if j < len(heading) else c for j, c in enumerate(active)
            ]
            norm = following
    scale = 4.0 / bound[0:1, 0:1]
    rows = [c * scale for c in walked] + rest
    rows = jnp.concatenate(rows + [zero] * (out.shape[0] - len(rows)), axis=0)
    out[...] = jnp.broadcast_to(rows, out.shape)
    trusted[0] = jnp.where(worst < TRUST, 1, 0)[0, 0]


def make_coefficients(products, bound):
    rank = bound.shape[1]
    return pl.pallas_call(
        coefficients_kernel,
        in_specs=[whole(products.shape), whole(bound.shape)],
        out_specs=[whole((16, rank)), SMEM],
        out_shape=[
            jax.ShapeDtypeStruct((16, rank), jnp.float32),
            jax.ShapeDtypeStruct((1,), jnp.int32),
        ],
        compiler_params=params(),
        name="make_coefficients",
    )(products, bound)


def combine_kernel(coefficients, basis, start, solution, residual):
    coarse = basis.shape[2]
    for phase in range(DEC):
        rows = pl.ds(phase, coarse, stride=DEC)
        total = start[rows, :]
        for j in range(ITERS):
            total += coefficients[j : j + 1, :] * basis[j, phase]
        solution[rows, :] = total
        total = coefficients[ITERS : ITERS + 1, :] * basis[0, phase]
        for j in range(1, ITERS + 1):
            total += coefficients[ITERS + j : ITERS + j + 1, :] * basis[j, phase]
        residual[rows, :] = total


def combine(coefficients, basis, start):
    arrays = (coefficients, basis, start)
    return pl.pallas_call(
        combine_kernel,
        in_specs=[whole(a.shape) for a in arrays],
        out_specs=[whole(start.shape)] * 2,
        out_shape=[jax.ShapeDtypeStruct(start.shape, jnp.float32)] * 2,
        compiler_params=params(),
        name="combine",
    )(*arrays)


def to_next(values, axis, count):
    return lax.ppermute(values, axis, [(i, (i + 1) % count) for i in range(count)])


def to_previous(values, axis, count):
    return lax.ppermute(values, axis, [((i + 1) % count, i) for i in range(count)])


def step_by_step(taps, multi, hyper, start, hyper_gram, multi_gram, devices):
    def widened(values, breadth):
        return jnp.concatenate(
            [
                to_next(values[-breadth:], BOTH, devices),
                values,
                to_previous(values[:breadth], BOTH, devices),
            ]
        )

    def down(values):
        rows = values.shape[0] // DEC
        parts = values.reshape(rows, DEC, -1)
        size = rows - 2 * REACH
        total = 0.0
        for offset in range(-W, W + 1):
            block, phase = divmod(offset, DEC)
            total = total + taps[offset + W] * lax.slice_in_dim(
                parts[:, phase], REACH + block, REACH + block + size, axis=0
            )
        return total

    def up(values):
        size = values.shape[0] - 2 * REACH
        phases = []
        for phase in range(DEC):
            total = 0.0
            for block in range(-REACH, REACH + 1):
                offset = DEC * block + phase
                if offset <= W:
                    total = total + taps[offset + W] * lax.slice_in_dim(
                        values, REACH - block, REACH - block + size, axis=0
                    )
            phases.append(total)
        return jnp.stack(phases, axis=1).reshape(DEC * size, -1)

    def operate(values):
        lowered = jnp.dot(down(widened(values, 2 * W)), hyper_gram, precision=FULL_PRECISION)
        return up(lowered) + jnp.dot(values, multi_gram, precision=FULL_PRECISION)

    def inner_sum(first, second):
        return lax.psum(jnp.sum(first * second), BOTH)

    solution = start
    residual = up(widened(hyper, REACH)) + multi - operate(solution)
    direction = residual
    norm = inner_sum(residual, residual)

    def iterate(_, state):
        solution, residual, direction, norm = state
        mapped = operate(direction)
        step = norm / inner_sum(direction, mapped)
        solution = solution + step * direction
        residual = residual - step * mapped
        following = inner_sum(residual, residual)
        return solution, residual, residual + following / norm * direction, following

    solution, residual, _, _ = lax.fori_loop(0, ITERS, iterate, (solution, residual, direction, norm))
    return solution, residual


def body(
    multispectral, hyperspectral, row_start, col_factor, band_factor, response, blur_taps, offsets
):
    across = lax.axis_size("col")
    devices = across * lax.axis_size("row")
    place = lax.axis_index("col")
    spread = jnp.arange(-W, W + 1, dtype=jnp.int32)
    taps = jnp.sum(
        jnp.where(offsets[:, None] == spread[None, :], blur_taps[:, None], jnp.float32(0.0)), axis=0
    )
    transposed = col_factor.T
    rank = band_factor.shape[1]
    before = to_next(transposed[:, -EDGE:], "col", across)
    after = to_previous(transposed[:, :EDGE], "col", across)
    blank = jnp.zeros((transposed.shape[0], rank - 2 * EDGE), transposed.dtype)
    gathered = lax.all_gather(
        jnp.concatenate([transposed, before, after, blank], axis=1), "row", axis=0, tiled=True
    )
    share = rank // lax.axis_size("row")
    multi_part, coarse, gram_part = contract_multi(
        share, taps, lax.axis_index("row")[None], gathered, band_factor, response, multispectral
    )

    fine = row_start.shape[0]

    def exchange(values, size, more):
        arrived = []
        for distance in range(1, across):
            piece = lax.dynamic_slice_in_dim(values, (place + distance) % across * size, size, 0)
            piece = jnp.concatenate([piece] + more)
            arrived.append(
                lax.ppermute(piece, "col", [(i, (i + distance) % across) for i in range(across)])
            )
        return arrived

    multi_arrived = exchange(multi_part, fine, [gram_part])
    hyper_part = contract_hyper(coarse, band_factor, hyperspectral)
    hyper_arrived = exchange(hyper_part, fine // DEC, [])
    gram = sum(a.astype(jnp.float32) for a in [gram_part] + [m[fine:] for m in multi_arrived])
    gram = gram[: 2 * share] + gram[2 * share :]
    gram, hyper_part = lax.optimization_barrier((gram, hyper_part))
    grams = lax.all_gather(gram, "row")
    hyper_gram, multi_gram, hyper_w, multi_w, bound = make_operator(
        taps, band_factor, response, grams
    )
    arrived = [a for pair in zip(multi_arrived, hyper_arrived) for a in pair]
    multi, hyper, low, high = add_sums(place[None], multi_part, hyper_part, arrived, row_start)
    before_rows = to_next(high, BOTH, devices)
    after_rows = to_previous(low, BOTH, devices)
    basis, products = make_basis(
        devices, taps, multi, hyper, row_start, before_rows, after_rows, hyper_w, multi_w, bound
    )
    products = lax.all_to_all(products, BOTH, 0, 0, tiled=True)
    coefficients, trusted = make_coefficients(products, bound)
    return lax.cond(
        trusted[0] != 0,
        lambda: tuple(combine(coefficients, basis, row_start)),
        lambda: step_by_step(taps, multi, hyper, row_start, hyper_gram, multi_gram, devices),
    )


def solution(mesh):
    in_specs = (
        P(None, "row", "col"),
        P(None, "row", "col"),
        P(("row", "col"), None),
        P("col", "row"),
        P(),
        P(),
        P(),
        P(),
    )
    out_specs = (P(("row", "col"), None), P(("row", "col"), None))
    return jax.shard_map(body, mesh=mesh, in_specs=in_specs, out_specs=out_specs, check_vma=False)
```

```python
import functools

import jax
import jax.numpy as jnp
from jax import lax
from jax.experimental import pallas as pl
from jax.experimental.pallas import tpu as pltpu
from jax.sharding import PartitionSpec as P

DEC = 4
W = 8
REACH = W // DEC
ITERS = 4
RIDGE_TERM = 0.1
FULL_PRECISION = lax.Precision.HIGHEST
BOTH = ("row", "col")
ROWS_A = 512
RIM = 24
RIM_MULTI = 16
PAIRS = [(i, j) for i in range(ITERS + 1) for j in range(i, ITERS + 1)]
TRUST = 2.0e4
EDGE = 16
VMEM_LIMIT = 32 * 1024 * 1024


def params():
    return pltpu.CompilerParams(vmem_limit_bytes=VMEM_LIMIT)


def whole(shape):
    return pl.BlockSpec(shape, lambda *_: (0,) * len(shape))


SMEM = pl.BlockSpec(memory_space=pltpu.SMEM)
VMEM = pl.BlockSpec(memory_space=pltpu.VMEM)


def in_space(values, space):
    return pltpu.with_memory_space_constraint(values, space)


def two_halves(matrix):
    high = matrix.astype(jnp.bfloat16)
    low = (matrix - high.astype(jnp.float32)).astype(jnp.bfloat16)
    return high, low


def gram_of(values):
    return lax.dot_general(
        values, values, (((0,), (0,)), ((), ())), precision=FULL_PRECISION,
        preferred_element_type=jnp.float32,
    )


def load_kernel(parts, *refs):
    count = len(parts)
    copies = []
    for source, target, number in zip(refs[:count], refs[count : 2 * count], parts):
        size = source.shape[0] // number
        for part in range(number):
            rows = pl.ds(part * size, size)
            copies.append(
                pltpu.make_async_copy(
                    source.at[rows], target.at[rows], refs[2 * count].at[len(copies)]
                )
            )
    for copy in copies:
        copy.start()
    for copy in copies:
        copy.wait()


def load(arrays, parts, name):
    size = sum(a.size * a.dtype.itemsize for a in arrays)
    return pl.pallas_call(
        functools.partial(load_kernel, parts),
        in_specs=[pl.BlockSpec(memory_space=pl.ANY)] * len(arrays),
        out_specs=[VMEM] * len(arrays),
        out_shape=[pltpu.VMEM(a.shape, a.dtype) for a in arrays],
        scratch_shapes=[pltpu.SemaphoreType.DMA((sum(parts),))],
        compiler_params=params(),
        cost_estimate=pl.CostEstimate(flops=0, bytes_accessed=2 * size, transcendentals=0),
        name=name,
    )(*[in_space(a, pltpu.HBM) for a in arrays])


def in_rank_order(place, share, pieces, target):
    pair = place[0] // 2
    core = place[0] % 2
    for distance, piece in enumerate(pieces):
        slot = 2 * (pair ^ distance)
        values = piece.astype(jnp.float32)
        first = pl.multiple_of((slot + core) * share, share)
        target[pl.ds(first, share), : values.shape[1]] = values[:share, :]
        second = pl.multiple_of((slot + 1 - core) * share, share)
        target[pl.ds(second, share), : values.shape[1]] = values[share:, :]


def multi_kernel(count, place, band, response, image, *refs):
    pieces = refs[:count]
    out, columns, pairs, ranks = refs[count:]
    depth = image.shape[2]
    rank = out.shape[1]
    in_rank_order(place, pieces[0].shape[0] // 2, [p[...] for p in pieces], ranks)
    for start in range(0, depth, rank):
        columns[start : start + rank, :] = ranks[:, start : start + rank].T
    merged = jnp.dot(
        response[...], band[...], precision=FULL_PRECISION, preferred_element_type=jnp.float32
    )
    field = columns[...]
    for k in range(2):
        pairs[k * depth : (k + 1) * depth, :] = (merged[k : k + 1, :] * field).astype(jnp.bfloat16)
    for start in range(0, out.shape[0], ROWS_A):
        rows = slice(start, start + ROWS_A)
        pixels = jnp.concatenate([image[0, rows, :], image[1, rows, :]], axis=1)
        total = jnp.dot(pixels, pairs[...], preferred_element_type=jnp.float32)
        out[rows, :] = total.astype(jnp.bfloat16)


def contract_multi(place, band, response, image, pieces):
    bands, rows, depth = image.shape
    rank = band.shape[1]
    outs = [
        jax.ShapeDtypeStruct((rows, rank), jnp.bfloat16),
        jax.ShapeDtypeStruct((depth, rank), jnp.float32),
    ]
    return pl.pallas_call(
        functools.partial(multi_kernel, len(pieces)),
        in_specs=[SMEM, whole(band.shape), whole(response.shape), VMEM]
        + [whole(p.shape) for p in pieces],
        out_specs=[whole(o.shape) for o in outs],
        out_shape=outs,
        scratch_shapes=[
            pltpu.VMEM((bands * depth, rank), jnp.bfloat16),
            pltpu.VMEM((rank, depth), jnp.float32),
        ],
        compiler_params=params(),
        cost_estimate=pl.CostEstimate(
            flops=2 * bands * rows * depth * rank, bytes_accessed=1 << 23, transcendentals=0
        ),
        name="contract_multi",
    )(place, band, response, in_space(image, pltpu.VMEM), *pieces)


def hyper_kernel(share, place, taps, columns, before, after, band, image, out, gram, wide, ranks, packed):
    depth, rank = columns.shape
    wide[EDGE : EDGE + depth, :] = columns[...]
    for edge, first in ((before, 0), (after, EDGE + depth)):
        values = edge[...].astype(jnp.float32)
        size = 2 * share
        in_rank_order(
            place, share, [values[i : i + size, :] for i in range(0, rank, size)], ranks
        )
        wide[first : first + EDGE, :] = ranks[...].T[:EDGE, :]
    coarse = jnp.zeros((depth // DEC, rank), jnp.float32)
    for offset in range(-W, W + 1):
        coarse += taps[offset + W] * wide[pl.ds(EDGE + offset, depth // DEC, stride=DEC), :]

    exact = columns[...].astype(jnp.bfloat16)
    fine_gram = lax.dot_general(
        exact, exact, (((0,), (0,)), ((), ())), preferred_element_type=jnp.float32
    )
    coarse_gram = gram_of(coarse)
    down = lax.broadcasted_iota(jnp.int32, (rank, rank), 0)
    along = lax.broadcasted_iota(jnp.int32, (rank, rank), 1)
    packed[:rank, :] = jnp.where(along >= down, fine_gram, coarse_gram)
    diagonal = jnp.sum(jnp.where(along == down, coarse_gram, 0.0), axis=0, keepdims=True)
    packed[rank:, :] = jnp.broadcast_to(diagonal, (packed.shape[0] - rank, rank))
    half = packed.shape[0] // 2
    part = packed[pl.ds(pl.multiple_of(place[0] % 2 * half, 8), half), :]
    high = part.astype(jnp.bfloat16).astype(jnp.float32)
    gram[...] = jnp.concatenate([high, part - high], axis=0).astype(jnp.bfloat16)

    bands = image.shape[0]
    pairs = jnp.concatenate(
        [(band[k : k + 1, :] * coarse).astype(jnp.bfloat16) for k in range(bands)], axis=0
    )
    pixels = jnp.concatenate([image[k] for k in range(bands)], axis=1)
    total = jnp.dot(pixels, pairs, preferred_element_type=jnp.float32)
    out[...] = total.astype(jnp.bfloat16)


def contract_hyper(share, place, taps, columns, before, after, band, image):
    bands, rows, depth = image.shape
    fine, rank = columns.shape
    outs = [
        jax.ShapeDtypeStruct((rows, rank), jnp.bfloat16),
        jax.ShapeDtypeStruct((rank + 16, rank), jnp.bfloat16),
    ]
    return pl.pallas_call(
        functools.partial(hyper_kernel, share),
        in_specs=[SMEM, SMEM] + [whole(a.shape) for a in (columns, before, after, band)] + [VMEM],
        out_specs=[whole(o.shape) for o in outs],
        out_shape=outs,
        scratch_shapes=[
            pltpu.VMEM((fine + 2 * EDGE, rank), jnp.float32),
            pltpu.VMEM((rank, rank), jnp.float32),
            pltpu.VMEM((rank + 16, rank), jnp.float32),
        ],
        compiler_params=params(),
        cost_estimate=pl.CostEstimate(
            flops=2 * bands * rows * depth * rank, bytes_accessed=1 << 24, transcendentals=0
        ),
        name="contract_hyper",
    )(place, taps, columns, before, after, band, in_space(image, pltpu.VMEM))


def operator_kernel(
    place, taps, band, response, own, other, hyper_out, multi_out, hyper_w, multi_w, bound
):
    rank = band.shape[1]
    even = place[0] % 2 == 0
    lower = jnp.where(even, own[...], other[...])
    upper = jnp.where(even, other[...], own[...])
    packed = jnp.concatenate([lower, upper], axis=0)
    diagonal = packed[rank : rank + 1, :]
    packed = packed[:rank, :]
    turned = packed.T
    down = lax.broadcasted_iota(jnp.int32, (rank, rank), 0)
    along = lax.broadcasted_iota(jnp.int32, (rank, rank), 1)
    column_gram = jnp.where(along >= down, packed, turned)
    coarse_gram = jnp.where(along < down, packed, jnp.where(along == down, diagonal, turned))
    merged = jnp.dot(
        response[...], band[...], precision=FULL_PRECISION, preferred_element_type=jnp.float32
    )
    hyper = coarse_gram * gram_of(band[...])
    multi = column_gram * gram_of(merged)
    eye = (along == down).astype(jnp.float32)
    multi = multi + RIDGE_TERM * eye
    hyper_out[...] = hyper
    multi_out[...] = multi
    squared = jnp.float32(0.0)
    for phase in range(DEC):
        in_phase = jnp.float32(0.0)
        for offset in range(-W, W + 1):
            if offset % DEC == phase:
                in_phase = in_phase + taps[offset + W]
        squared = squared + in_phase * in_phase
    largest = squared * hyper + multi

    def trace(values):
        return jnp.sum(jnp.sum(values * eye, axis=1, keepdims=True), axis=0, keepdims=True)

    power = largest / trace(largest)
    for _ in range(4):
        power = jnp.dot(power, power, preferred_element_type=jnp.float32)
        power = power / trace(power)
    value = jnp.sum(jnp.sum(power * largest, axis=1, keepdims=True), axis=0, keepdims=True)
    top = 1.1 * value
    bound[...] = jnp.broadcast_to(top, bound.shape)
    for matrix, weights in ((hyper, hyper_w), (multi, multi_w)):
        high, low = two_halves(matrix * (4.0 / top))
        weights[:rank, :rank] = high
        weights[:rank, rank:] = low
        weights[rank:, :rank] = high
        weights[rank:, rank:] = jnp.zeros_like(high)


def make_operator(place, taps, band, response, own, other):
    rank = band.shape[1]
    square = jax.ShapeDtypeStruct((rank, rank), jnp.float32)
    weights = jax.ShapeDtypeStruct((2 * rank, 2 * rank), jnp.bfloat16)
    bound = jax.ShapeDtypeStruct((8, rank), jnp.float32)
    outs = [square, square, weights, weights, bound]
    return pl.pallas_call(
        operator_kernel,
        in_specs=[SMEM, SMEM] + [whole(a.shape) for a in (band, response, own, other)],
        out_specs=[whole(o.shape) for o in outs],
        out_shape=outs,
        compiler_params=params(),
        name="make_operator",
    )(place, taps, band, response, own, other)


def times(values, weights):
    rank = values.shape[1]
    both = jnp.dot(
        jnp.concatenate(two_halves(values), axis=1), weights, preferred_element_type=jnp.float32
    )
    return both[:, :rank] + both[:, rank:]


def shifted(values, by):
    size = values.shape[0]
    return values if by == 0 else pltpu.roll(values, by % size, 0)


def blur_down(taps, field):
    total = None
    for block in range(-REACH, REACH + 1):
        term = None
        for phase in range(DEC):
            offset = DEC * block + phase
            if offset <= W:
                more = taps[offset + W] * field(phase)
                term = more if term is None else term + more
        term = shifted(term, -block)
        total = term if total is None else total + term
    return total


def blur_up(taps, values, phase):
    total = None
    for block in range(-REACH, REACH + 1):
        offset = DEC * block + phase
        if offset <= W:
            term = taps[offset + W] * shifted(values, block)
            total = term if total is None else total + term
    return total


def sum_kernel(place, own, *refs):
    del place
    total = own[...].astype(jnp.float32)
    for values in refs[:-1]:
        total += values[...].astype(jnp.float32)
    refs[-1][...] = total


def sum_arrived(place, own, arrived):
    shape = arrived[0].shape
    return pl.pallas_call(
        sum_kernel,
        grid_spec=pltpu.PrefetchScalarGridSpec(
            num_scalar_prefetch=1,
            grid=(1,),
            in_specs=[pl.BlockSpec(shape, lambda i, place: (place[0], 0))]
            + [whole(shape) for _ in arrived],
            out_specs=whole(shape),
        ),
        out_shape=jax.ShapeDtypeStruct(shape, jnp.float32),
        compiler_params=params(),
        cost_estimate=pl.CostEstimate(flops=0, bytes_accessed=1 << 26, transcendentals=0),
        name="sum_arrived",
    )(place, own, *arrived)


def sums_kernel(count, place, *refs):
    del place
    own, own_gram, multi, start = refs[:4]
    arrived = refs[4 : 4 + count]
    hyper, gram, low, high = refs[4 + count :]
    rows = hyper.shape[0]
    total = own[...].astype(jnp.float32)
    grams = own_gram[...].astype(jnp.float32)
    for values in arrived:
        total += values[:rows, :].astype(jnp.float32)
        grams += values[rows:, :].astype(jnp.float32)
    hyper[...] = total
    half = gram.shape[0]
    gram[...] = grams[:half, :] + grams[half:, :]
    first, second = DEC * RIM_MULTI, DEC * RIM_MULTI + RIM
    for pack, top in ((low, True), (high, False)):
        for source, begin, size in (
            (multi, 0, first),
            (hyper, first, RIM),
            (start, second, DEC * RIM),
        ):
            rows = source.shape[0]
            at = 0 if top else rows - size
            pack[begin : begin + size, :] = source[at : at + size, :]


def add_sums(place, hyper_part, gram_part, multi, start, arrived):
    fine, rank = start.shape
    coarse = fine // DEC
    pack = jax.ShapeDtypeStruct((DEC * RIM_MULTI + RIM + DEC * RIM, rank), jnp.float32)
    outs = [
        jax.ShapeDtypeStruct((coarse, rank), jnp.float32),
        jax.ShapeDtypeStruct((gram_part.shape[0] // 2, rank), jnp.float32),
        pack,
        pack,
    ]
    return pl.pallas_call(
        functools.partial(sums_kernel, len(arrived)),
        grid_spec=pltpu.PrefetchScalarGridSpec(
            num_scalar_prefetch=1,
            grid=(1,),
            in_specs=[pl.BlockSpec((coarse, rank), lambda i, place: (place[0], 0))]
            + [whole(a.shape) for a in (gram_part, multi, start, *arrived)],
            out_specs=[whole(o.shape) for o in outs],
        ),
        out_shape=outs,
        compiler_params=params(),
        name="add_sums",
    )(place, hyper_part, gram_part, multi, start, *arrived)


def basis_kernel(
    devices, taps, multi, hyper, start, before, after, hyper_w, multi_w, bound, basis, products,
    natural, lifted, held,
):
    fine = multi.shape[0]
    coarse = fine // DEC
    wide = coarse + 2 * RIM
    first, second = DEC * RIM_MULTI, DEC * RIM_MULTI + RIM
    own = slice(RIM, RIM + coarse)

    def apply(field):
        lowered = times(blur_down(taps, field), hyper_w[...])
        return [blur_up(taps, lowered, phase) + times(field(phase), multi_w[...]) for phase in range(DEC)]

    natural[: DEC * RIM, :] = before[second:, :]
    natural[DEC * RIM : DEC * RIM + fine, :] = start[...]
    natural[DEC * RIM + fine :, :] = after[second:, :]
    for phase in range(DEC):
        held[1, phase] = natural[pl.ds(phase, wide, stride=DEC), :]
        basis[ITERS + 1, phase] = held[1, phase, own, :]
    mapped = apply(lambda phase: held[1, phase])

    lifted[:RIM, :] = before[first:second, :]
    lifted[own, :] = hyper[...]
    lifted[RIM + coarse :, :] = after[first:second, :]
    margin = DEC * (RIM - RIM_MULTI)
    none = jnp.zeros((margin, multi.shape[1]), jnp.float32)
    natural[:margin, :] = none
    natural[margin : DEC * RIM, :] = before[:first, :]
    natural[DEC * RIM : DEC * RIM + fine, :] = multi[...]
    natural[DEC * RIM + fine : 2 * DEC * RIM + fine - margin, :] = after[:first, :]
    natural[2 * DEC * RIM + fine - margin :, :] = none
    quarter = bound[0:1, :] * 0.25
    sums = lifted[...]
    for phase in range(DEC):
        right = natural[pl.ds(phase, wide, stride=DEC), :] + blur_up(taps, sums, phase)
        held[0, phase] = right - quarter * mapped[phase]

    for step in range(ITERS):
        now = step % 2
        mapped = apply(lambda phase: held[now, phase])
        for phase in range(DEC):
            basis[step, phase] = held[now, phase, own, :]
            if step == 0:
                result = 0.5 * mapped[phase] - held[now, phase]
            else:
                result = mapped[phase] - 2.0 * held[now, phase] - held[1 - now, phase]
            if step < ITERS - 1:
                held[1 - now, phase] = result
            else:
                basis[ITERS, phase] = result[own, :]
    rows = []
    for i, j in PAIRS:
        total = jnp.zeros((coarse, multi.shape[1]), jnp.float32)
        for phase in range(DEC):
            total += basis[i, phase] * basis[j, phase]
        rows.append(jnp.sum(total, axis=0, keepdims=True))
    rows.append(jnp.zeros_like(rows[0]))
    block = jnp.concatenate(rows, axis=0)
    lanes = block.shape[1]
    half = block.shape[0] // 2
    block = block + pltpu.roll(block, lanes // 2, 1)
    lane = lax.broadcasted_iota(jnp.int32, (half, lanes), 1)
    block = jnp.where(lane < lanes // 2, block[:half, :], block[half:, :])
    for device in range(devices):
        products[device] = block


def make_basis(devices, taps, multi, hyper, start, before, after, hyper_w, multi_w, bound):
    fine, rank = multi.shape
    coarse = fine // DEC
    wide = coarse + 2 * RIM
    arrays = (multi, hyper, start, before, after, hyper_w, multi_w, bound)
    outs = [
        jax.ShapeDtypeStruct((ITERS + 2, DEC, coarse, rank), jnp.float32),
        jax.ShapeDtypeStruct((devices, (len(PAIRS) + 1) // 2, rank), jnp.float32),
    ]
    return pl.pallas_call(
        functools.partial(basis_kernel, devices),
        in_specs=[SMEM] + [whole(a.shape) for a in arrays],
        out_specs=[whole(o.shape) for o in outs],
        out_shape=outs,
        scratch_shapes=[
            pltpu.VMEM((DEC * wide, rank), jnp.float32),
            pltpu.VMEM((wide, rank), jnp.float32),
            pltpu.VMEM((2, DEC, wide, rank), jnp.float32),
        ],
        compiler_params=params(),
        name="make_basis",
    )(taps, *arrays)


def coefficients_kernel(products, bound, out, trusted):
    count = ITERS + 1
    folded = jnp.sum(products[...], axis=0)
    lanes = folded.shape[1]
    lane = lax.broadcasted_iota(jnp.int32, folded.shape, 1)
    left = jnp.sum(jnp.where(lane < lanes // 2, folded, 0.0), axis=1, keepdims=True)
    right = jnp.sum(jnp.where(lane < lanes // 2, 0.0, folded), axis=1, keepdims=True)
    sums = jnp.concatenate([left, right], axis=0)
    inner = {}
    for number, (i, j) in enumerate(PAIRS):
        inner[i, j] = inner[j, i] = sums[number : number + 1, :]
    zero = jnp.zeros((1, 1), jnp.float32)
    one = jnp.ones((1, 1), jnp.float32)

    def mapped_of(coefficients):
        result = [2.0 * c for c in coefficients] + [zero] * (count - len(coefficients))
        for j, c in enumerate(coefficients):
            if j + 1 < count:
                result[j + 1] = result[j + 1] + (2.0 * c if j == 0 else c)
            if j > 0:
                result[j - 1] = result[j - 1] + c
        return result

    def product(first, second):
        total = spread = zero
        for i, a in enumerate(first):
            if a is zero:
                continue
            for j, b in enumerate(second):
                if b is zero:
                    continue
                term = a * b * inner[i, j]
                total = total + term
                spread = spread + jnp.abs(term)
        return total, spread / jnp.abs(total)

    walked = [zero] * ITERS
    rest = [one] + [zero] * ITERS
    heading = [one]
    norm = inner[0, 0]
    worst = zero
    for iteration in range(ITERS):
        mapped = mapped_of(heading)
        mapped = mapped[: iteration + 2]
        curved, spread = product(heading, mapped)
        worst = jnp.maximum(worst, spread)
        step = norm / curved
        for j, c in enumerate(heading):
            walked[j] = walked[j] + step * c
        for j, c in enumerate(mapped):
            rest[j] = rest[j] - step * c
        if iteration < ITERS - 1:
            active = rest[: iteration + 2]
            following, spread = product(active, active)
            worst = jnp.maximum(worst, spread)
            ratio = following / norm
            heading = [
                c + ratio * heading[j] if j < len(heading) else c for j, c in enumerate(active)
            ]
            norm = following
    scale = 4.0 / bound[0:1, 0:1]
    rows = [c * scale for c in walked] + rest
    rows = jnp.concatenate(rows + [zero] * (out.shape[0] - len(rows)), axis=0)
    out[...] = jnp.broadcast_to(rows, out.shape)
    trusted[0] = jnp.where(worst < TRUST, 1, 0)[0, 0]


def make_coefficients(products, bound):
    rank = bound.shape[1]
    return pl.pallas_call(
        coefficients_kernel,
        in_specs=[whole(products.shape), whole(bound.shape)],
        out_specs=[whole((16, rank)), SMEM],
        out_shape=[
            jax.ShapeDtypeStruct((16, rank), jnp.float32),
            jax.ShapeDtypeStruct((1,), jnp.int32),
        ],
        compiler_params=params(),
        name="make_coefficients",
    )(products, bound)


def combine_kernel(coefficients, basis, solution, residual):
    coarse = basis.shape[2]
    for phase in range(DEC):
        rows = pl.ds(phase, coarse, stride=DEC)
        total = basis[ITERS + 1, phase]
        for j in range(ITERS):
            total += coefficients[j : j + 1, :] * basis[j, phase]
        solution[rows, :] = total
        total = coefficients[ITERS : ITERS + 1, :] * basis[0, phase]
        for j in range(1, ITERS + 1):
            total += coefficients[ITERS + j : ITERS + j + 1, :] * basis[j, phase]
        residual[rows, :] = total


def combine(coefficients, basis):
    arrays = (coefficients, basis)
    out = jax.ShapeDtypeStruct((DEC * basis.shape[2], basis.shape[3]), jnp.float32)
    return pl.pallas_call(
        combine_kernel,
        in_specs=[whole(a.shape) for a in arrays],
        out_specs=[whole(out.shape)] * 2,
        out_shape=[out] * 2,
        compiler_params=params(),
        name="combine",
    )(*arrays)


def to_next(values, axis, count):
    return lax.ppermute(values, axis, [(i, (i + 1) % count) for i in range(count)])


def to_previous(values, axis, count):
    return lax.ppermute(values, axis, [((i + 1) % count, i) for i in range(count)])


def step_by_step(taps, multi, hyper, start, hyper_gram, multi_gram, devices):
    def widened(values, breadth):
        return jnp.concatenate(
            [
                to_next(values[-breadth:], BOTH, devices),
                values,
                to_previous(values[:breadth], BOTH, devices),
            ]
        )

    def down(values):
        rows = values.shape[0] // DEC
        parts = values.reshape(rows, DEC, -1)
        size = rows - 2 * REACH
        total = 0.0
        for offset in range(-W, W + 1):
            block, phase = divmod(offset, DEC)
            total = total + taps[offset + W] * lax.slice_in_dim(
                parts[:, phase], REACH + block, REACH + block + size, axis=0
            )
        return total

    def up(values):
        size = values.shape[0] - 2 * REACH
        phases = []
        for phase in range(DEC):
            total = 0.0
            for block in range(-REACH, REACH + 1):
                offset = DEC * block + phase
                if offset <= W:
                    total = total + taps[offset + W] * lax.slice_in_dim(
                        values, REACH - block, REACH - block + size, axis=0
                    )
            phases.append(total)
        return jnp.stack(phases, axis=1).reshape(DEC * size, -1)

    def operate(values):
        lowered = jnp.dot(down(widened(values, 2 * W)), hyper_gram, precision=FULL_PRECISION)
        return up(lowered) + jnp.dot(values, multi_gram, precision=FULL_PRECISION)

    def inner_sum(first, second):
        return lax.psum(jnp.sum(first * second), BOTH)

    solution = start
    residual = up(widened(hyper, REACH)) + multi - operate(solution)
    direction = residual
    norm = inner_sum(residual, residual)

    def iterate(_, state):
        solution, residual, direction, norm = state
        mapped = operate(direction)
        step = norm / inner_sum(direction, mapped)
        solution = solution + step * direction
        residual = residual - step * mapped
        following = inner_sum(residual, residual)
        return solution, residual, residual + following / norm * direction, following

    solution, residual, _, _ = lax.fori_loop(0, ITERS, iterate, (solution, residual, direction, norm))
    return solution, residual


def body(
    multispectral, hyperspectral, row_start, col_factor, band_factor, response, blur_taps, offsets
):
    across = lax.axis_size("col")
    along = lax.axis_size("row")
    devices = across * along
    place = lax.axis_index("col")
    row = lax.axis_index("row")[None]
    rank = band_factor.shape[1]
    share = rank // along
    fine = row_start.shape[0]

    def exchanged(values, distance):
        return lax.ppermute(values, "row", [(i, i ^ distance) for i in range(along)])

    own = col_factor.T
    pair = jnp.concatenate([own, exchanged(own, 1)])
    multispectral, band_factor, response, row_start = load(
        (multispectral, band_factor, response, row_start), (2, 1, 1, 1), "load_multi"
    )
    pair, hyperspectral = lax.optimization_barrier((pair, hyperspectral))
    pieces = [pair] + [exchanged(pair, distance) for distance in range(2, along, 2)]
    (hyperspectral,) = load((hyperspectral,), (8,), "load_hyper")
    before = to_next(jnp.concatenate([p[:, -EDGE:] for p in pieces]), "col", across)
    after = to_previous(jnp.concatenate([p[:, :EDGE] for p in pieces]), "col", across)
    spread = jnp.arange(-W, W + 1, dtype=jnp.int32)
    taps = jnp.sum(
        jnp.where(offsets[:, None] == spread[None, :], blur_taps[:, None], jnp.float32(0.0)), axis=0
    )
    multi_part, columns = contract_multi(row, band_factor, response, multispectral, pieces)

    def exchange(values, size, more):
        arrived = []
        for distance in range(1, across):
            piece = lax.dynamic_slice_in_dim(values, (place + distance) % across * size, size, 0)
            if more:
                piece = jnp.concatenate([piece] + more)
            arrived.append(
                lax.ppermute(piece, "col", [(i, (i + distance) % across) for i in range(across)])
            )
        return arrived

    multi_arrived = exchange(multi_part, fine, [])
    hyper_part, gram_part = contract_hyper(
        share, row, taps, columns, before, after, band_factor, hyperspectral
    )
    hyper_arrived = exchange(hyper_part, fine // DEC, [gram_part])
    multi = sum_arrived(place[None], multi_part, multi_arrived)
    hyper, gram, low, high = add_sums(
        place[None], hyper_part, gram_part, multi, row_start, hyper_arrived
    )
    before_rows = to_next(high, BOTH, devices)
    after_rows = to_previous(low, BOTH, devices)
    hyper_gram, multi_gram, hyper_w, multi_w, bound = make_operator(
        row, taps, band_factor, response, gram, exchanged(gram, 1)
    )
    basis, products = make_basis(
        devices, taps, multi, hyper, row_start, before_rows, after_rows, hyper_w, multi_w, bound
    )
    products = lax.all_to_all(products, BOTH, 0, 0, tiled=True)
    coefficients, trusted = make_coefficients(products, bound)

    def from_start():
        start = jnp.stack(list(basis[ITERS + 1]), axis=1).reshape(fine, rank)
        return step_by_step(taps, multi, hyper, start, hyper_gram, multi_gram, devices)

    return lax.cond(trusted[0] != 0, lambda: tuple(combine(coefficients, basis)), from_start)


def solution(mesh):
    in_specs = (
        P(None, "row", "col"),
        P(None, "row", "col"),
        P(("row", "col"), None),
        P("col", "row"),
        P(),
        P(),
        P(),
        P(),
    )
    out_specs = (P(("row", "col"), None), P(("row", "col"), None))
    return jax.shard_map(body, mesh=mesh, in_specs=in_specs, out_specs=out_specs, check_vma=False)
```

```python
import functools
import math

import jax
import jax.numpy as jnp
from jax import lax
from jax.experimental import pallas as pl
from jax.experimental.pallas import tpu as pltpu
from jax.sharding import PartitionSpec as P

DEC = 4
W = 8
REACH = W // DEC
ITERS = 4
RIDGE_TERM = 0.1
FULL_PRECISION = lax.Precision.HIGHEST
BOTH = ("row", "col")
ROWS_A = 512
RIM = 24
RIM_MULTI = 16
RIM_START = 20
PAIRS = [(i, j) for i in range(ITERS + 1) for j in range(i, ITERS + 1)]
TRUST = 2.0e4
EDGE = 16
EARLY = 36
LATER = 20
VMEM_LIMIT = 20 * 1024 * 1024


def params():
    return pltpu.CompilerParams(vmem_limit_bytes=VMEM_LIMIT)


def whole(shape):
    return pl.BlockSpec(shape, lambda *_: (0,) * len(shape))


SMEM = pl.BlockSpec(memory_space=pltpu.SMEM)
VMEM = pl.BlockSpec(memory_space=pltpu.VMEM)


def in_space(values, space):
    return pltpu.with_memory_space_constraint(values, space)


def two_halves(matrix):
    high = matrix.astype(jnp.bfloat16)
    low = (matrix - high.astype(jnp.float32)).astype(jnp.bfloat16)
    return high, low


def gram_of(values):
    return lax.dot_general(
        values, values, (((0,), (0,)), ((), ())), precision=FULL_PRECISION,
        preferred_element_type=jnp.float32,
    )


def load_kernel(ranges, *refs):
    count = len(ranges)
    copies = []
    for source, target, (rows, parts, _) in zip(refs[:count], refs[count : 2 * count], ranges):
        size = rows // parts
        for part in range(parts):
            piece = pl.ds(part * size, size)
            copies.append(
                pltpu.make_async_copy(
                    source.at[piece], target.at[piece], refs[2 * count].at[len(copies)]
                )
            )
    for copy in copies:
        copy.start()
    for copy in copies:
        copy.wait()


def load(arrays, ranges):
    shapes = [(room, *a.shape[1:]) for a, (_, _, room) in zip(arrays, ranges)]
    size = sum(a.dtype.itemsize * math.prod(shape) for a, shape in zip(arrays, shapes))
    return pl.pallas_call(
        functools.partial(load_kernel, ranges),
        in_specs=[pl.BlockSpec(memory_space=pl.ANY)] * len(arrays),
        out_specs=[VMEM] * len(arrays),
        out_shape=[pltpu.VMEM(shape, a.dtype) for a, shape in zip(arrays, shapes)],
        scratch_shapes=[pltpu.SemaphoreType.DMA((sum(parts for _, parts, _ in ranges),))],
        compiler_params=params(),
        cost_estimate=pl.CostEstimate(flops=0, bytes_accessed=2 * size, transcendentals=0),
        name="load",
    )(*[in_space(a, pltpu.HBM) for a in arrays])


def in_rank_order(place, share, pieces, target):
    pair = place[0] // 2
    core = place[0] % 2
    for distance, piece in enumerate(pieces):
        slot = 2 * (pair ^ distance)
        values = piece.astype(jnp.float32)
        first = pl.multiple_of((slot + core) * share, share)
        target[pl.ds(first, share), : values.shape[1]] = values[:share, :]
        second = pl.multiple_of((slot + 1 - core) * share, share)
        target[pl.ds(second, share), : values.shape[1]] = values[share:, :]


def multi_kernel(count, first, place, band, response, image, other, held, *refs):
    del held
    pieces = refs[:count]
    out, columns, bands, pairs, ranks, semaphore = refs[count:]
    rows = pl.ds(first, bands.shape[0] - first)
    copy = pltpu.make_async_copy(other.at[rows], bands.at[rows], semaphore)
    copy.start()
    depth = image.shape[2]
    rank = out.shape[1]
    in_rank_order(place, pieces[0].shape[0] // 2, [p[:, :depth] for p in pieces], ranks)
    for start in range(0, depth, rank):
        columns[start : start + rank, :] = ranks[:, start : start + rank].T
    merged = jnp.dot(
        response[...], band[...], precision=FULL_PRECISION, preferred_element_type=jnp.float32
    )
    field = columns[...]
    for k in range(2):
        pairs[k * depth : (k + 1) * depth, :] = (merged[k : k + 1, :] * field).astype(jnp.bfloat16)

    @pl.when(place[0] >= 0)
    def _():
        for start in range(0, out.shape[0], ROWS_A):
            rows = slice(start, start + ROWS_A)
            pixels = jnp.concatenate([image[0, rows, :], image[1, rows, :]], axis=1)
            total = jnp.dot(pixels, pairs[...], preferred_element_type=jnp.float32)
            out[rows, :] = total.astype(jnp.bfloat16)

    copy.wait()


def contract_multi(place, band, response, image, pieces, other, held, first):
    bands, rows, depth = image.shape
    rank = band.shape[1]
    outs = [
        jax.ShapeDtypeStruct((rows, rank), jnp.bfloat16),
        jax.ShapeDtypeStruct((depth, rank), jnp.float32),
        pltpu.VMEM(held.shape, held.dtype),
    ]
    return pl.pallas_call(
        functools.partial(multi_kernel, len(pieces), first),
        in_specs=[SMEM, whole(band.shape), whole(response.shape), VMEM]
        + [pl.BlockSpec(memory_space=pl.ANY), VMEM]
        + [whole(p.shape) for p in pieces],
        out_specs=[whole(o.shape) for o in outs[:2]] + [VMEM],
        input_output_aliases={5: 2},
        out_shape=outs,
        scratch_shapes=[
            pltpu.VMEM((bands * depth, rank), jnp.bfloat16),
            pltpu.VMEM((rank, depth), jnp.float32),
            pltpu.SemaphoreType.DMA,
        ],
        compiler_params=params(),
        cost_estimate=pl.CostEstimate(
            flops=2 * bands * rows * depth * rank, bytes_accessed=1 << 23, transcendentals=0
        ),
        name="contract_multi",
    )(
        place, band, response, in_space(image, pltpu.VMEM), in_space(other, pltpu.HBM),
        in_space(held, pltpu.VMEM), *pieces,
    )


def hyper_kernel(
    share, place, taps, columns, before, after, band, held, image, out, gram, wide, ranks, packed,
    rest, total, semaphore,
):
    depth, rank = columns.shape
    ready = held.shape[0]
    copy = pltpu.make_async_copy(image.at[pl.ds(ready, rest.shape[0])], rest, semaphore)
    copy.start()
    wide[EDGE : EDGE + depth, :] = columns[...]
    for edge, first in ((before, 0), (after, EDGE + depth)):
        values = edge[...].astype(jnp.float32)
        size = 2 * share
        in_rank_order(place, share, [values[i : i + size, :] for i in range(0, rank, size)], ranks)
        wide[first : first + EDGE, :] = ranks[...].T[:EDGE, :]
    coarse = jnp.zeros((depth // DEC, rank), jnp.float32)
    for offset in range(-W, W + 1):
        coarse += taps[offset + W] * wide[pl.ds(EDGE + offset, depth // DEC, stride=DEC), :]

    exact = columns[...].astype(jnp.bfloat16)
    fine_gram = lax.dot_general(
        exact, exact, (((0,), (0,)), ((), ())), preferred_element_type=jnp.float32
    )
    coarse_gram = gram_of(coarse)
    down = lax.broadcasted_iota(jnp.int32, (rank, rank), 0)
    along = lax.broadcasted_iota(jnp.int32, (rank, rank), 1)
    packed[:rank, :] = jnp.where(along >= down, fine_gram, coarse_gram)
    diagonal = jnp.sum(jnp.where(along == down, coarse_gram, 0.0), axis=0, keepdims=True)
    packed[rank:, :] = jnp.broadcast_to(diagonal, (packed.shape[0] - rank, rank))
    half = packed.shape[0] // 2
    part = packed[pl.ds(pl.multiple_of(place[0] % 2 * half, 8), half), :]
    high = part.astype(jnp.bfloat16).astype(jnp.float32)
    gram[...] = jnp.concatenate([high, part - high], axis=0).astype(jnp.bfloat16)

    def product(source, offset):
        pixels = [source[k] for k in range(source.shape[0])]
        pairs = [
            (band[offset + k : offset + k + 1, :] * coarse).astype(jnp.bfloat16)
            for k in range(len(pixels))
        ]
        return jnp.dot(
            jnp.concatenate(pixels, axis=1),
            jnp.concatenate(pairs, axis=0),
            preferred_element_type=jnp.float32,
        )

    @pl.when(place[0] >= 0)
    def _():
        total[...] = product(held, 0)

    copy.wait()
    out[...] = (total[...] + product(rest, ready)).astype(jnp.bfloat16)


def contract_hyper(share, place, taps, columns, before, after, band, held, image):
    bands, rows, depth = image.shape
    fine, rank = columns.shape
    rest = bands - held.shape[0]
    outs = [
        jax.ShapeDtypeStruct((rows, rank), jnp.bfloat16),
        jax.ShapeDtypeStruct((rank + 16, rank), jnp.bfloat16),
    ]
    return pl.pallas_call(
        functools.partial(hyper_kernel, share),
        in_specs=[SMEM, SMEM]
        + [whole(a.shape) for a in (columns, before, after, band)]
        + [VMEM, pl.BlockSpec(memory_space=pl.ANY)],
        out_specs=[whole(o.shape) for o in outs],
        out_shape=outs,
        scratch_shapes=[
            pltpu.VMEM((fine + 2 * EDGE, rank), jnp.float32),
            pltpu.VMEM((rank, rank), jnp.float32),
            pltpu.VMEM((rank + 16, rank), jnp.float32),
            pltpu.VMEM((rest, rows, depth), image.dtype),
            pltpu.VMEM((rows, rank), jnp.float32),
            pltpu.SemaphoreType.DMA,
        ],
        compiler_params=params(),
        name="contract_hyper",
    )(
        place, taps, columns, before, after, band, in_space(held, pltpu.VMEM),
        in_space(image, pltpu.HBM),
    )


def operator_kernel(
    place, taps, band_gram, merged_gram, own, other, hyper_out, multi_out, hyper_w, multi_w, bound
):
    rank = band_gram.shape[1]
    even = place[0] % 2 == 0
    lower = jnp.where(even, own[...], other[...])
    upper = jnp.where(even, other[...], own[...])
    packed = jnp.concatenate([lower, upper], axis=0)
    diagonal = packed[rank : rank + 1, :]
    packed = packed[:rank, :]
    turned = packed.T
    down = lax.broadcasted_iota(jnp.int32, (rank, rank), 0)
    along = lax.broadcasted_iota(jnp.int32, (rank, rank), 1)
    column_gram = jnp.where(along >= down, packed, turned)
    coarse_gram = jnp.where(along < down, packed, jnp.where(along == down, diagonal, turned))
    hyper = coarse_gram * band_gram[...]
    multi = column_gram * merged_gram[...] + jnp.where(along == down, RIDGE_TERM, 0.0)
    hyper_out[...] = hyper
    multi_out[...] = multi
    squared = jnp.float32(0.0)
    for phase in range(DEC):
        in_phase = jnp.float32(0.0)
        for offset in range(-W, W + 1):
            if offset % DEC == phase:
                in_phase = in_phase + taps[offset + W]
        squared = squared + in_phase * in_phase
    largest = squared * hyper + multi

    def total_of(values):
        return jnp.sum(jnp.sum(values, axis=1, keepdims=True), axis=0, keepdims=True)

    def trace(values):
        return total_of(jnp.where(along == down, values, 0.0))

    power = largest / trace(largest)
    for _ in range(4):
        power = jnp.dot(power, power, preferred_element_type=jnp.float32)
    top = 1.1 * total_of(power * largest) / trace(power)
    bound[...] = jnp.broadcast_to(top, bound.shape)
    for matrix, weights in ((hyper, hyper_w), (multi, multi_w)):
        high, low = two_halves(matrix * (4.0 / top))
        weights[:rank, :rank] = high
        weights[:rank, rank:] = low
        weights[rank:, :rank] = high
        weights[rank:, rank:] = jnp.zeros_like(high)


def make_operator(place, taps, band_gram, merged_gram, own, other):
    rank = band_gram.shape[1]
    square = jax.ShapeDtypeStruct((rank, rank), jnp.float32)
    weights = jax.ShapeDtypeStruct((2 * rank, 2 * rank), jnp.bfloat16)
    bound = jax.ShapeDtypeStruct((8, rank), jnp.float32)
    outs = [square, square, weights, weights, bound]
    arrays = (band_gram, merged_gram, own, other)
    return pl.pallas_call(
        operator_kernel,
        in_specs=[SMEM, SMEM] + [whole(a.shape) for a in arrays],
        out_specs=[whole(o.shape) for o in outs],
        out_shape=outs,
        compiler_params=params(),
        cost_estimate=pl.CostEstimate(flops=0, bytes_accessed=1 << 26, transcendentals=0),
        name="make_operator",
    )(place, taps, *arrays)


def times(values, weights):
    rank = values.shape[1]
    both = jnp.dot(
        jnp.concatenate(two_halves(values), axis=1), weights, preferred_element_type=jnp.float32
    )
    return both[:, :rank] + both[:, rank:]


def shifted(values, by):
    size = values.shape[0]
    return values if by == 0 else pltpu.roll(values, by % size, 0)


def blur_down(taps, field):
    total = None
    for block in range(-REACH, REACH + 1):
        term = None
        for phase in range(DEC):
            offset = DEC * block + phase
            if offset <= W:
                more = taps[offset + W] * field(phase)
                term = more if term is None else term + more
        term = shifted(term, -block)
        total = term if total is None else total + term
    return total


def blur_up(taps, values, phase):
    total = None
    for block in range(-REACH, REACH + 1):
        offset = DEC * block + phase
        if offset <= W:
            term = taps[offset + W] * shifted(values, block)
            total = term if total is None else total + term
    return total


def sum_kernel(place, band, response, own, *refs):
    del place
    out, band_gram, merged_gram = refs[-3:]
    total = own[...].astype(jnp.float32)
    for values in refs[:-3]:
        total += values[...].astype(jnp.float32)
    out[...] = total
    merged = jnp.dot(
        response[...], band[...], precision=FULL_PRECISION, preferred_element_type=jnp.float32
    )
    band_gram[...] = gram_of(band[...])
    merged_gram[...] = gram_of(merged)


def sum_arrived(place, band, response, own, arrived):
    shape = arrived[0].shape
    rank = band.shape[1]
    square = jax.ShapeDtypeStruct((rank, rank), jnp.float32)
    outs = [jax.ShapeDtypeStruct(shape, jnp.float32), square, square]
    return pl.pallas_call(
        sum_kernel,
        grid_spec=pltpu.PrefetchScalarGridSpec(
            num_scalar_prefetch=1,
            grid=(1,),
            in_specs=[whole(band.shape), whole(response.shape)]
            + [pl.BlockSpec(shape, lambda i, place: (place[0], 0))]
            + [whole(shape) for _ in arrived],
            out_specs=[whole(o.shape) for o in outs],
        ),
        out_shape=outs,
        compiler_params=params(),
        name="sum_arrived",
    )(place, band, response, own, *arrived)


def sums_kernel(count, place, *refs):
    del place
    own, own_gram, multi, start = refs[:4]
    arrived = refs[4 : 4 + count]
    hyper, gram, low, high = refs[4 + count :]
    rows = hyper.shape[0]
    total = own[...].astype(jnp.float32)
    grams = own_gram[...].astype(jnp.float32)
    for values in arrived:
        total += values[:rows, :].astype(jnp.float32)
        grams += values[rows:, :].astype(jnp.float32)
    hyper[...] = total
    half = gram.shape[0]
    gram[...] = grams[:half, :] + grams[half:, :]
    first, second = DEC * RIM_MULTI, DEC * RIM_MULTI + RIM
    for pack, top in ((low, True), (high, False)):
        for source, begin, size in (
            (multi, 0, first),
            (hyper, first, RIM),
            (start, second, DEC * RIM_START),
        ):
            rows = source.shape[0]
            at = 0 if top else rows - size
            pack[begin : begin + size, :] = source[at : at + size, :]


def add_sums(place, hyper_part, gram_part, multi, start, arrived):
    fine, rank = start.shape
    coarse = fine // DEC
    pack = jax.ShapeDtypeStruct((DEC * (RIM_MULTI + RIM_START) + RIM, rank), jnp.float32)
    outs = [
        jax.ShapeDtypeStruct((coarse, rank), jnp.float32),
        jax.ShapeDtypeStruct((gram_part.shape[0] // 2, rank), jnp.float32),
        pack,
        pack,
    ]
    return pl.pallas_call(
        functools.partial(sums_kernel, len(arrived)),
        grid_spec=pltpu.PrefetchScalarGridSpec(
            num_scalar_prefetch=1,
            grid=(1,),
            in_specs=[pl.BlockSpec((coarse, rank), lambda i, place: (place[0], 0))]
            + [whole(a.shape) for a in (gram_part, multi, start, *arrived)],
            out_specs=[whole(o.shape) for o in outs],
        ),
        out_shape=outs,
        compiler_params=params(),
        name="add_sums",
    )(place, hyper_part, gram_part, multi, start, *arrived)


def on_diagonal(rows, lanes):
    down = lax.broadcasted_iota(jnp.int32, (rows, lanes), 0)
    along = lax.broadcasted_iota(jnp.int32, (rows, lanes), 1)
    return down == along


def basis_kernel(
    devices, taps, multi, hyper, start, before, after, hyper_w, multi_w, bound, basis, products,
    natural, lifted, held,
):
    fine = multi.shape[0]
    coarse = fine // DEC
    wide = coarse + 2 * RIM
    first, second = DEC * RIM_MULTI, DEC * RIM_MULTI + RIM
    own = slice(RIM, RIM + coarse)

    def apply(field):
        lowered = times(blur_down(taps, field), hyper_w[...])
        return [blur_up(taps, lowered, phase) + times(field(phase), multi_w[...]) for phase in range(DEC)]

    margin = DEC * (RIM - RIM_START)
    none = jnp.zeros((margin, multi.shape[1]), jnp.float32)
    natural[:margin, :] = none
    natural[margin : DEC * RIM, :] = before[second:, :]
    natural[DEC * RIM : DEC * RIM + fine, :] = start[...]
    natural[DEC * RIM + fine : 2 * DEC * RIM + fine - margin, :] = after[second:, :]
    natural[2 * DEC * RIM + fine - margin :, :] = none
    for phase in range(DEC):
        held[1, phase] = natural[pl.ds(phase, wide, stride=DEC), :]
        basis[ITERS + 1, phase] = held[1, phase, own, :]
    mapped = apply(lambda phase: held[1, phase])

    lifted[:RIM, :] = before[first:second, :]
    lifted[own, :] = hyper[...]
    lifted[RIM + coarse :, :] = after[first:second, :]
    margin = DEC * (RIM - RIM_MULTI)
    none = jnp.zeros((margin, multi.shape[1]), jnp.float32)
    natural[:margin, :] = none
    natural[margin : DEC * RIM, :] = before[:first, :]
    natural[DEC * RIM : DEC * RIM + fine, :] = multi[...]
    natural[DEC * RIM + fine : 2 * DEC * RIM + fine - margin, :] = after[:first, :]
    natural[2 * DEC * RIM + fine - margin :, :] = none
    quarter = bound[0:1, :] * 0.25
    sums = lifted[...]
    for phase in range(DEC):
        right = natural[pl.ds(phase, wide, stride=DEC), :] + blur_up(taps, sums, phase)
        held[0, phase] = right - quarter * mapped[phase]

    for step in range(ITERS):
        now = step % 2
        mapped = apply(lambda phase: held[now, phase])
        for phase in range(DEC):
            basis[step, phase] = held[now, phase, own, :]
            if step == 0:
                result = 0.5 * mapped[phase] - held[now, phase]
            else:
                result = mapped[phase] - 2.0 * held[now, phase] - held[1 - now, phase]
            if step < ITERS - 1:
                held[1 - now, phase] = result
            else:
                basis[ITERS, phase] = result[own, :]
    rows = []
    for i, j in PAIRS:
        total = jnp.zeros((coarse, multi.shape[1]), jnp.float32)
        for phase in range(DEC):
            total += basis[i, phase] * basis[j, phase]
        rows.append(jnp.sum(total, axis=0, keepdims=True))
    rows.append(jnp.zeros_like(rows[0]))
    block = jnp.sum(jnp.concatenate(rows, axis=0), axis=1, keepdims=True)
    block = jnp.where(on_diagonal(block.shape[0], multi.shape[1]), block, 0.0)
    block = jnp.sum(block, axis=0, keepdims=True)
    for device in range(devices):
        products[device] = block


def make_basis(devices, taps, multi, hyper, start, before, after, hyper_w, multi_w, bound):
    fine, rank = multi.shape
    coarse = fine // DEC
    wide = coarse + 2 * RIM
    arrays = (multi, hyper, start, before, after, hyper_w, multi_w, bound)
    outs = [
        jax.ShapeDtypeStruct((ITERS + 2, DEC, coarse, rank), jnp.float32),
        jax.ShapeDtypeStruct((devices, 1, rank), jnp.float32),
    ]
    return pl.pallas_call(
        functools.partial(basis_kernel, devices),
        in_specs=[SMEM] + [whole(a.shape) for a in arrays],
        out_specs=[whole(o.shape) for o in outs],
        out_shape=outs,
        scratch_shapes=[
            pltpu.VMEM((DEC * wide, rank), jnp.float32),
            pltpu.VMEM((wide, rank), jnp.float32),
            pltpu.VMEM((2, DEC, wide, rank), jnp.float32),
        ],
        compiler_params=params(),
        name="make_basis",
    )(taps, *arrays)


def coefficients_kernel(products, bound, out, trusted):
    count = ITERS + 1
    row = jnp.sum(products[...], axis=0)
    sums = jnp.broadcast_to(row, (16, row.shape[1]))
    sums = jnp.sum(jnp.where(on_diagonal(*sums.shape), sums, 0.0), axis=1, keepdims=True)
    inner = {}
    for number, (i, j) in enumerate(PAIRS):
        inner[i, j] = inner[j, i] = sums[number : number + 1, :]
    zero = jnp.zeros((1, 1), jnp.float32)
    one = jnp.ones((1, 1), jnp.float32)

    def mapped_of(coefficients):
        result = [2.0 * c for c in coefficients] + [zero] * (count - len(coefficients))
        for j, c in enumerate(coefficients):
            if j + 1 < count:
                result[j + 1] = result[j + 1] + (2.0 * c if j == 0 else c)
            if j > 0:
                result[j - 1] = result[j - 1] + c
        return result

    def product(first, second):
        total = spread = zero
        for i, a in enumerate(first):
            if a is zero:
                continue
            for j, b in enumerate(second):
                if b is zero:
                    continue
                term = a * b * inner[i, j]
                total = total + term
                spread = spread + jnp.abs(term)
        return total, spread / jnp.abs(total)

    walked = [zero] * ITERS
    rest = [one] + [zero] * ITERS
    heading = [one]
    norm = inner[0, 0]
    worst = zero
    for iteration in range(ITERS):
        mapped = mapped_of(heading)
        mapped = mapped[: iteration + 2]
        curved, spread = product(heading, mapped)
        worst = jnp.maximum(worst, spread)
        step = norm / curved
        for j, c in enumerate(heading):
            walked[j] = walked[j] + step * c
        for j, c in enumerate(mapped):
            rest[j] = rest[j] - step * c
        if iteration < ITERS - 1:
            active = rest[: iteration + 2]
            following, spread = product(active, active)
            worst = jnp.maximum(worst, spread)
            ratio = following / norm
            heading = [
                c + ratio * heading[j] if j < len(heading) else c for j, c in enumerate(active)
            ]
            norm = following
    scale = 4.0 / bound[0:1, 0:1]
    rows = [c * scale for c in walked] + rest
    rows = jnp.concatenate(rows + [zero] * (out.shape[0] - len(rows)), axis=0)
    out[...] = jnp.broadcast_to(rows, out.shape)
    trusted[0] = jnp.where(worst < TRUST, 1, 0)[0, 0]


def make_coefficients(products, bound):
    rank = bound.shape[1]
    return pl.pallas_call(
        coefficients_kernel,
        in_specs=[whole(products.shape), whole(bound.shape)],
        out_specs=[whole((16, rank)), SMEM],
        out_shape=[
            jax.ShapeDtypeStruct((16, rank), jnp.float32),
            jax.ShapeDtypeStruct((1,), jnp.int32),
        ],
        compiler_params=params(),
        name="make_coefficients",
    )(products, bound)


def combine_kernel(coefficients, basis, solution, residual):
    coarse = basis.shape[2]
    for phase in range(DEC):
        rows = pl.ds(phase, coarse, stride=DEC)
        total = basis[ITERS + 1, phase]
        for j in range(ITERS):
            total += coefficients[j : j + 1, :] * basis[j, phase]
        solution[rows, :] = total
        total = coefficients[ITERS : ITERS + 1, :] * basis[0, phase]
        for j in range(1, ITERS + 1):
            total += coefficients[ITERS + j : ITERS + j + 1, :] * basis[j, phase]
        residual[rows, :] = total


def combine(coefficients, basis):
    arrays = (coefficients, basis)
    out = jax.ShapeDtypeStruct((DEC * basis.shape[2], basis.shape[3]), jnp.float32)
    return pl.pallas_call(
        combine_kernel,
        in_specs=[whole(a.shape) for a in arrays],
        out_specs=[whole(out.shape)] * 2,
        out_shape=[out] * 2,
        compiler_params=params(),
        name="combine",
    )(*arrays)


def to_next(values, axis, count):
    return lax.ppermute(values, axis, [(i, (i + 1) % count) for i in range(count)])


def to_previous(values, axis, count):
    return lax.ppermute(values, axis, [((i + 1) % count, i) for i in range(count)])


def step_by_step(taps, multi, hyper, start, hyper_gram, multi_gram, devices):
    def widened(values, breadth):
        return jnp.concatenate(
            [
                to_next(values[-breadth:], BOTH, devices),
                values,
                to_previous(values[:breadth], BOTH, devices),
            ]
        )

    def down(values):
        rows = values.shape[0] // DEC
        parts = values.reshape(rows, DEC, -1)
        size = rows - 2 * REACH
        total = 0.0
        for offset in range(-W, W + 1):
            block, phase = divmod(offset, DEC)
            total = total + taps[offset + W] * lax.slice_in_dim(
                parts[:, phase], REACH + block, REACH + block + size, axis=0
            )
        return total

    def up(values):
        size = values.shape[0] - 2 * REACH
        phases = []
        for phase in range(DEC):
            total = 0.0
            for block in range(-REACH, REACH + 1):
                offset = DEC * block + phase
                if offset <= W:
                    total = total + taps[offset + W] * lax.slice_in_dim(
                        values, REACH - block, REACH - block + size, axis=0
                    )
            phases.append(total)
        return jnp.stack(phases, axis=1).reshape(DEC * size, -1)

    def operate(values):
        lowered = jnp.dot(down(widened(values, 2 * W)), hyper_gram, precision=FULL_PRECISION)
        return up(lowered) + jnp.dot(values, multi_gram, precision=FULL_PRECISION)

    def inner_sum(first, second):
        return lax.psum(jnp.sum(first * second), BOTH)

    solution = start
    residual = up(widened(hyper, REACH)) + multi - operate(solution)
    direction = residual
    norm = inner_sum(residual, residual)

    def iterate(_, state):
        solution, residual, direction, norm = state
        mapped = operate(direction)
        step = norm / inner_sum(direction, mapped)
        solution = solution + step * direction
        residual = residual - step * mapped
        following = inner_sum(residual, residual)
        return solution, residual, residual + following / norm * direction, following

    solution, residual, _, _ = lax.fori_loop(0, ITERS, iterate, (solution, residual, direction, norm))
    return solution, residual


def body(
    multispectral, hyperspectral, row_start, col_factor, band_factor, response, blur_taps, offsets
):
    across = lax.axis_size("col")
    along = lax.axis_size("row")
    devices = across * along
    place = lax.axis_index("col")
    row = lax.axis_index("row")[None]
    rank = band_factor.shape[1]
    share = rank // along
    fine = row_start.shape[0]

    def exchanged(values, distance):
        return lax.ppermute(values, "row", [(i, i ^ distance) for i in range(along)])

    own = col_factor.T
    partner = exchanged(own, 1)
    half = lax.optimization_barrier(jnp.concatenate([own, jnp.zeros_like(own)]))
    pair = jnp.concatenate([half[:share], partner])
    pair, image = lax.optimization_barrier((pair, multispectral))
    pieces = [pair] + [exchanged(pair, distance) for distance in range(2, along, 2)]
    image, band_factor, response, row_start, held = load(
        (image, band_factor, response, row_start, hyperspectral),
        (
            (2, 2, 2),
            (band_factor.shape[0], 1, band_factor.shape[0]),
            (2, 1, 2),
            (fine, 1, fine),
            (EARLY, 4, EARLY + LATER),
        ),
    )
    before = to_next(jnp.concatenate([p[:, -EDGE:] for p in pieces]), "col", across)
    after = to_previous(jnp.concatenate([p[:, :EDGE] for p in pieces]), "col", across)
    multi_part, columns, held = contract_multi(
        row, band_factor, response, image, pieces, hyperspectral, held, EARLY
    )
    spread = jnp.arange(-W, W + 1, dtype=jnp.int32)
    taps = jnp.sum(
        jnp.where(offsets[:, None] == spread[None, :], blur_taps[:, None], jnp.float32(0.0)), axis=0
    )

    def exchange(values, size, more):
        arrived = []
        for distance in range(1, across):
            piece = lax.dynamic_slice_in_dim(values, (place + distance) % across * size, size, 0)
            if more:
                piece = jnp.concatenate([piece] + more)
            arrived.append(
                lax.ppermute(piece, "col", [(i, (i + distance) % across) for i in range(across)])
            )
        return arrived

    multi_arrived = exchange(multi_part, fine, [])
    hyper_part, gram_part = contract_hyper(
        share, row, taps, columns, before, after, band_factor, held, hyperspectral
    )
    hyper_arrived = exchange(hyper_part, fine // DEC, [gram_part])
    multi, band_gram, merged_gram = sum_arrived(
        place[None], band_factor, response, multi_part, multi_arrived
    )
    hyper, gram, low, high = add_sums(
        place[None], hyper_part, gram_part, multi, row_start, hyper_arrived
    )
    hyper_gram, multi_gram, hyper_w, multi_w, bound = make_operator(
        row, taps, band_gram, merged_gram, gram, exchanged(gram, 1)
    )
    before_rows = to_next(high, BOTH, devices)
    after_rows = to_previous(low, BOTH, devices)
    basis, products = make_basis(
        devices, taps, multi, hyper, row_start, before_rows, after_rows, hyper_w, multi_w, bound
    )
    products = lax.all_to_all(products, BOTH, 0, 0, tiled=True)
    coefficients, trusted = make_coefficients(products, bound)

    def from_start():
        start = jnp.stack(list(basis[ITERS + 1]), axis=1).reshape(fine, rank)
        return step_by_step(taps, multi, hyper, start, hyper_gram, multi_gram, devices)

    return lax.cond(trusted[0] != 0, lambda: tuple(combine(coefficients, basis)), from_start)


def solution(mesh):
    in_specs = (
        P(None, "row", "col"),
        P(None, "row", "col"),
        P(("row", "col"), None),
        P("col", "row"),
        P(),
        P(),
        P(),
        P(),
    )
    out_specs = (P(("row", "col"), None), P(("row", "col"), None))
    return jax.shard_map(body, mesh=mesh, in_specs=in_specs, out_specs=out_specs, check_vma=False)
```

```python
import functools
import math

import jax
import jax.numpy as jnp
from jax import lax
from jax.experimental import pallas as pl
from jax.experimental.pallas import tpu as pltpu
from jax.sharding import PartitionSpec as P

DEC = 4
W = 8
REACH = W // DEC
ITERS = 4
RIDGE_TERM = 0.1
FULL_PRECISION = lax.Precision.HIGHEST
BOTH = ("row", "col")
ROWS_A = 512
RIM = 24
RIM_MULTI = 16
RIM_START = 20
PAIRS = [(i, j) for i in range(ITERS + 1) for j in range(i, ITERS + 1)]
TRUST = 2.0e4
EDGE = 16
EARLY = 36
LATER = 20
VMEM_LIMIT = 20 * 1024 * 1024


def params():
    return pltpu.CompilerParams(vmem_limit_bytes=VMEM_LIMIT)


def whole(shape):
    return pl.BlockSpec(shape, lambda *_: (0,) * len(shape))


SMEM = pl.BlockSpec(memory_space=pltpu.SMEM)
VMEM = pl.BlockSpec(memory_space=pltpu.VMEM)


def in_space(values, space):
    return pltpu.with_memory_space_constraint(values, space)


def two_halves(matrix):
    high = matrix.astype(jnp.bfloat16)
    low = (matrix - high.astype(jnp.float32)).astype(jnp.bfloat16)
    return high, low


def gram_of(values):
    return lax.dot_general(
        values, values, (((0,), (0,)), ((), ())), precision=FULL_PRECISION,
        preferred_element_type=jnp.float32,
    )


def load_kernel(ranges, *refs):
    count = len(ranges)
    copies = []
    for source, target, (rows, parts, _) in zip(refs[:count], refs[count : 2 * count], ranges):
        size = rows // parts
        for part in range(parts):
            piece = pl.ds(part * size, size)
            copies.append(
                pltpu.make_async_copy(
                    source.at[piece], target.at[piece], refs[2 * count].at[len(copies)]
                )
            )
    for copy in copies:
        copy.start()
    for copy in copies:
        copy.wait()


def load(arrays, ranges):
    shapes = [(room, *a.shape[1:]) for a, (_, _, room) in zip(arrays, ranges)]
    size = sum(a.dtype.itemsize * math.prod(shape) for a, shape in zip(arrays, shapes))
    return pl.pallas_call(
        functools.partial(load_kernel, ranges),
        in_specs=[pl.BlockSpec(memory_space=pl.ANY)] * len(arrays),
        out_specs=[VMEM] * len(arrays),
        out_shape=[pltpu.VMEM(shape, a.dtype) for a, shape in zip(arrays, shapes)],
        scratch_shapes=[pltpu.SemaphoreType.DMA((sum(parts for _, parts, _ in ranges),))],
        compiler_params=params(),
        cost_estimate=pl.CostEstimate(flops=0, bytes_accessed=2 * size, transcendentals=0),
        name="load",
    )(*[in_space(a, pltpu.HBM) for a in arrays])


def in_rank_order(place, share, pieces, target):
    pair = place[0] // 2
    core = place[0] % 2
    for distance, piece in enumerate(pieces):
        slot = 2 * (pair ^ distance)
        values = piece.astype(jnp.float32)
        first = pl.multiple_of((slot + core) * share, share)
        target[pl.ds(first, share), : values.shape[1]] = values[:share, :]
        second = pl.multiple_of((slot + 1 - core) * share, share)
        target[pl.ds(second, share), : values.shape[1]] = values[share:, :]


def multi_kernel(count, first, place, band, response, image, other, held, *refs):
    del held
    pieces = refs[:count]
    out, columns, bands, pairs, ranks, semaphore = refs[count:]
    rows = pl.ds(first, bands.shape[0] - first)
    copy = pltpu.make_async_copy(other.at[rows], bands.at[rows], semaphore)
    copy.start()
    depth = image.shape[2]
    rank = out.shape[1]
    in_rank_order(place, pieces[0].shape[0] // 2, [p[:, :depth] for p in pieces], ranks)
    for start in range(0, depth, rank):
        columns[start : start + rank, :] = ranks[:, start : start + rank].T
    merged = jnp.dot(
        response[...], band[...], precision=FULL_PRECISION, preferred_element_type=jnp.float32
    )
    field = columns[...]
    for k in range(2):
        pairs[k * depth : (k + 1) * depth, :] = (merged[k : k + 1, :] * field).astype(jnp.bfloat16)

    @pl.when(place[0] >= 0)
    def _():
        for start in range(0, out.shape[0], ROWS_A):
            rows = slice(start, start + ROWS_A)
            pixels = jnp.concatenate([image[0, rows, :], image[1, rows, :]], axis=1)
            total = jnp.dot(pixels, pairs[...], preferred_element_type=jnp.float32)
            out[rows, :] = total.astype(jnp.bfloat16)

    copy.wait()


def contract_multi(place, band, response, image, pieces, other, held, first):
    bands, rows, depth = image.shape
    rank = band.shape[1]
    outs = [
        jax.ShapeDtypeStruct((rows, rank), jnp.bfloat16),
        jax.ShapeDtypeStruct((depth, rank), jnp.float32),
        pltpu.VMEM(held.shape, held.dtype),
    ]
    return pl.pallas_call(
        functools.partial(multi_kernel, len(pieces), first),
        in_specs=[SMEM, whole(band.shape), whole(response.shape), VMEM]
        + [pl.BlockSpec(memory_space=pl.ANY), VMEM]
        + [whole(p.shape) for p in pieces],
        out_specs=[whole(o.shape) for o in outs[:2]] + [VMEM],
        input_output_aliases={5: 2},
        out_shape=outs,
        scratch_shapes=[
            pltpu.VMEM((bands * depth, rank), jnp.bfloat16),
            pltpu.VMEM((rank, depth), jnp.float32),
            pltpu.SemaphoreType.DMA,
        ],
        compiler_params=params(),
        cost_estimate=pl.CostEstimate(
            flops=2 * bands * rows * depth * rank, bytes_accessed=1 << 23, transcendentals=0
        ),
        name="contract_multi",
    )(
        place, band, response, in_space(image, pltpu.VMEM), in_space(other, pltpu.HBM),
        in_space(held, pltpu.VMEM), *pieces,
    )


def hyper_kernel(
    share, place, taps, columns, before, after, band, held, image, out, gram, wide, ranks, packed,
    rest, total, semaphore,
):
    depth, rank = columns.shape
    ready = held.shape[0]
    copy = pltpu.make_async_copy(image.at[pl.ds(ready, rest.shape[0])], rest, semaphore)
    copy.start()
    wide[EDGE : EDGE + depth, :] = columns[...]
    for edge, first in ((before, 0), (after, EDGE + depth)):
        values = edge[...].astype(jnp.float32)
        size = 2 * share
        in_rank_order(place, share, [values[i : i + size, :] for i in range(0, rank, size)], ranks)
        wide[first : first + EDGE, :] = ranks[...].T[:EDGE, :]
    coarse = jnp.zeros((depth // DEC, rank), jnp.float32)
    for offset in range(-W, W + 1):
        coarse += taps[offset + W] * wide[pl.ds(EDGE + offset, depth // DEC, stride=DEC), :]

    exact = columns[...].astype(jnp.bfloat16)
    fine_gram = lax.dot_general(
        exact, exact, (((0,), (0,)), ((), ())), preferred_element_type=jnp.float32
    )
    coarse_gram = gram_of(coarse)
    down = lax.broadcasted_iota(jnp.int32, (rank, rank), 0)
    along = lax.broadcasted_iota(jnp.int32, (rank, rank), 1)
    packed[:rank, :] = jnp.where(along >= down, fine_gram, coarse_gram)
    diagonal = jnp.sum(jnp.where(along == down, coarse_gram, 0.0), axis=0, keepdims=True)
    packed[rank:, :] = jnp.broadcast_to(diagonal, (packed.shape[0] - rank, rank))
    half = packed.shape[0] // 2
    part = packed[pl.ds(pl.multiple_of(place[0] % 2 * half, 8), half), :]
    high = part.astype(jnp.bfloat16).astype(jnp.float32)
    gram[...] = jnp.concatenate([high, part - high], axis=0).astype(jnp.bfloat16)

    def product(source, offset):
        pixels = [source[k] for k in range(source.shape[0])]
        pairs = [
            (band[offset + k : offset + k + 1, :] * coarse).astype(jnp.bfloat16)
            for k in range(len(pixels))
        ]
        return jnp.dot(
            jnp.concatenate(pixels, axis=1),
            jnp.concatenate(pairs, axis=0),
            preferred_element_type=jnp.float32,
        )

    @pl.when(place[0] >= 0)
    def _():
        total[...] = product(held, 0)

    copy.wait()
    out[...] = (total[...] + product(rest, ready)).astype(jnp.bfloat16)


def contract_hyper(share, place, taps, columns, before, after, band, held, image):
    bands, rows, depth = image.shape
    fine, rank = columns.shape
    rest = bands - held.shape[0]
    outs = [
        jax.ShapeDtypeStruct((rows, rank), jnp.bfloat16),
        jax.ShapeDtypeStruct((rank + 16, rank), jnp.bfloat16),
    ]
    return pl.pallas_call(
        functools.partial(hyper_kernel, share),
        in_specs=[SMEM, SMEM]
        + [whole(a.shape) for a in (columns, before, after, band)]
        + [VMEM, pl.BlockSpec(memory_space=pl.ANY)],
        out_specs=[whole(o.shape) for o in outs],
        out_shape=outs,
        scratch_shapes=[
            pltpu.VMEM((fine + 2 * EDGE, rank), jnp.float32),
            pltpu.VMEM((rank, rank), jnp.float32),
            pltpu.VMEM((rank + 16, rank), jnp.float32),
            pltpu.VMEM((rest, rows, depth), image.dtype),
            pltpu.VMEM((rows, rank), jnp.float32),
            pltpu.SemaphoreType.DMA,
        ],
        compiler_params=params(),
        name="contract_hyper",
    )(
        place, taps, columns, before, after, band, in_space(held, pltpu.VMEM),
        in_space(image, pltpu.HBM),
    )


def operator_kernel(
    place, taps, band_gram, merged_gram, own, other, hyper_out, multi_out, hyper_w, multi_w, bound
):
    rank = band_gram.shape[1]
    even = place[0] % 2 == 0
    lower = jnp.where(even, own[...], other[...])
    upper = jnp.where(even, other[...], own[...])
    packed = jnp.concatenate([lower, upper], axis=0)
    diagonal = packed[rank : rank + 1, :]
    packed = packed[:rank, :]
    turned = packed.T
    down = lax.broadcasted_iota(jnp.int32, (rank, rank), 0)
    along = lax.broadcasted_iota(jnp.int32, (rank, rank), 1)
    column_gram = jnp.where(along >= down, packed, turned)
    coarse_gram = jnp.where(along < down, packed, jnp.where(along == down, diagonal, turned))
    hyper = coarse_gram * band_gram[...]
    multi = column_gram * merged_gram[...] + jnp.where(along == down, RIDGE_TERM, 0.0)
    hyper_out[...] = hyper
    multi_out[...] = multi
    squared = jnp.float32(0.0)
    for phase in range(DEC):
        in_phase = jnp.float32(0.0)
        for offset in range(-W, W + 1):
            if offset % DEC == phase:
                in_phase = in_phase + taps[offset + W]
        squared = squared + in_phase * in_phase
    largest = squared * hyper + multi

    def total_of(values):
        return jnp.sum(jnp.sum(values, axis=1, keepdims=True), axis=0, keepdims=True)

    def trace(values):
        return total_of(jnp.where(along == down, values, 0.0))

    power = largest / trace(largest)
    for _ in range(4):
        power = jnp.dot(power, power, preferred_element_type=jnp.float32)
    top = 1.1 * total_of(power * largest) / trace(power)
    bound[...] = jnp.broadcast_to(top, bound.shape)
    for matrix, weights in ((hyper, hyper_w), (multi, multi_w)):
        high, low = two_halves(matrix * (4.0 / top))
        weights[:rank, :rank] = high
        weights[:rank, rank:] = low
        weights[rank:, :rank] = high
        weights[rank:, rank:] = jnp.zeros_like(high)


def make_operator(place, taps, band_gram, merged_gram, own, other):
    rank = band_gram.shape[1]
    square = jax.ShapeDtypeStruct((rank, rank), jnp.float32)
    weights = jax.ShapeDtypeStruct((2 * rank, 2 * rank), jnp.bfloat16)
    bound = jax.ShapeDtypeStruct((8, rank), jnp.float32)
    outs = [square, square, weights, weights, bound]
    arrays = (band_gram, merged_gram, own, other)
    return pl.pallas_call(
        operator_kernel,
        in_specs=[SMEM, SMEM] + [whole(a.shape) for a in arrays],
        out_specs=[whole(o.shape) for o in outs],
        out_shape=outs,
        compiler_params=params(),
        cost_estimate=pl.CostEstimate(flops=0, bytes_accessed=1 << 26, transcendentals=0),
        name="make_operator",
    )(place, taps, *arrays)


def times(values, weights):
    rank = values.shape[1]
    both = jnp.dot(
        jnp.concatenate(two_halves(values), axis=1), weights, preferred_element_type=jnp.float32
    )
    return both[:, :rank] + both[:, rank:]


def shifted(values, by):
    size = values.shape[0]
    return values if by == 0 else pltpu.roll(values, by % size, 0)


def blur_down(taps, field):
    total = None
    for block in range(-REACH, REACH + 1):
        term = None
        for phase in range(DEC):
            offset = DEC * block + phase
            if offset <= W:
                more = taps[offset + W] * field(phase)
                term = more if term is None else term + more
        term = shifted(term, -block)
        total = term if total is None else total + term
    return total


def blur_up(taps, values, phase):
    total = None
    for block in range(-REACH, REACH + 1):
        offset = DEC * block + phase
        if offset <= W:
            term = taps[offset + W] * shifted(values, block)
            total = term if total is None else total + term
    return total


def sum_kernel(place, band, response, own, *refs):
    del place
    out, band_gram, merged_gram = refs[-3:]
    total = own[...].astype(jnp.float32)
    for values in refs[:-3]:
        total += values[...].astype(jnp.float32)
    out[...] = total
    merged = jnp.dot(
        response[...], band[...], precision=FULL_PRECISION, preferred_element_type=jnp.float32
    )
    band_gram[...] = gram_of(band[...])
    merged_gram[...] = gram_of(merged)


def sum_arrived(place, band, response, own, arrived):
    shape = arrived[0].shape
    rank = band.shape[1]
    square = jax.ShapeDtypeStruct((rank, rank), jnp.float32)
    outs = [jax.ShapeDtypeStruct(shape, jnp.float32), square, square]
    return pl.pallas_call(
        sum_kernel,
        grid_spec=pltpu.PrefetchScalarGridSpec(
            num_scalar_prefetch=1,
            grid=(1,),
            in_specs=[whole(band.shape), whole(response.shape)]
            + [pl.BlockSpec(shape, lambda i, place: (place[0], 0))]
            + [whole(shape) for _ in arrived],
            out_specs=[whole(o.shape) for o in outs],
        ),
        out_shape=outs,
        compiler_params=params(),
        name="sum_arrived",
    )(place, band, response, own, *arrived)


def sums_kernel(count, place, *refs):
    del place
    own, own_gram, multi, start = refs[:4]
    arrived = refs[4 : 4 + count]
    hyper, gram, low, high = refs[4 + count :]
    rows = hyper.shape[0]
    total = own[...].astype(jnp.float32)
    grams = own_gram[...].astype(jnp.float32)
    for values in arrived:
        total += values[:rows, :].astype(jnp.float32)
        grams += values[rows:, :].astype(jnp.float32)
    hyper[...] = total
    half = gram.shape[0]
    gram[...] = grams[:half, :] + grams[half:, :]
    first, second = DEC * RIM_MULTI, DEC * RIM_MULTI + RIM
    for pack, top in ((low, True), (high, False)):
        for source, begin, size in (
            (multi, 0, first),
            (hyper, first, RIM),
            (start, second, DEC * RIM_START),
        ):
            rows = source.shape[0]
            at = 0 if top else rows - size
            pack[begin : begin + size, :] = source[at : at + size, :]


def add_sums(place, hyper_part, gram_part, multi, start, arrived):
    fine, rank = start.shape
    coarse = fine // DEC
    pack = jax.ShapeDtypeStruct((DEC * (RIM_MULTI + RIM_START) + RIM, rank), jnp.float32)
    outs = [
        jax.ShapeDtypeStruct((coarse, rank), jnp.float32),
        jax.ShapeDtypeStruct((gram_part.shape[0] // 2, rank), jnp.float32),
        pack,
        pack,
    ]
    return pl.pallas_call(
        functools.partial(sums_kernel, len(arrived)),
        grid_spec=pltpu.PrefetchScalarGridSpec(
            num_scalar_prefetch=1,
            grid=(1,),
            in_specs=[pl.BlockSpec((coarse, rank), lambda i, place: (place[0], 0))]
            + [whole(a.shape) for a in (gram_part, multi, start, *arrived)],
            out_specs=[whole(o.shape) for o in outs],
        ),
        out_shape=outs,
        compiler_params=params(),
        name="add_sums",
    )(place, hyper_part, gram_part, multi, start, *arrived)


def on_diagonal(rows, lanes):
    down = lax.broadcasted_iota(jnp.int32, (rows, lanes), 0)
    along = lax.broadcasted_iota(jnp.int32, (rows, lanes), 1)
    return down == along


def basis_kernel(
    devices, taps, multi, hyper, start, before, after, hyper_w, multi_w, bound, basis, products,
    natural, lifted, held,
):
    fine = multi.shape[0]
    coarse = fine // DEC
    wide = coarse + 2 * RIM
    first, second = DEC * RIM_MULTI, DEC * RIM_MULTI + RIM
    own = slice(RIM, RIM + coarse)

    def apply(which, rim):
        rows = slice(RIM - rim, RIM + coarse + rim)
        fields = [held[which, phase, rows, :] for phase in range(DEC)]
        lowered = times(blur_down(taps, lambda phase: fields[phase]), hyper_w[...])
        return rows, [
            blur_up(taps, lowered, phase) + times(fields[phase], multi_w[...])
            for phase in range(DEC)
        ]

    margin = DEC * (RIM - RIM_START)
    none = jnp.zeros((margin, multi.shape[1]), jnp.float32)
    natural[:margin, :] = none
    natural[margin : DEC * RIM, :] = before[second:, :]
    natural[DEC * RIM : DEC * RIM + fine, :] = start[...]
    natural[DEC * RIM + fine : 2 * DEC * RIM + fine - margin, :] = after[second:, :]
    natural[2 * DEC * RIM + fine - margin :, :] = none
    for phase in range(DEC):
        held[1, phase] = natural[pl.ds(phase, wide, stride=DEC), :]
        basis[ITERS + 1, phase] = held[1, phase, own, :]
    _, mapped = apply(1, RIM)

    lifted[:RIM, :] = before[first:second, :]
    lifted[own, :] = hyper[...]
    lifted[RIM + coarse :, :] = after[first:second, :]
    margin = DEC * (RIM - RIM_MULTI)
    none = jnp.zeros((margin, multi.shape[1]), jnp.float32)
    natural[:margin, :] = none
    natural[margin : DEC * RIM, :] = before[:first, :]
    natural[DEC * RIM : DEC * RIM + fine, :] = multi[...]
    natural[DEC * RIM + fine : 2 * DEC * RIM + fine - margin, :] = after[:first, :]
    natural[2 * DEC * RIM + fine - margin :, :] = none
    quarter = bound[0:1, :] * 0.25
    sums = lifted[...]
    for phase in range(DEC):
        right = natural[pl.ds(phase, wide, stride=DEC), :] + blur_up(taps, sums, phase)
        held[0, phase] = right - quarter * mapped[phase]

    for step in range(ITERS):
        now = step % 2
        rim = -(-REACH * 2 * (ITERS - step) // 8) * 8
        rows, mapped = apply(now, rim)
        for phase in range(DEC):
            basis[step, phase] = held[now, phase, own, :]
            field = held[now, phase, rows, :]
            if step == 0:
                result = 0.5 * mapped[phase] - field
            else:
                result = mapped[phase] - 2.0 * field - held[1 - now, phase, rows, :]
            if step < ITERS - 1:
                held[1 - now, phase, rows, :] = result
            else:
                basis[ITERS, phase] = result[rim : rim + coarse, :]
    rows = []
    for i, j in PAIRS:
        total = jnp.zeros((coarse, multi.shape[1]), jnp.float32)
        for phase in range(DEC):
            total += basis[i, phase] * basis[j, phase]
        rows.append(jnp.sum(total, axis=0, keepdims=True))
    rows.append(jnp.zeros_like(rows[0]))
    block = jnp.sum(jnp.concatenate(rows, axis=0), axis=1, keepdims=True)
    block = jnp.where(on_diagonal(block.shape[0], multi.shape[1]), block, 0.0)
    block = jnp.sum(block, axis=0, keepdims=True)
    for device in range(devices):
        products[device] = block


def make_basis(devices, taps, multi, hyper, start, before, after, hyper_w, multi_w, bound):
    fine, rank = multi.shape
    coarse = fine // DEC
    wide = coarse + 2 * RIM
    arrays = (multi, hyper, start, before, after, hyper_w, multi_w, bound)
    outs = [
        jax.ShapeDtypeStruct((ITERS + 2, DEC, coarse, rank), jnp.float32),
        pltpu.VMEM((devices, 1, rank), jnp.float32),
    ]
    return pl.pallas_call(
        functools.partial(basis_kernel, devices),
        in_specs=[SMEM] + [whole(a.shape) for a in arrays],
        out_specs=[whole(o.shape) for o in outs],
        out_shape=outs,
        scratch_shapes=[
            pltpu.VMEM((DEC * wide, rank), jnp.float32),
            pltpu.VMEM((wide, rank), jnp.float32),
            pltpu.VMEM((2, DEC, wide, rank), jnp.float32),
        ],
        compiler_params=params(),
        name="make_basis",
    )(taps, *arrays)


def coefficients_kernel(products, bound, out, trusted):
    count = ITERS + 1
    row = jnp.sum(products[...], axis=0)
    sums = jnp.broadcast_to(row, (16, row.shape[1]))
    sums = jnp.sum(jnp.where(on_diagonal(*sums.shape), sums, 0.0), axis=1, keepdims=True)
    inner = {}
    for number, (i, j) in enumerate(PAIRS):
        inner[i, j] = inner[j, i] = sums[number : number + 1, :]
    zero = jnp.zeros((1, 1), jnp.float32)
    one = jnp.ones((1, 1), jnp.float32)

    def mapped_of(coefficients):
        result = [2.0 * c for c in coefficients] + [zero] * (count - len(coefficients))
        for j, c in enumerate(coefficients):
            if j + 1 < count:
                result[j + 1] = result[j + 1] + (2.0 * c if j == 0 else c)
            if j > 0:
                result[j - 1] = result[j - 1] + c
        return result

    def product(first, second):
        total = spread = zero
        for i, a in enumerate(first):
            if a is zero:
                continue
            for j, b in enumerate(second):
                if b is zero:
                    continue
                term = a * b * inner[i, j]
                total = total + term
                spread = spread + jnp.abs(term)
        return total, spread / jnp.abs(total)

    walked = [zero] * ITERS
    rest = [one] + [zero] * ITERS
    heading = [one]
    norm = inner[0, 0]
    worst = zero
    for iteration in range(ITERS):
        mapped = mapped_of(heading)
        mapped = mapped[: iteration + 2]
        curved, spread = product(heading, mapped)
        worst = jnp.maximum(worst, spread)
        step = norm / curved
        for j, c in enumerate(heading):
            walked[j] = walked[j] + step * c
        for j, c in enumerate(mapped):
            rest[j] = rest[j] - step * c
        if iteration < ITERS - 1:
            active = rest[: iteration + 2]
            following, spread = product(active, active)
            worst = jnp.maximum(worst, spread)
            ratio = following / norm
            heading = [
                c + ratio * heading[j] if j < len(heading) else c for j, c in enumerate(active)
            ]
            norm = following
    scale = 4.0 / bound[0:1, 0:1]
    rows = [c * scale for c in walked] + rest
    rows = jnp.concatenate(rows + [zero] * (out.shape[0] - len(rows)), axis=0)
    out[...] = jnp.broadcast_to(rows, out.shape)
    trusted[0] = jnp.where(worst < TRUST, 1, 0)[0, 0]


def make_coefficients(products, bound):
    rank = bound.shape[1]
    return pl.pallas_call(
        coefficients_kernel,
        in_specs=[whole(products.shape), whole(bound.shape)],
        out_specs=[whole((16, rank)), SMEM],
        out_shape=[
            jax.ShapeDtypeStruct((16, rank), jnp.float32),
            pltpu.SMEM((1,), jnp.int32),
        ],
        compiler_params=params(),
        name="make_coefficients",
    )(products, bound)


def combine_kernel(coefficients, basis, solution, residual):
    coarse = basis.shape[2]
    for phase in range(DEC):
        rows = pl.ds(phase, coarse, stride=DEC)
        total = basis[ITERS + 1, phase]
        for j in range(ITERS):
            total += coefficients[j : j + 1, :] * basis[j, phase]
        solution[rows, :] = total
        total = coefficients[ITERS : ITERS + 1, :] * basis[0, phase]
        for j in range(1, ITERS + 1):
            total += coefficients[ITERS + j : ITERS + j + 1, :] * basis[j, phase]
        residual[rows, :] = total


def combine(coefficients, basis):
    arrays = (coefficients, basis)
    out = jax.ShapeDtypeStruct((DEC * basis.shape[2], basis.shape[3]), jnp.float32)
    return pl.pallas_call(
        combine_kernel,
        in_specs=[whole(a.shape) for a in arrays],
        out_specs=[whole(out.shape)] * 2,
        out_shape=[out] * 2,
        compiler_params=params(),
        name="combine",
    )(*arrays)


def to_next(values, axis, count):
    return lax.ppermute(values, axis, [(i, (i + 1) % count) for i in range(count)])


def to_previous(values, axis, count):
    return lax.ppermute(values, axis, [((i + 1) % count, i) for i in range(count)])


def step_by_step(taps, multi, hyper, start, hyper_gram, multi_gram, devices):
    def widened(values, breadth):
        return jnp.concatenate(
            [
                to_next(values[-breadth:], BOTH, devices),
                values,
                to_previous(values[:breadth], BOTH, devices),
            ]
        )

    def down(values):
        rows = values.shape[0] // DEC
        parts = values.reshape(rows, DEC, -1)
        size = rows - 2 * REACH
        total = 0.0
        for offset in range(-W, W + 1):
            block, phase = divmod(offset, DEC)
            total = total + taps[offset + W] * lax.slice_in_dim(
                parts[:, phase], REACH + block, REACH + block + size, axis=0
            )
        return total

    def up(values):
        size = values.shape[0] - 2 * REACH
        phases = []
        for phase in range(DEC):
            total = 0.0
            for block in range(-REACH, REACH + 1):
                offset = DEC * block + phase
                if offset <= W:
                    total = total + taps[offset + W] * lax.slice_in_dim(
                        values, REACH - block, REACH - block + size, axis=0
                    )
            phases.append(total)
        return jnp.stack(phases, axis=1).reshape(DEC * size, -1)

    def operate(values):
        lowered = jnp.dot(down(widened(values, 2 * W)), hyper_gram, precision=FULL_PRECISION)
        return up(lowered) + jnp.dot(values, multi_gram, precision=FULL_PRECISION)

    def inner_sum(first, second):
        return lax.psum(jnp.sum(first * second), BOTH)

    solution = start
    residual = up(widened(hyper, REACH)) + multi - operate(solution)
    direction = residual
    norm = inner_sum(residual, residual)

    def iterate(_, state):
        solution, residual, direction, norm = state
        mapped = operate(direction)
        step = norm / inner_sum(direction, mapped)
        solution = solution + step * direction
        residual = residual - step * mapped
        following = inner_sum(residual, residual)
        return solution, residual, residual + following / norm * direction, following

    solution, residual, _, _ = lax.fori_loop(0, ITERS, iterate, (solution, residual, direction, norm))
    return solution, residual


def body(
    multispectral, hyperspectral, row_start, col_factor, band_factor, response, blur_taps, offsets
):
    across = lax.axis_size("col")
    along = lax.axis_size("row")
    devices = across * along
    place = lax.axis_index("col")
    row = lax.axis_index("row")[None]
    rank = band_factor.shape[1]
    share = rank // along
    fine = row_start.shape[0]

    def exchanged(values, distance):
        return lax.ppermute(values, "row", [(i, i ^ distance) for i in range(along)])

    own = col_factor.T
    partner = exchanged(own, 1)
    half = lax.optimization_barrier(jnp.concatenate([own, jnp.zeros_like(own)]))
    pair = jnp.concatenate([half[:share], partner])
    pair, image = lax.optimization_barrier((pair, multispectral))
    pieces = [pair] + [exchanged(pair, distance) for distance in range(2, along, 2)]
    image, band_factor, response, row_start, held = load(
        (image, band_factor, response, row_start, hyperspectral),
        (
            (2, 2, 2),
            (band_factor.shape[0], 1, band_factor.shape[0]),
            (2, 1, 2),
            (fine, 1, fine),
            (EARLY, 4, EARLY + LATER),
        ),
    )
    before = to_next(jnp.concatenate([p[:, -EDGE:] for p in pieces]), "col", across)
    after = to_previous(jnp.concatenate([p[:, :EDGE] for p in pieces]), "col", across)
    multi_part, columns, held = contract_multi(
        row, band_factor, response, image, pieces, hyperspectral, held, EARLY
    )
    spread = jnp.arange(-W, W + 1, dtype=jnp.int32)
    taps = jnp.sum(
        jnp.where(offsets[:, None] == spread[None, :], blur_taps[:, None], jnp.float32(0.0)), axis=0
    )

    def exchange(values, size, more):
        arrived = []
        for distance in range(1, across):
            piece = lax.dynamic_slice_in_dim(values, (place + distance) % across * size, size, 0)
            if more:
                piece = jnp.concatenate([piece] + more)
            arrived.append(
                lax.ppermute(piece, "col", [(i, (i + distance) % across) for i in range(across)])
            )
        return arrived

    multi_arrived = exchange(multi_part, fine, [])
    hyper_part, gram_part = contract_hyper(
        share, row, taps, columns, before, after, band_factor, held, hyperspectral
    )
    hyper_arrived = exchange(hyper_part, fine // DEC, [gram_part])
    multi, band_gram, merged_gram = sum_arrived(
        place[None], band_factor, response, multi_part, multi_arrived
    )
    hyper, gram, low, high = add_sums(
        place[None], hyper_part, gram_part, multi, row_start, hyper_arrived
    )
    hyper_gram, multi_gram, hyper_w, multi_w, bound = make_operator(
        row, taps, band_gram, merged_gram, gram, exchanged(gram, 1)
    )
    before_rows = to_next(high, BOTH, devices)
    after_rows = to_previous(low, BOTH, devices)
    basis, products = make_basis(
        devices, taps, multi, hyper, row_start, before_rows, after_rows, hyper_w, multi_w, bound
    )
    products = lax.all_to_all(products, BOTH, 0, 0, tiled=True)
    coefficients, trusted = make_coefficients(products, bound)

    def from_start():
        start = jnp.stack(list(basis[ITERS + 1]), axis=1).reshape(fine, rank)
        return step_by_step(taps, multi, hyper, start, hyper_gram, multi_gram, devices)

    return lax.cond(trusted[0] != 0, lambda: tuple(combine(coefficients, basis)), from_start)


def solution(mesh):
    in_specs = (
        P(None, "row", "col"),
        P(None, "row", "col"),
        P(("row", "col"), None),
        P("col", "row"),
        P(),
        P(),
        P(),
        P(),
    )
    out_specs = (P(("row", "col"), None), P(("row", "col"), None))
    return jax.shard_map(body, mesh=mesh, in_specs=in_specs, out_specs=out_specs, check_vma=False)
```

```python
import functools
import math

import jax
import jax.numpy as jnp
from jax import lax
from jax.experimental import pallas as pl
from jax.experimental.pallas import tpu as pltpu
from jax.sharding import PartitionSpec as P

DEC = 4
W = 8
REACH = W // DEC
ITERS = 4
RIDGE_TERM = 0.1
FULL_PRECISION = lax.Precision.HIGHEST
BOTH = ("row", "col")
ROWS_A = 512
RIM = 24
RIM_MULTI = 16
RIM_START = 20
PAIRS = [(i, j) for i in range(ITERS + 1) for j in range(i, ITERS + 1)]
TRUST = 2.0e4
EDGE = 16
EARLY = 36
LATER = 20
VMEM_LIMIT = 20 * 1024 * 1024


def params():
    return pltpu.CompilerParams(vmem_limit_bytes=VMEM_LIMIT)


def whole(shape):
    return pl.BlockSpec(shape, lambda *_: (0,) * len(shape))


SMEM = pl.BlockSpec(memory_space=pltpu.SMEM)
VMEM = pl.BlockSpec(memory_space=pltpu.VMEM)


def in_space(values, space):
    return pltpu.with_memory_space_constraint(values, space)


def two_halves(matrix):
    high = matrix.astype(jnp.bfloat16)
    low = (matrix - high.astype(jnp.float32)).astype(jnp.bfloat16)
    return high, low


def gram_of(values):
    return lax.dot_general(
        values, values, (((0,), (0,)), ((), ())), precision=FULL_PRECISION,
        preferred_element_type=jnp.float32,
    )


def load_kernel(ranges, *refs):
    count = len(ranges)
    copies = []
    for source, target, (rows, parts, _) in zip(refs[:count], refs[count : 2 * count], ranges):
        size = rows // parts
        for part in range(parts):
            piece = pl.ds(part * size, size)
            copies.append(
                pltpu.make_async_copy(
                    source.at[piece], target.at[piece], refs[2 * count].at[len(copies)]
                )
            )
    for copy in copies:
        copy.start()
    for copy in copies:
        copy.wait()


def load(arrays, ranges):
    shapes = [(room, *a.shape[1:]) for a, (_, _, room) in zip(arrays, ranges)]
    size = sum(a.dtype.itemsize * math.prod(shape) for a, shape in zip(arrays, shapes))
    return pl.pallas_call(
        functools.partial(load_kernel, ranges),
        in_specs=[pl.BlockSpec(memory_space=pl.ANY)] * len(arrays),
        out_specs=[VMEM] * len(arrays),
        out_shape=[pltpu.VMEM(shape, a.dtype) for a, shape in zip(arrays, shapes)],
        scratch_shapes=[pltpu.SemaphoreType.DMA((sum(parts for _, parts, _ in ranges),))],
        compiler_params=params(),
        cost_estimate=pl.CostEstimate(flops=0, bytes_accessed=2 * size, transcendentals=0),
        name="load",
    )(*[in_space(a, pltpu.HBM) for a in arrays])


def in_rank_order(place, share, pieces, target):
    pair = place[0] // 2
    core = place[0] % 2
    for distance, piece in enumerate(pieces):
        slot = 2 * (pair ^ distance)
        values = piece.astype(jnp.float32)
        first = pl.multiple_of((slot + core) * share, share)
        target[pl.ds(first, share), : values.shape[1]] = values[:share, :]
        second = pl.multiple_of((slot + 1 - core) * share, share)
        target[pl.ds(second, share), : values.shape[1]] = values[share:, :]


def multi_kernel(count, first, place, band, response, image, other, held, *refs):
    del held
    pieces = refs[:count]
    out, columns, bands, pairs, ranks, semaphore = refs[count:]
    rows = pl.ds(first, bands.shape[0] - first)
    copy = pltpu.make_async_copy(other.at[rows], bands.at[rows], semaphore)
    copy.start()
    depth = image.shape[2]
    rank = out.shape[1]
    in_rank_order(place, pieces[0].shape[0] // 2, [p[:, :depth] for p in pieces], ranks)
    for start in range(0, depth, rank):
        columns[start : start + rank, :] = ranks[:, start : start + rank].T
    merged = jnp.dot(
        response[...], band[...], precision=FULL_PRECISION, preferred_element_type=jnp.float32
    )
    field = columns[...]
    for k in range(2):
        pairs[k * depth : (k + 1) * depth, :] = (merged[k : k + 1, :] * field).astype(jnp.bfloat16)

    @pl.when(place[0] >= 0)
    def _():
        for start in range(0, out.shape[0], ROWS_A):
            rows = slice(start, start + ROWS_A)
            pixels = jnp.concatenate([image[0, rows, :], image[1, rows, :]], axis=1)
            total = jnp.dot(pixels, pairs[...], preferred_element_type=jnp.float32)
            out[rows, :] = total.astype(jnp.bfloat16)

    copy.wait()


def contract_multi(place, band, response, image, pieces, other, held, first):
    bands, rows, depth = image.shape
    rank = band.shape[1]
    outs = [
        jax.ShapeDtypeStruct((rows, rank), jnp.bfloat16),
        jax.ShapeDtypeStruct((depth, rank), jnp.float32),
        pltpu.VMEM(held.shape, held.dtype),
    ]
    return pl.pallas_call(
        functools.partial(multi_kernel, len(pieces), first),
        in_specs=[SMEM, whole(band.shape), whole(response.shape), VMEM]
        + [pl.BlockSpec(memory_space=pl.ANY), VMEM]
        + [whole(p.shape) for p in pieces],
        out_specs=[whole(o.shape) for o in outs[:2]] + [VMEM],
        input_output_aliases={5: 2},
        out_shape=outs,
        scratch_shapes=[
            pltpu.VMEM((bands * depth, rank), jnp.bfloat16),
            pltpu.VMEM((rank, depth), jnp.float32),
            pltpu.SemaphoreType.DMA,
        ],
        compiler_params=params(),
        cost_estimate=pl.CostEstimate(
            flops=2 * bands * rows * depth * rank, bytes_accessed=1 << 23, transcendentals=0
        ),
        name="contract_multi",
    )(
        place, band, response, in_space(image, pltpu.VMEM), in_space(other, pltpu.HBM),
        in_space(held, pltpu.VMEM), *pieces,
    )


def hyper_kernel(
    share, place, taps, columns, before, after, band, held, image, out, gram, wide, ranks, packed,
    rest, total, semaphore,
):
    depth, rank = columns.shape
    ready = held.shape[0]
    copy = pltpu.make_async_copy(image.at[pl.ds(ready, rest.shape[0])], rest, semaphore)
    copy.start()
    wide[EDGE : EDGE + depth, :] = columns[...]
    for edge, first in ((before, 0), (after, EDGE + depth)):
        values = edge[...].astype(jnp.float32)
        size = 2 * share
        in_rank_order(place, share, [values[i : i + size, :] for i in range(0, rank, size)], ranks)
        wide[first : first + EDGE, :] = ranks[...].T[:EDGE, :]
    coarse = jnp.zeros((depth // DEC, rank), jnp.float32)
    for offset in range(-W, W + 1):
        coarse += taps[offset + W] * wide[pl.ds(EDGE + offset, depth // DEC, stride=DEC), :]

    exact = columns[...].astype(jnp.bfloat16)
    fine_gram = lax.dot_general(
        exact, exact, (((0,), (0,)), ((), ())), preferred_element_type=jnp.float32
    )
    coarse_gram = gram_of(coarse)
    down = lax.broadcasted_iota(jnp.int32, (rank, rank), 0)
    along = lax.broadcasted_iota(jnp.int32, (rank, rank), 1)
    packed[:rank, :] = jnp.where(along >= down, fine_gram, coarse_gram)
    diagonal = jnp.sum(jnp.where(along == down, coarse_gram, 0.0), axis=0, keepdims=True)
    packed[rank:, :] = jnp.broadcast_to(diagonal, (packed.shape[0] - rank, rank))
    half = packed.shape[0] // 2
    part = packed[pl.ds(pl.multiple_of(place[0] % 2 * half, 8), half), :]
    high = part.astype(jnp.bfloat16).astype(jnp.float32)
    gram[...] = jnp.concatenate([high, part - high], axis=0).astype(jnp.bfloat16)

    def product(source, offset):
        pixels = [source[k] for k in range(source.shape[0])]
        pairs = [
            (band[offset + k : offset + k + 1, :] * coarse).astype(jnp.bfloat16)
            for k in range(len(pixels))
        ]
        return jnp.dot(
            jnp.concatenate(pixels, axis=1),
            jnp.concatenate(pairs, axis=0),
            preferred_element_type=jnp.float32,
        )

    @pl.when(place[0] >= 0)
    def _():
        total[...] = product(held, 0)

    copy.wait()
    out[...] = (total[...] + product(rest, ready)).astype(jnp.bfloat16)


def contract_hyper(share, place, taps, columns, before, after, band, held, image):
    bands, rows, depth = image.shape
    fine, rank = columns.shape
    rest = bands - held.shape[0]
    outs = [
        jax.ShapeDtypeStruct((rows, rank), jnp.bfloat16),
        jax.ShapeDtypeStruct((rank + 16, rank), jnp.bfloat16),
    ]
    return pl.pallas_call(
        functools.partial(hyper_kernel, share),
        in_specs=[SMEM, SMEM]
        + [whole(a.shape) for a in (columns, before, after, band)]
        + [VMEM, pl.BlockSpec(memory_space=pl.ANY)],
        out_specs=[whole(o.shape) for o in outs],
        out_shape=outs,
        scratch_shapes=[
            pltpu.VMEM((fine + 2 * EDGE, rank), jnp.float32),
            pltpu.VMEM((rank, rank), jnp.float32),
            pltpu.VMEM((rank + 16, rank), jnp.float32),
            pltpu.VMEM((rest, rows, depth), image.dtype),
            pltpu.VMEM((rows, rank), jnp.float32),
            pltpu.SemaphoreType.DMA,
        ],
        compiler_params=params(),
        name="contract_hyper",
    )(
        place, taps, columns, before, after, band, in_space(held, pltpu.VMEM),
        in_space(image, pltpu.HBM),
    )


def operator_kernel(
    place, taps, band_gram, merged_gram, own, other, hyper_out, multi_out, hyper_w, multi_w, bound
):
    rank = band_gram.shape[1]
    even = place[0] % 2 == 0
    lower = jnp.where(even, own[...], other[...])
    upper = jnp.where(even, other[...], own[...])
    packed = jnp.concatenate([lower, upper], axis=0)
    diagonal = packed[rank : rank + 1, :]
    packed = packed[:rank, :]
    turned = packed.T
    down = lax.broadcasted_iota(jnp.int32, (rank, rank), 0)
    along = lax.broadcasted_iota(jnp.int32, (rank, rank), 1)
    column_gram = jnp.where(along >= down, packed, turned)
    coarse_gram = jnp.where(along < down, packed, jnp.where(along == down, diagonal, turned))
    hyper = coarse_gram * band_gram[...]
    multi = column_gram * merged_gram[...] + jnp.where(along == down, RIDGE_TERM, 0.0)
    hyper_out[...] = hyper
    multi_out[...] = multi
    squared = jnp.float32(0.0)
    for phase in range(DEC):
        in_phase = jnp.float32(0.0)
        for offset in range(-W, W + 1):
            if offset % DEC == phase:
                in_phase = in_phase + taps[offset + W]
        squared = squared + in_phase * in_phase
    largest = squared * hyper + multi

    def total_of(values):
        return jnp.sum(jnp.sum(values, axis=1, keepdims=True), axis=0, keepdims=True)

    def trace(values):
        return total_of(jnp.where(along == down, values, 0.0))

    power = largest / trace(largest)
    for _ in range(4):
        power = jnp.dot(power, power, preferred_element_type=jnp.float32)
    top = 1.1 * total_of(power * largest) / trace(power)
    bound[...] = jnp.broadcast_to(top, bound.shape)
    for matrix, weights in ((hyper, hyper_w), (multi, multi_w)):
        high, low = two_halves(matrix * (4.0 / top))
        weights[:rank, :rank] = high
        weights[:rank, rank:] = low
        weights[rank:, :rank] = high
        weights[rank:, rank:] = jnp.zeros_like(high)


def make_operator(place, taps, band_gram, merged_gram, own, other):
    rank = band_gram.shape[1]
    square = jax.ShapeDtypeStruct((rank, rank), jnp.float32)
    weights = jax.ShapeDtypeStruct((2 * rank, 2 * rank), jnp.bfloat16)
    bound = jax.ShapeDtypeStruct((8, rank), jnp.float32)
    outs = [square, square, weights, weights, bound]
    arrays = (band_gram, merged_gram, own, other)
    return pl.pallas_call(
        operator_kernel,
        in_specs=[SMEM, SMEM] + [whole(a.shape) for a in arrays],
        out_specs=[whole(o.shape) for o in outs],
        out_shape=outs,
        compiler_params=params(),
        cost_estimate=pl.CostEstimate(flops=0, bytes_accessed=1 << 26, transcendentals=0),
        name="make_operator",
    )(place, taps, *arrays)


def times(values, weights):
    rank = values.shape[1]
    both = jnp.dot(
        jnp.concatenate(two_halves(values), axis=1), weights, preferred_element_type=jnp.float32
    )
    return both[:, :rank] + both[:, rank:]


def shifted(values, by):
    size = values.shape[0]
    return values if by == 0 else pltpu.roll(values, by % size, 0)


def blur_down(taps, field):
    total = None
    for block in range(-REACH, REACH + 1):
        term = None
        for phase in range(DEC):
            offset = DEC * block + phase
            if offset <= W:
                more = taps[offset + W] * field(phase)
                term = more if term is None else term + more
        term = shifted(term, -block)
        total = term if total is None else total + term
    return total


def blur_up(taps, values, phase):
    total = None
    for block in range(-REACH, REACH + 1):
        offset = DEC * block + phase
        if offset <= W:
            term = taps[offset + W] * shifted(values, block)
            total = term if total is None else total + term
    return total


def sum_kernel(place, band, response, own, *refs):
    del place
    out, band_gram, merged_gram = refs[-3:]
    total = own[...].astype(jnp.float32)
    for values in refs[:-3]:
        total += values[...].astype(jnp.float32)
    out[...] = total
    merged = jnp.dot(
        response[...], band[...], precision=FULL_PRECISION, preferred_element_type=jnp.float32
    )
    band_gram[...] = gram_of(band[...])
    merged_gram[...] = gram_of(merged)


def sum_arrived(place, band, response, own, arrived):
    shape = arrived[0].shape
    rank = band.shape[1]
    square = jax.ShapeDtypeStruct((rank, rank), jnp.float32)
    outs = [jax.ShapeDtypeStruct(shape, jnp.float32), square, square]
    return pl.pallas_call(
        sum_kernel,
        grid_spec=pltpu.PrefetchScalarGridSpec(
            num_scalar_prefetch=1,
            grid=(1,),
            in_specs=[whole(band.shape), whole(response.shape)]
            + [pl.BlockSpec(shape, lambda i, place: (place[0], 0))]
            + [whole(shape) for _ in arrived],
            out_specs=[whole(o.shape) for o in outs],
        ),
        out_shape=outs,
        compiler_params=params(),
        name="sum_arrived",
    )(place, band, response, own, *arrived)


def sums_kernel(count, place, *refs):
    even = place[0] % 2 == 0
    own, own_gram, multi, start = refs[:4]
    arrived = refs[4 : 4 + count]
    hyper, gram, first_pack, second_pack = refs[4 + count :]
    rows = hyper.shape[0]
    total = own[...].astype(jnp.float32)
    grams = own_gram[...].astype(jnp.float32)
    for values in arrived:
        total += values[:rows, :].astype(jnp.float32)
        grams += values[rows:, :].astype(jnp.float32)
    hyper[...] = total
    half = gram.shape[0]
    gram[...] = grams[:half, :] + grams[half:, :]
    first, second = DEC * RIM_MULTI, DEC * RIM_MULTI + RIM
    for source, begin, size in (
        (multi, 0, first),
        (hyper, first, RIM),
        (start, second, DEC * RIM_START),
    ):
        low = source[:size, :]
        high = source[source.shape[0] - size :, :]
        first_pack[begin : begin + size, :] = jnp.where(even, high, low)
        second_pack[begin : begin + size, :] = jnp.where(even, low, high)


def add_sums(place, hyper_part, gram_part, multi, start, arrived):
    fine, rank = start.shape
    coarse = fine // DEC
    pack = jax.ShapeDtypeStruct((DEC * (RIM_MULTI + RIM_START) + RIM, rank), jnp.float32)
    outs = [
        jax.ShapeDtypeStruct((coarse, rank), jnp.float32),
        jax.ShapeDtypeStruct((gram_part.shape[0] // 2, rank), jnp.float32),
        pack,
        pack,
    ]
    return pl.pallas_call(
        functools.partial(sums_kernel, len(arrived)),
        grid_spec=pltpu.PrefetchScalarGridSpec(
            num_scalar_prefetch=1,
            grid=(1,),
            in_specs=[pl.BlockSpec((coarse, rank), lambda i, place: (place[0], 0))]
            + [whole(a.shape) for a in (gram_part, multi, start, *arrived)],
            out_specs=[whole(o.shape) for o in outs],
        ),
        out_shape=outs,
        compiler_params=params(),
        name="add_sums",
    )(place, hyper_part, gram_part, multi, start, *arrived)


def on_diagonal(rows, lanes):
    down = lax.broadcasted_iota(jnp.int32, (rows, lanes), 0)
    along = lax.broadcasted_iota(jnp.int32, (rows, lanes), 1)
    return down == along


def basis_kernel(
    devices, place, taps, multi, hyper, start, first_rows, second_rows, hyper_w, multi_w, bound,
    basis, products, natural, lifted, held,
):
    even = place[0] % 2 == 0
    before = jnp.where(even, second_rows[...], first_rows[...])
    after = jnp.where(even, first_rows[...], second_rows[...])
    fine = multi.shape[0]
    coarse = fine // DEC
    wide = coarse + 2 * RIM
    first, second = DEC * RIM_MULTI, DEC * RIM_MULTI + RIM
    own = slice(RIM, RIM + coarse)

    def apply(which, rim):
        rows = slice(RIM - rim, RIM + coarse + rim)
        fields = [held[which, phase, rows, :] for phase in range(DEC)]
        lowered = times(blur_down(taps, lambda phase: fields[phase]), hyper_w[...])
        return rows, [
            blur_up(taps, lowered, phase) + times(fields[phase], multi_w[...])
            for phase in range(DEC)
        ]

    margin = DEC * (RIM - RIM_START)
    none = jnp.zeros((margin, multi.shape[1]), jnp.float32)
    natural[:margin, :] = none
    natural[margin : DEC * RIM, :] = before[second:, :]
    natural[DEC * RIM : DEC * RIM + fine, :] = start[...]
    natural[DEC * RIM + fine : 2 * DEC * RIM + fine - margin, :] = after[second:, :]
    natural[2 * DEC * RIM + fine - margin :, :] = none
    for phase in range(DEC):
        held[1, phase] = natural[pl.ds(phase, wide, stride=DEC), :]
        basis[ITERS + 1, phase] = held[1, phase, own, :]
    _, mapped = apply(1, RIM)

    lifted[:RIM, :] = before[first:second, :]
    lifted[own, :] = hyper[...]
    lifted[RIM + coarse :, :] = after[first:second, :]
    margin = DEC * (RIM - RIM_MULTI)
    none = jnp.zeros((margin, multi.shape[1]), jnp.float32)
    natural[:margin, :] = none
    natural[margin : DEC * RIM, :] = before[:first, :]
    natural[DEC * RIM : DEC * RIM + fine, :] = multi[...]
    natural[DEC * RIM + fine : 2 * DEC * RIM + fine - margin, :] = after[:first, :]
    natural[2 * DEC * RIM + fine - margin :, :] = none
    quarter = bound[0:1, :] * 0.25
    sums = lifted[...]
    for phase in range(DEC):
        right = natural[pl.ds(phase, wide, stride=DEC), :] + blur_up(taps, sums, phase)
        held[0, phase] = right - quarter * mapped[phase]

    for step in range(ITERS):
        now = step % 2
        rim = -(-REACH * 2 * (ITERS - step) // 8) * 8
        rows, mapped = apply(now, rim)
        for phase in range(DEC):
            basis[step, phase] = held[now, phase, own, :]
            field = held[now, phase, rows, :]
            if step == 0:
                result = 0.5 * mapped[phase] - field
            else:
                result = mapped[phase] - 2.0 * field - held[1 - now, phase, rows, :]
            if step < ITERS - 1:
                held[1 - now, phase, rows, :] = result
            else:
                basis[ITERS, phase] = result[rim : rim + coarse, :]
    rows = []
    for i, j in PAIRS:
        total = jnp.zeros((coarse, multi.shape[1]), jnp.float32)
        for phase in range(DEC):
            total += basis[i, phase] * basis[j, phase]
        rows.append(jnp.sum(total, axis=0, keepdims=True))
    rows.append(jnp.zeros_like(rows[0]))
    block = jnp.sum(jnp.concatenate(rows, axis=0), axis=1, keepdims=True)
    block = jnp.where(on_diagonal(block.shape[0], multi.shape[1]), block, 0.0)
    block = jnp.sum(block, axis=0, keepdims=True)
    for device in range(devices):
        products[device] = block


def make_basis(
    devices, place, taps, multi, hyper, start, first_rows, second_rows, hyper_w, multi_w, bound
):
    fine, rank = multi.shape
    coarse = fine // DEC
    wide = coarse + 2 * RIM
    arrays = (multi, hyper, start, first_rows, second_rows, hyper_w, multi_w, bound)
    outs = [
        jax.ShapeDtypeStruct((ITERS + 2, DEC, coarse, rank), jnp.float32),
        pltpu.VMEM((devices, 1, rank), jnp.float32),
    ]
    return pl.pallas_call(
        functools.partial(basis_kernel, devices),
        in_specs=[SMEM, SMEM] + [whole(a.shape) for a in arrays],
        out_specs=[whole(o.shape) for o in outs],
        out_shape=outs,
        scratch_shapes=[
            pltpu.VMEM((DEC * wide, rank), jnp.float32),
            pltpu.VMEM((wide, rank), jnp.float32),
            pltpu.VMEM((2, DEC, wide, rank), jnp.float32),
        ],
        compiler_params=params(),
        name="make_basis",
    )(place, taps, *arrays)


def coefficients_kernel(products, bound, out, trusted):
    count = ITERS + 1
    row = jnp.sum(products[...], axis=0)
    sums = jnp.broadcast_to(row, (16, row.shape[1]))
    sums = jnp.sum(jnp.where(on_diagonal(*sums.shape), sums, 0.0), axis=1, keepdims=True)
    inner = {}
    for number, (i, j) in enumerate(PAIRS):
        inner[i, j] = inner[j, i] = sums[number : number + 1, :]
    zero = jnp.zeros((1, 1), jnp.float32)
    one = jnp.ones((1, 1), jnp.float32)

    def mapped_of(coefficients):
        result = [2.0 * c for c in coefficients] + [zero] * (count - len(coefficients))
        for j, c in enumerate(coefficients):
            if j + 1 < count:
                result[j + 1] = result[j + 1] + (2.0 * c if j == 0 else c)
            if j > 0:
                result[j - 1] = result[j - 1] + c
        return result

    def product(first, second):
        total = spread = zero
        for i, a in enumerate(first):
            if a is zero:
                continue
            for j, b in enumerate(second):
                if b is zero:
                    continue
                term = a * b * inner[i, j]
                total = total + term
                spread = spread + jnp.abs(term)
        return total, spread / jnp.abs(total)

    walked = [zero] * ITERS
    rest = [one] + [zero] * ITERS
    heading = [one]
    norm = inner[0, 0]
    worst = zero
    for iteration in range(ITERS):
        mapped = mapped_of(heading)
        mapped = mapped[: iteration + 2]
        curved, spread = product(heading, mapped)
        worst = jnp.maximum(worst, spread)
        step = norm / curved
        for j, c in enumerate(heading):
            walked[j] = walked[j] + step * c
        for j, c in enumerate(mapped):
            rest[j] = rest[j] - step * c
        if iteration < ITERS - 1:
            active = rest[: iteration + 2]
            following, spread = product(active, active)
            worst = jnp.maximum(worst, spread)
            ratio = following / norm
            heading = [
                c + ratio * heading[j] if j < len(heading) else c for j, c in enumerate(active)
            ]
            norm = following
    scale = 4.0 / bound[0:1, 0:1]
    rows = [c * scale for c in walked] + rest
    rows = jnp.concatenate(rows + [zero] * (out.shape[0] - len(rows)), axis=0)
    out[...] = jnp.broadcast_to(rows, out.shape)
    trusted[0] = jnp.where(worst < TRUST, 1, 0)[0, 0]


def make_coefficients(products, bound):
    rank = bound.shape[1]
    return pl.pallas_call(
        coefficients_kernel,
        in_specs=[whole(products.shape), whole(bound.shape)],
        out_specs=[whole((16, rank)), SMEM],
        out_shape=[
            jax.ShapeDtypeStruct((16, rank), jnp.float32),
            pltpu.SMEM((1,), jnp.int32),
        ],
        compiler_params=params(),
        name="make_coefficients",
    )(products, bound)


def combine_kernel(coefficients, basis, solution, residual):
    coarse = basis.shape[2]
    for phase in range(DEC):
        rows = pl.ds(phase, coarse, stride=DEC)
        total = basis[ITERS + 1, phase]
        for j in range(ITERS):
            total += coefficients[j : j + 1, :] * basis[j, phase]
        solution[rows, :] = total
        total = coefficients[ITERS : ITERS + 1, :] * basis[0, phase]
        for j in range(1, ITERS + 1):
            total += coefficients[ITERS + j : ITERS + j + 1, :] * basis[j, phase]
        residual[rows, :] = total


def combine(coefficients, basis):
    arrays = (coefficients, basis)
    out = jax.ShapeDtypeStruct((DEC * basis.shape[2], basis.shape[3]), jnp.float32)
    return pl.pallas_call(
        combine_kernel,
        in_specs=[whole(a.shape) for a in arrays],
        out_specs=[whole(out.shape)] * 2,
        out_shape=[out] * 2,
        compiler_params=params(),
        name="combine",
    )(*arrays)


def to_next(values, axis, count):
    return lax.ppermute(values, axis, [(i, (i + 1) % count) for i in range(count)])


def to_previous(values, axis, count):
    return lax.ppermute(values, axis, [((i + 1) % count, i) for i in range(count)])


def step_by_step(taps, multi, hyper, start, hyper_gram, multi_gram, devices):
    def widened(values, breadth):
        return jnp.concatenate(
            [
                to_next(values[-breadth:], BOTH, devices),
                values,
                to_previous(values[:breadth], BOTH, devices),
            ]
        )

    def down(values):
        rows = values.shape[0] // DEC
        parts = values.reshape(rows, DEC, -1)
        size = rows - 2 * REACH
        total = 0.0
        for offset in range(-W, W + 1):
            block, phase = divmod(offset, DEC)
            total = total + taps[offset + W] * lax.slice_in_dim(
                parts[:, phase], REACH + block, REACH + block + size, axis=0
            )
        return total

    def up(values):
        size = values.shape[0] - 2 * REACH
        phases = []
        for phase in range(DEC):
            total = 0.0
            for block in range(-REACH, REACH + 1):
                offset = DEC * block + phase
                if offset <= W:
                    total = total + taps[offset + W] * lax.slice_in_dim(
                        values, REACH - block, REACH - block + size, axis=0
                    )
            phases.append(total)
        return jnp.stack(phases, axis=1).reshape(DEC * size, -1)

    def operate(values):
        lowered = jnp.dot(down(widened(values, 2 * W)), hyper_gram, precision=FULL_PRECISION)
        return up(lowered) + jnp.dot(values, multi_gram, precision=FULL_PRECISION)

    def inner_sum(first, second):
        return lax.psum(jnp.sum(first * second), BOTH)

    solution = start
    residual = up(widened(hyper, REACH)) + multi - operate(solution)
    direction = residual
    norm = inner_sum(residual, residual)

    def iterate(_, state):
        solution, residual, direction, norm = state
        mapped = operate(direction)
        step = norm / inner_sum(direction, mapped)
        solution = solution + step * direction
        residual = residual - step * mapped
        following = inner_sum(residual, residual)
        return solution, residual, residual + following / norm * direction, following

    solution, residual, _, _ = lax.fori_loop(0, ITERS, iterate, (solution, residual, direction, norm))
    return solution, residual


def body(
    multispectral, hyperspectral, row_start, col_factor, band_factor, response, blur_taps, offsets
):
    across = lax.axis_size("col")
    along = lax.axis_size("row")
    devices = across * along
    place = lax.axis_index("col")
    row = lax.axis_index("row")[None]
    rank = band_factor.shape[1]
    share = rank // along
    fine = row_start.shape[0]

    def exchanged(values, distance):
        return lax.ppermute(values, "row", [(i, i ^ distance) for i in range(along)])

    own = col_factor.T
    partner = exchanged(own, 1)
    half = lax.optimization_barrier(jnp.concatenate([own, jnp.zeros_like(own)]))
    pair = jnp.concatenate([half[:share], partner])
    pair, image = lax.optimization_barrier((pair, multispectral))
    pieces = [pair] + [exchanged(pair, distance) for distance in range(2, along, 2)]
    image, band_factor, response, row_start, held = load(
        (image, band_factor, response, row_start, hyperspectral),
        (
            (2, 2, 2),
            (band_factor.shape[0], 1, band_factor.shape[0]),
            (2, 1, 2),
            (fine, 1, fine),
            (EARLY, 4, EARLY + LATER),
        ),
    )
    before = to_next(jnp.concatenate([p[:, -EDGE:] for p in pieces]), "col", across)
    after = to_previous(jnp.concatenate([p[:, :EDGE] for p in pieces]), "col", across)
    multi_part, columns, held = contract_multi(
        row, band_factor, response, image, pieces, hyperspectral, held, EARLY
    )
    spread = jnp.arange(-W, W + 1, dtype=jnp.int32)
    taps = jnp.sum(
        jnp.where(offsets[:, None] == spread[None, :], blur_taps[:, None], jnp.float32(0.0)), axis=0
    )

    def exchange(values, size, more):
        arrived = []
        for distance in range(1, across):
            piece = lax.dynamic_slice_in_dim(values, (place + distance) % across * size, size, 0)
            if more:
                piece = jnp.concatenate([piece] + more)
            arrived.append(
                lax.ppermute(piece, "col", [(i, (i + distance) % across) for i in range(across)])
            )
        return arrived

    multi_arrived = exchange(multi_part, fine, [])
    hyper_part, gram_part = contract_hyper(
        share, row, taps, columns, before, after, band_factor, held, hyperspectral
    )
    hyper_arrived = exchange(hyper_part, fine // DEC, [gram_part])
    multi, band_gram, merged_gram = sum_arrived(
        place[None], band_factor, response, multi_part, multi_arrived
    )
    hyper, gram, first_pack, second_pack = add_sums(
        place[None], hyper_part, gram_part, multi, row_start, hyper_arrived
    )
    hyper_gram, multi_gram, hyper_w, multi_w, bound = make_operator(
        row, taps, band_gram, merged_gram, gram, exchanged(gram, 1)
    )
    first_rows = lax.ppermute(first_pack, BOTH, [(i, i ^ 1) for i in range(devices)])
    second_rows = lax.ppermute(
        second_pack, BOTH, [((i + 1) % devices, ((i ^ 1) + 1) % devices) for i in range(devices)]
    )
    basis, products = make_basis(
        devices, place[None], taps, multi, hyper, row_start, first_rows, second_rows, hyper_w,
        multi_w, bound,
    )
    products = lax.all_to_all(products, BOTH, 0, 0, tiled=True)
    coefficients, trusted = make_coefficients(products, bound)

    def from_start():
        start = jnp.stack(list(basis[ITERS + 1]), axis=1).reshape(fine, rank)
        return step_by_step(taps, multi, hyper, start, hyper_gram, multi_gram, devices)

    return lax.cond(trusted[0] != 0, lambda: tuple(combine(coefficients, basis)), from_start)


def solution(mesh):
    in_specs = (
        P(None, "row", "col"),
        P(None, "row", "col"),
        P(("row", "col"), None),
        P("col", "row"),
        P(),
        P(),
        P(),
        P(),
    )
    out_specs = (P(("row", "col"), None), P(("row", "col"), None))
    return jax.shard_map(body, mesh=mesh, in_specs=in_specs, out_specs=out_specs, check_vma=False)
```

```python
import functools
import math

import jax
import jax.numpy as jnp
from jax import lax
from jax.experimental import pallas as pl
from jax.experimental.pallas import tpu as pltpu
from jax.sharding import PartitionSpec as P

DEC = 4
W = 8
REACH = W // DEC
ITERS = 4
RIDGE_TERM = 0.1
FULL_PRECISION = lax.Precision.HIGHEST
BOTH = ("row", "col")
ROWS_A = 512
RIM = 24
RIM_MULTI = 16
RIM_START = 20
PAIRS = [(i, j) for i in range(ITERS + 1) for j in range(i, ITERS + 1)]
TRUST = 2.0e4
EDGE = 16
EARLY = 36
LATER = 20
VMEM_LIMIT = 20 * 1024 * 1024


def params():
    return pltpu.CompilerParams(vmem_limit_bytes=VMEM_LIMIT)


def whole(shape):
    return pl.BlockSpec(shape, lambda *_: (0,) * len(shape))


SMEM = pl.BlockSpec(memory_space=pltpu.SMEM)
VMEM = pl.BlockSpec(memory_space=pltpu.VMEM)


def in_space(values, space):
    return pltpu.with_memory_space_constraint(values, space)


def two_halves(matrix):
    high = matrix.astype(jnp.bfloat16)
    low = (matrix - high.astype(jnp.float32)).astype(jnp.bfloat16)
    return high, low


def gram_of(values):
    return lax.dot_general(
        values, values, (((0,), (0,)), ((), ())), precision=FULL_PRECISION,
        preferred_element_type=jnp.float32,
    )


def load_kernel(ranges, *refs):
    count = len(ranges)
    copies = []
    for source, target, (rows, parts, _) in zip(refs[:count], refs[count : 2 * count], ranges):
        size = rows // parts
        for part in range(parts):
            piece = pl.ds(part * size, size)
            copies.append(
                pltpu.make_async_copy(
                    source.at[piece], target.at[piece], refs[2 * count].at[len(copies)]
                )
            )
    for copy in copies:
        copy.start()
    for copy in copies:
        copy.wait()


def load(arrays, ranges):
    shapes = [(room, *a.shape[1:]) for a, (_, _, room) in zip(arrays, ranges)]
    size = sum(a.dtype.itemsize * math.prod(shape) for a, shape in zip(arrays, shapes))
    return pl.pallas_call(
        functools.partial(load_kernel, ranges),
        in_specs=[pl.BlockSpec(memory_space=pl.ANY)] * len(arrays),
        out_specs=[VMEM] * len(arrays),
        out_shape=[pltpu.VMEM(shape, a.dtype) for a, shape in zip(arrays, shapes)],
        scratch_shapes=[pltpu.SemaphoreType.DMA((sum(parts for _, parts, _ in ranges),))],
        compiler_params=params(),
        cost_estimate=pl.CostEstimate(flops=0, bytes_accessed=2 * size, transcendentals=0),
        name="load",
    )(*[in_space(a, pltpu.HBM) for a in arrays])


def in_rank_order(place, share, pieces, target):
    pair = place[0] // 2
    core = place[0] % 2
    for distance, piece in enumerate(pieces):
        slot = 2 * (pair ^ distance)
        values = piece.astype(jnp.float32)
        first = pl.multiple_of((slot + core) * share, share)
        target[pl.ds(first, share), : values.shape[1]] = values[:share, :]
        second = pl.multiple_of((slot + 1 - core) * share, share)
        target[pl.ds(second, share), : values.shape[1]] = values[share:, :]


def multi_kernel(count, first, place, band, response, image, other, held, *refs):
    del held
    pieces = refs[:count]
    out, columns, bands, pairs, ranks, semaphore = refs[count:]
    rows = pl.ds(first, bands.shape[0] - first)
    copy = pltpu.make_async_copy(other.at[rows], bands.at[rows], semaphore)
    copy.start()
    depth = image.shape[2]
    rank = out.shape[1]
    in_rank_order(place, pieces[0].shape[0] // 2, [p[:, :depth] for p in pieces], ranks)
    for start in range(0, depth, rank):
        columns[start : start + rank, :] = ranks[:, start : start + rank].T
    merged = jnp.dot(
        response[...], band[...], precision=FULL_PRECISION, preferred_element_type=jnp.float32
    )
    field = columns[...]
    for k in range(2):
        pairs[k * depth : (k + 1) * depth, :] = (merged[k : k + 1, :] * field).astype(jnp.bfloat16)

    @pl.when(place[0] >= 0)
    def _():
        for start in range(0, out.shape[0], ROWS_A):
            rows = slice(start, start + ROWS_A)
            pixels = jnp.concatenate([image[0, rows, :], image[1, rows, :]], axis=1)
            total = jnp.dot(pixels, pairs[...], preferred_element_type=jnp.float32)
            out[rows, :] = total.astype(jnp.bfloat16)

    copy.wait()


def contract_multi(place, band, response, image, pieces, other, held, first):
    bands, rows, depth = image.shape
    rank = band.shape[1]
    outs = [
        jax.ShapeDtypeStruct((rows, rank), jnp.bfloat16),
        jax.ShapeDtypeStruct((depth, rank), jnp.float32),
        pltpu.VMEM(held.shape, held.dtype),
    ]
    return pl.pallas_call(
        functools.partial(multi_kernel, len(pieces), first),
        in_specs=[SMEM, whole(band.shape), whole(response.shape), VMEM]
        + [pl.BlockSpec(memory_space=pl.ANY), VMEM]
        + [whole(p.shape) for p in pieces],
        out_specs=[whole(o.shape) for o in outs[:2]] + [VMEM],
        input_output_aliases={5: 2},
        out_shape=outs,
        scratch_shapes=[
            pltpu.VMEM((bands * depth, rank), jnp.bfloat16),
            pltpu.VMEM((rank, depth), jnp.float32),
            pltpu.SemaphoreType.DMA,
        ],
        compiler_params=params(),
        cost_estimate=pl.CostEstimate(
            flops=2 * bands * rows * depth * rank, bytes_accessed=1 << 23, transcendentals=0
        ),
        name="contract_multi",
    )(
        place, band, response, in_space(image, pltpu.VMEM), in_space(other, pltpu.HBM),
        in_space(held, pltpu.VMEM), *pieces,
    )


def hyper_kernel(
    share, place, taps, columns, before, after, band, held, image, out, gram, wide, ranks, packed,
    rest, total, semaphore,
):
    depth, rank = columns.shape
    ready = held.shape[0]
    copy = pltpu.make_async_copy(image.at[pl.ds(ready, rest.shape[0])], rest, semaphore)
    copy.start()
    wide[EDGE : EDGE + depth, :] = columns[...]
    for edge, first in ((before, 0), (after, EDGE + depth)):
        values = edge[...].astype(jnp.float32)
        size = 2 * share
        in_rank_order(place, share, [values[i : i + size, :] for i in range(0, rank, size)], ranks)
        wide[first : first + EDGE, :] = ranks[...].T[:EDGE, :]
    coarse = jnp.zeros((depth // DEC, rank), jnp.float32)
    for offset in range(-W, W + 1):
        coarse += taps[offset + W] * wide[pl.ds(EDGE + offset, depth // DEC, stride=DEC), :]

    exact = columns[...].astype(jnp.bfloat16)
    fine_gram = lax.dot_general(
        exact, exact, (((0,), (0,)), ((), ())), preferred_element_type=jnp.float32
    )
    coarse_gram = gram_of(coarse)
    down = lax.broadcasted_iota(jnp.int32, (rank, rank), 0)
    along = lax.broadcasted_iota(jnp.int32, (rank, rank), 1)
    packed[:rank, :] = jnp.where(along >= down, fine_gram, coarse_gram)
    diagonal = jnp.sum(jnp.where(along == down, coarse_gram, 0.0), axis=0, keepdims=True)
    packed[rank:, :] = jnp.broadcast_to(diagonal, (packed.shape[0] - rank, rank))
    half = packed.shape[0] // 2
    part = packed[pl.ds(pl.multiple_of(place[0] % 2 * half, 8), half), :]
    high = part.astype(jnp.bfloat16).astype(jnp.float32)
    gram[...] = jnp.concatenate([high, part - high], axis=0).astype(jnp.bfloat16)

    def product(source, offset):
        pixels = [source[k] for k in range(source.shape[0])]
        pairs = [
            (band[offset + k : offset + k + 1, :] * coarse).astype(jnp.bfloat16)
            for k in range(len(pixels))
        ]
        return jnp.dot(
            jnp.concatenate(pixels, axis=1),
            jnp.concatenate(pairs, axis=0),
            preferred_element_type=jnp.float32,
        )

    @pl.when(place[0] >= 0)
    def _():
        total[...] = product(held, 0)

    copy.wait()
    out[...] = (total[...] + product(rest, ready)).astype(jnp.bfloat16)


def contract_hyper(share, place, taps, columns, before, after, band, held, image):
    bands, rows, depth = image.shape
    fine, rank = columns.shape
    rest = bands - held.shape[0]
    outs = [
        jax.ShapeDtypeStruct((rows, rank), jnp.bfloat16),
        jax.ShapeDtypeStruct((rank + 16, rank), jnp.bfloat16),
    ]
    return pl.pallas_call(
        functools.partial(hyper_kernel, share),
        in_specs=[SMEM, SMEM]
        + [whole(a.shape) for a in (columns, before, after, band)]
        + [VMEM, pl.BlockSpec(memory_space=pl.ANY)],
        out_specs=[whole(o.shape) for o in outs],
        out_shape=outs,
        scratch_shapes=[
            pltpu.VMEM((fine + 2 * EDGE, rank), jnp.float32),
            pltpu.VMEM((rank, rank), jnp.float32),
            pltpu.VMEM((rank + 16, rank), jnp.float32),
            pltpu.VMEM((rest, rows, depth), image.dtype),
            pltpu.VMEM((rows, rank), jnp.float32),
            pltpu.SemaphoreType.DMA,
        ],
        compiler_params=params(),
        name="contract_hyper",
    )(
        place, taps, columns, before, after, band, in_space(held, pltpu.VMEM),
        in_space(image, pltpu.HBM),
    )


def operator_kernel(
    place, taps, band_gram, merged_gram, own, other, hyper_out, multi_out, hyper_w, multi_w, bound
):
    rank = band_gram.shape[1]
    even = place[0] % 2 == 0
    lower = jnp.where(even, own[...], other[...])
    upper = jnp.where(even, other[...], own[...])
    packed = jnp.concatenate([lower, upper], axis=0)
    diagonal = packed[rank : rank + 1, :]
    packed = packed[:rank, :]
    turned = packed.T
    down = lax.broadcasted_iota(jnp.int32, (rank, rank), 0)
    along = lax.broadcasted_iota(jnp.int32, (rank, rank), 1)
    column_gram = jnp.where(along >= down, packed, turned)
    coarse_gram = jnp.where(along < down, packed, jnp.where(along == down, diagonal, turned))
    hyper = coarse_gram * band_gram[...]
    multi = column_gram * merged_gram[...] + jnp.where(along == down, RIDGE_TERM, 0.0)
    hyper_out[...] = hyper
    multi_out[...] = multi
    squared = jnp.float32(0.0)
    for phase in range(DEC):
        in_phase = jnp.float32(0.0)
        for offset in range(-W, W + 1):
            if offset % DEC == phase:
                in_phase = in_phase + taps[offset + W]
        squared = squared + in_phase * in_phase
    largest = squared * hyper + multi

    def total_of(values):
        return jnp.sum(jnp.sum(values, axis=1, keepdims=True), axis=0, keepdims=True)

    def trace(values):
        return total_of(jnp.where(along == down, values, 0.0))

    power = largest / trace(largest)
    for _ in range(4):
        power = jnp.dot(power, power, preferred_element_type=jnp.float32)
    top = 1.1 * total_of(power * largest) / trace(power)
    bound[...] = jnp.broadcast_to(top, bound.shape)
    for matrix, weights in ((hyper, hyper_w), (multi, multi_w)):
        high, low = two_halves(matrix * (4.0 / top))
        weights[:rank, :rank] = high
        weights[:rank, rank:] = low
        weights[rank:, :rank] = high
        weights[rank:, rank:] = jnp.zeros_like(high)


def make_operator(place, taps, band_gram, merged_gram, own, other):
    rank = band_gram.shape[1]
    square = jax.ShapeDtypeStruct((rank, rank), jnp.float32)
    weights = jax.ShapeDtypeStruct((2 * rank, 2 * rank), jnp.bfloat16)
    bound = jax.ShapeDtypeStruct((8, rank), jnp.float32)
    outs = [square, square, weights, weights, bound]
    arrays = (band_gram, merged_gram, own, other)
    return pl.pallas_call(
        operator_kernel,
        in_specs=[SMEM, SMEM] + [whole(a.shape) for a in arrays],
        out_specs=[whole(o.shape) for o in outs],
        out_shape=outs,
        compiler_params=params(),
        cost_estimate=pl.CostEstimate(flops=0, bytes_accessed=1 << 26, transcendentals=0),
        name="make_operator",
    )(place, taps, *arrays)


def times(values, weights):
    rank = values.shape[1]
    both = jnp.dot(
        jnp.concatenate(two_halves(values), axis=1), weights, preferred_element_type=jnp.float32
    )
    return both[:, :rank] + both[:, rank:]


def shifted(values, by):
    size = values.shape[0]
    return values if by == 0 else pltpu.roll(values, by % size, 0)


def blur_down(taps, field):
    total = None
    for block in range(-REACH, REACH + 1):
        term = None
        for phase in range(DEC):
            offset = DEC * block + phase
            if offset <= W:
                more = taps[offset + W] * field(phase)
                term = more if term is None else term + more
        term = shifted(term, -block)
        total = term if total is None else total + term
    return total


def blur_up(taps, values, phase):
    total = None
    for block in range(-REACH, REACH + 1):
        offset = DEC * block + phase
        if offset <= W:
            term = taps[offset + W] * shifted(values, block)
            total = term if total is None else total + term
    return total


def sum_kernel(place, band, response, own, *refs):
    del place
    out, band_gram, merged_gram = refs[-3:]
    total = own[...].astype(jnp.float32)
    for values in refs[:-3]:
        total += values[...].astype(jnp.float32)
    out[...] = total
    merged = jnp.dot(
        response[...], band[...], precision=FULL_PRECISION, preferred_element_type=jnp.float32
    )
    band_gram[...] = gram_of(band[...])
    merged_gram[...] = gram_of(merged)


def sum_arrived(place, band, response, own, arrived):
    shape = arrived[0].shape
    rank = band.shape[1]
    square = jax.ShapeDtypeStruct((rank, rank), jnp.float32)
    outs = [jax.ShapeDtypeStruct(shape, jnp.float32), square, square]
    return pl.pallas_call(
        sum_kernel,
        grid_spec=pltpu.PrefetchScalarGridSpec(
            num_scalar_prefetch=1,
            grid=(1,),
            in_specs=[whole(band.shape), whole(response.shape)]
            + [pl.BlockSpec(shape, lambda i, place: (place[0], 0))]
            + [whole(shape) for _ in arrived],
            out_specs=[whole(o.shape) for o in outs],
        ),
        out_shape=outs,
        compiler_params=params(),
        name="sum_arrived",
    )(place, band, response, own, *arrived)


def sums_kernel(count, place, *refs):
    even = place[0] % 2 == 0
    own, own_gram, multi, start = refs[:4]
    arrived = refs[4 : 4 + count]
    hyper, gram, first_pack, second_pack = refs[4 + count :]
    rows = hyper.shape[0]
    total = own[...].astype(jnp.float32)
    grams = own_gram[...].astype(jnp.float32)
    for values in arrived:
        total += values[:rows, :].astype(jnp.float32)
        grams += values[rows:, :].astype(jnp.float32)
    hyper[...] = total
    half = gram.shape[0]
    gram[...] = grams[:half, :] + grams[half:, :]
    first, second = DEC * RIM_MULTI, DEC * RIM_MULTI + RIM
    for source, begin, size in (
        (multi, 0, first),
        (hyper, first, RIM),
        (start, second, DEC * RIM_START),
    ):
        low = source[:size, :]
        high = source[source.shape[0] - size :, :]
        first_pack[begin : begin + size, :] = jnp.where(even, high, low)
        second_pack[begin : begin + size, :] = jnp.where(even, low, high)


def add_sums(place, hyper_part, gram_part, multi, start, arrived):
    fine, rank = start.shape
    coarse = fine // DEC
    pack = jax.ShapeDtypeStruct((DEC * (RIM_MULTI + RIM_START) + RIM, rank), jnp.float32)
    outs = [
        jax.ShapeDtypeStruct((coarse, rank), jnp.float32),
        jax.ShapeDtypeStruct((gram_part.shape[0] // 2, rank), jnp.float32),
        pack,
        pack,
    ]
    return pl.pallas_call(
        functools.partial(sums_kernel, len(arrived)),
        grid_spec=pltpu.PrefetchScalarGridSpec(
            num_scalar_prefetch=1,
            grid=(1,),
            in_specs=[pl.BlockSpec((coarse, rank), lambda i, place: (place[0], 0))]
            + [whole(a.shape) for a in (gram_part, multi, start, *arrived)],
            out_specs=[whole(o.shape) for o in outs],
        ),
        out_shape=outs,
        compiler_params=params(),
        name="add_sums",
    )(place, hyper_part, gram_part, multi, start, *arrived)


def on_diagonal(rows, lanes):
    down = lax.broadcasted_iota(jnp.int32, (rows, lanes), 0)
    along = lax.broadcasted_iota(jnp.int32, (rows, lanes), 1)
    return down == along


def basis_kernel(
    devices, place, taps, multi, hyper, start, first_rows, second_rows, hyper_w, multi_w, bound,
    basis, products, natural, lifted, held,
):
    even = place[0] % 2 == 0
    before = jnp.where(even, second_rows[...], first_rows[...])
    after = jnp.where(even, first_rows[...], second_rows[...])
    fine = multi.shape[0]
    coarse = fine // DEC
    wide = coarse + 2 * RIM
    first, second = DEC * RIM_MULTI, DEC * RIM_MULTI + RIM
    own = slice(RIM, RIM + coarse)

    def apply(which, rim):
        rows = slice(RIM - rim, RIM + coarse + rim)
        fields = [held[which, phase, rows, :] for phase in range(DEC)]
        lowered = times(blur_down(taps, lambda phase: fields[phase]), hyper_w[...])
        return rows, [
            blur_up(taps, lowered, phase) + times(fields[phase], multi_w[...])
            for phase in range(DEC)
        ]

    margin = DEC * (RIM - RIM_START)
    none = jnp.zeros((margin, multi.shape[1]), jnp.float32)
    natural[:margin, :] = none
    natural[margin : DEC * RIM, :] = before[second:, :]
    natural[DEC * RIM : DEC * RIM + fine, :] = start[...]
    natural[DEC * RIM + fine : 2 * DEC * RIM + fine - margin, :] = after[second:, :]
    natural[2 * DEC * RIM + fine - margin :, :] = none
    for phase in range(DEC):
        held[1, phase] = natural[pl.ds(phase, wide, stride=DEC), :]
        basis[ITERS + 1, phase] = held[1, phase, own, :]
    _, mapped = apply(1, RIM)

    lifted[:RIM, :] = before[first:second, :]
    lifted[own, :] = hyper[...]
    lifted[RIM + coarse :, :] = after[first:second, :]
    margin = DEC * (RIM - RIM_MULTI)
    none = jnp.zeros((margin, multi.shape[1]), jnp.float32)
    natural[:margin, :] = none
    natural[margin : DEC * RIM, :] = before[:first, :]
    natural[DEC * RIM : DEC * RIM + fine, :] = multi[...]
    natural[DEC * RIM + fine : 2 * DEC * RIM + fine - margin, :] = after[:first, :]
    natural[2 * DEC * RIM + fine - margin :, :] = none
    quarter = bound[0:1, :] * 0.25
    sums = lifted[...]
    for phase in range(DEC):
        right = natural[pl.ds(phase, wide, stride=DEC), :] + blur_up(taps, sums, phase)
        held[0, phase] = right - quarter * mapped[phase]

    for step in range(ITERS):
        now = step % 2
        rim = -(-REACH * 2 * (ITERS - step) // 8) * 8
        rows, mapped = apply(now, rim)
        for phase in range(DEC):
            basis[step, phase] = held[now, phase, own, :]
            field = held[now, phase, rows, :]
            if step == 0:
                result = 0.5 * mapped[phase] - field
            else:
                result = mapped[phase] - 2.0 * field - held[1 - now, phase, rows, :]
            if step < ITERS - 1:
                held[1 - now, phase, rows, :] = result
            else:
                basis[ITERS, phase] = result[rim : rim + coarse, :]
    rows = []
    for i, j in PAIRS:
        total = jnp.zeros((coarse, multi.shape[1]), jnp.float32)
        for phase in range(DEC):
            total += basis[i, phase] * basis[j, phase]
        rows.append(jnp.sum(total, axis=0, keepdims=True))
    rows.append(jnp.zeros_like(rows[0]))
    block = jnp.sum(jnp.concatenate(rows, axis=0), axis=1, keepdims=True)
    block = jnp.where(on_diagonal(block.shape[0], multi.shape[1]), block, 0.0)
    block = jnp.sum(block, axis=0, keepdims=True)
    for device in range(devices):
        products[device] = block


def make_basis(
    devices, place, taps, multi, hyper, start, first_rows, second_rows, hyper_w, multi_w, bound
):
    fine, rank = multi.shape
    coarse = fine // DEC
    wide = coarse + 2 * RIM
    arrays = (multi, hyper, start, first_rows, second_rows, hyper_w, multi_w, bound)
    outs = [
        jax.ShapeDtypeStruct((ITERS + 2, DEC, coarse, rank), jnp.float32),
        pltpu.VMEM((devices, 1, rank), jnp.float32),
    ]
    return pl.pallas_call(
        functools.partial(basis_kernel, devices),
        in_specs=[SMEM, SMEM] + [whole(a.shape) for a in arrays],
        out_specs=[whole(o.shape) for o in outs],
        out_shape=outs,
        scratch_shapes=[
            pltpu.VMEM((DEC * wide, rank), jnp.float32),
            pltpu.VMEM((wide, rank), jnp.float32),
            pltpu.VMEM((2, DEC, wide, rank), jnp.float32),
        ],
        compiler_params=params(),
        name="make_basis",
    )(place, taps, *arrays)


def coefficients_kernel(products, bound, out, trusted):
    count = ITERS + 1
    row = jnp.sum(products[...], axis=0)
    sums = jnp.broadcast_to(row, (16, row.shape[1]))
    sums = jnp.sum(jnp.where(on_diagonal(*sums.shape), sums, 0.0), axis=1, keepdims=True)
    inner = {}
    for number, (i, j) in enumerate(PAIRS):
        inner[i, j] = inner[j, i] = sums[number : number + 1, :]
    zero = jnp.zeros((1, 1), jnp.float32)
    one = jnp.ones((1, 1), jnp.float32)

    def mapped_of(coefficients):
        result = [2.0 * c for c in coefficients] + [zero] * (count - len(coefficients))
        for j, c in enumerate(coefficients):
            if j + 1 < count:
                result[j + 1] = result[j + 1] + (2.0 * c if j == 0 else c)
            if j > 0:
                result[j - 1] = result[j - 1] + c
        return result

    def product(first, second):
        total = spread = zero
        for i, a in enumerate(first):
            if a is zero:
                continue
            for j, b in enumerate(second):
                if b is zero:
                    continue
                term = a * b * inner[i, j]
                total = total + term
                spread = spread + jnp.abs(term)
        return total, spread / jnp.abs(total)

    walked = [zero] * ITERS
    rest = [one] + [zero] * ITERS
    heading = [one]
    norm = inner[0, 0]
    worst = zero
    for iteration in range(ITERS):
        mapped = mapped_of(heading)
        mapped = mapped[: iteration + 2]
        curved, spread = product(heading, mapped)
        worst = jnp.maximum(worst, spread)
        step = norm / curved
        for j, c in enumerate(heading):
            walked[j] = walked[j] + step * c
        for j, c in enumerate(mapped):
            rest[j] = rest[j] - step * c
        if iteration < ITERS - 1:
            active = rest[: iteration + 2]
            following, spread = product(active, active)
            worst = jnp.maximum(worst, spread)
            ratio = following / norm
            heading = [
                c + ratio * heading[j] if j < len(heading) else c for j, c in enumerate(active)
            ]
            norm = following
    scale = 4.0 / bound[0:1, 0:1]
    rows = [c * scale for c in walked] + rest
    rows = jnp.concatenate(rows + [zero] * (out.shape[0] - len(rows)), axis=0)
    out[...] = jnp.broadcast_to(rows, out.shape)
    trusted[0] = jnp.where(worst < TRUST, 1, 0)[0, 0]


def make_coefficients(products, bound):
    rank = bound.shape[1]
    return pl.pallas_call(
        coefficients_kernel,
        in_specs=[whole(products.shape), whole(bound.shape)],
        out_specs=[whole((16, rank)), SMEM],
        out_shape=[
            jax.ShapeDtypeStruct((16, rank), jnp.float32),
            pltpu.SMEM((1,), jnp.int32),
        ],
        compiler_params=params(),
        name="make_coefficients",
    )(products, bound)


def combine_kernel(coefficients, basis, solution, residual):
    coarse = basis.shape[2]
    for phase in range(DEC):
        rows = pl.ds(phase, coarse, stride=DEC)
        total = basis[ITERS + 1, phase]
        for j in range(ITERS):
            total += coefficients[j : j + 1, :] * basis[j, phase]
        solution[rows, :] = total
        total = coefficients[ITERS : ITERS + 1, :] * basis[0, phase]
        for j in range(1, ITERS + 1):
            total += coefficients[ITERS + j : ITERS + j + 1, :] * basis[j, phase]
        residual[rows, :] = total


def combine(coefficients, basis):
    arrays = (coefficients, basis)
    out = jax.ShapeDtypeStruct((DEC * basis.shape[2], basis.shape[3]), jnp.float32)
    return pl.pallas_call(
        combine_kernel,
        in_specs=[whole(a.shape) for a in arrays],
        out_specs=[whole(out.shape)] * 2,
        out_shape=[out] * 2,
        compiler_params=params(),
        name="combine",
    )(*arrays)


def to_next(values, axis, count):
    return lax.ppermute(values, axis, [(i, (i + 1) % count) for i in range(count)])


def to_previous(values, axis, count):
    return lax.ppermute(values, axis, [((i + 1) % count, i) for i in range(count)])


def step_by_step(taps, multi, hyper, start, hyper_gram, multi_gram, devices):
    def widened(values, breadth):
        return jnp.concatenate(
            [
                to_next(values[-breadth:], BOTH, devices),
                values,
                to_previous(values[:breadth], BOTH, devices),
            ]
        )

    def down(values):
        rows = values.shape[0] // DEC
        parts = values.reshape(rows, DEC, -1)
        size = rows - 2 * REACH
        total = 0.0
        for offset in range(-W, W + 1):
            block, phase = divmod(offset, DEC)
            total = total + taps[offset + W] * lax.slice_in_dim(
                parts[:, phase], REACH + block, REACH + block + size, axis=0
            )
        return total

    def up(values):
        size = values.shape[0] - 2 * REACH
        phases = []
        for phase in range(DEC):
            total = 0.0
            for block in range(-REACH, REACH + 1):
                offset = DEC * block + phase
                if offset <= W:
                    total = total + taps[offset + W] * lax.slice_in_dim(
                        values, REACH - block, REACH - block + size, axis=0
                    )
            phases.append(total)
        return jnp.stack(phases, axis=1).reshape(DEC * size, -1)

    def operate(values):
        lowered = jnp.dot(down(widened(values, 2 * W)), hyper_gram, precision=FULL_PRECISION)
        return up(lowered) + jnp.dot(values, multi_gram, precision=FULL_PRECISION)

    def inner_sum(first, second):
        return lax.psum(jnp.sum(first * second), BOTH)

    solution = start
    residual = up(widened(hyper, REACH)) + multi - operate(solution)
    direction = residual
    norm = inner_sum(residual, residual)

    def iterate(_, state):
        solution, residual, direction, norm = state
        mapped = operate(direction)
        step = norm / inner_sum(direction, mapped)
        solution = solution + step * direction
        residual = residual - step * mapped
        following = inner_sum(residual, residual)
        return solution, residual, residual + following / norm * direction, following

    solution, residual, _, _ = lax.fori_loop(0, ITERS, iterate, (solution, residual, direction, norm))
    return solution, residual


def body(
    multispectral, hyperspectral, row_start, col_factor, band_factor, response, blur_taps, offsets
):
    across = lax.axis_size("col")
    along = lax.axis_size("row")
    devices = across * along
    place = lax.axis_index("col")
    row = lax.axis_index("row")[None]
    rank = band_factor.shape[1]
    share = rank // along
    fine = row_start.shape[0]

    def exchanged(values, distance):
        return lax.ppermute(values, "row", [(i, i ^ distance) for i in range(along)])

    own = col_factor.T
    partner = exchanged(own, 1)
    half = lax.optimization_barrier(jnp.concatenate([own, jnp.zeros_like(own)]))
    pair = jnp.concatenate([half[:share], partner])
    pair, image = lax.optimization_barrier((pair, multispectral))
    pieces = [pair] + [exchanged(pair, distance) for distance in range(2, along, 2)]
    image, band_factor, response, row_start, held = load(
        (image, band_factor, response, row_start, hyperspectral),
        (
            (2, 2, 2),
            (band_factor.shape[0], 1, band_factor.shape[0]),
            (2, 1, 2),
            (fine, 1, fine),
            (EARLY, 4, EARLY + LATER),
        ),
    )
    before = to_next(jnp.concatenate([p[:, -EDGE:] for p in pieces]), "col", across)
    after = to_previous(jnp.concatenate([p[:, :EDGE] for p in pieces]), "col", across)
    multi_part, columns, held = contract_multi(
        row, band_factor, response, image, pieces, hyperspectral, held, EARLY
    )
    spread = jnp.arange(-W, W + 1, dtype=jnp.int32)
    taps = jnp.sum(
        jnp.where(offsets[:, None] == spread[None, :], blur_taps[:, None], jnp.float32(0.0)), axis=0
    )

    def exchange(values, size, more):
        arrived = []
        for distance in range(1, across):
            piece = lax.dynamic_slice_in_dim(values, (place + distance) % across * size, size, 0)
            if more:
                piece = jnp.concatenate([piece] + more)
            arrived.append(
                lax.ppermute(piece, "col", [(i, (i + distance) % across) for i in range(across)])
            )
        return arrived

    multi_arrived = exchange(multi_part, fine, [])
    hyper_part, gram_part = contract_hyper(
        share, row, taps, columns, before, after, band_factor, held, hyperspectral
    )
    hyper_arrived = exchange(hyper_part, fine // DEC, [gram_part])
    multi, band_gram, merged_gram = sum_arrived(
        place[None], band_factor, response, multi_part, multi_arrived
    )
    hyper, gram, first_pack, second_pack = add_sums(
        place[None], hyper_part, gram_part, multi, row_start, hyper_arrived
    )
    hyper_gram, multi_gram, hyper_w, multi_w, bound = make_operator(
        row, taps, band_gram, merged_gram, gram, exchanged(gram, 1)
    )
    second_rows = lax.ppermute(
        second_pack, BOTH, [((i + 1) % devices, ((i ^ 1) + 1) % devices) for i in range(devices)]
    )
    first_rows = lax.ppermute(first_pack, BOTH, [(i, i ^ 1) for i in range(devices)])
    basis, products = make_basis(
        devices, place[None], taps, multi, hyper, row_start, first_rows, second_rows, hyper_w,
        multi_w, bound,
    )
    products = lax.all_to_all(products, BOTH, 0, 0, tiled=True)
    coefficients, trusted = make_coefficients(products, bound)

    def from_start():
        start = jnp.stack(list(basis[ITERS + 1]), axis=1).reshape(fine, rank)
        return step_by_step(taps, multi, hyper, start, hyper_gram, multi_gram, devices)

    return lax.cond(trusted[0] != 0, lambda: tuple(combine(coefficients, basis)), from_start)


def solution(mesh):
    in_specs = (
        P(None, "row", "col"),
        P(None, "row", "col"),
        P(("row", "col"), None),
        P("col", "row"),
        P(),
        P(),
        P(),
        P(),
    )
    out_specs = (P(("row", "col"), None), P(("row", "col"), None))
    return jax.shard_map(body, mesh=mesh, in_specs=in_specs, out_specs=out_specs, check_vma=False)
```
